32 devices in a mesh: dp: 4 (over y, core), seq: 8 (over z, x).
Axes of the slice: x: 2, y: 2, z: 4, core: 2. Of those that a mesh axis runs over, the one named last changes fastest.
Arguments:
- hidden_in: float32 [8, 2048, 1024], P('dp', 'seq'), may hold values from -6 to 6
- lengths: int32 [8], P('dp'), may hold values from 512 to 2048, as said below
- norm_gain: float32 [1024], replicated, may hold values from 0.1 to 1.9
- in_weight: float32 [4489216], P(('dp', 'seq')), may hold values from -0.1875 to 0.1875
- conv_weight: float32 [9216], P(('dp', 'seq')), may hold values from -3 to 3
- conv_bias: float32 [2304], P(('dp', 'seq')), may hold values from -3 to 3
- dt_bias: float32 [32], replicated, may hold values from -9 to -1
- a_log: float32 [32], replicated, may hold values from -6 to -1
- skip_gain: float32 [32], replicated, may hold values from 0.5 to 2
- gated_gain: float32 [2048], replicated, may hold values from 0.1 to 1.9
- out_weight: float32 [2097152], P(('dp', 'seq')), may hold values from -0.125 to 0.125
- cotangent: float32 [8, 2048, 1024], P('dp', 'seq'), may hold values from -6 to 6
Outputs:
- output: float32 [8, 2048, 1024], P('dp', 'seq')
- grad_input: float32 [8, 2048, 1024], P('dp', 'seq')
- grad_norm_gain: float32 [1024], replicated
- grad_in_weight: float32 [4489216], P(('dp', 'seq'))
- grad_conv_weight: float32 [9216], P(('dp', 'seq'))
- grad_conv_bias: float32 [2304], P(('dp', 'seq'))
- grad_dt_bias: float32 [32], replicated
- grad_a_log: float32 [32], replicated
- grad_skip_gain: float32 [32], replicated
- grad_gated_gain: float32 [2048], replicated
- grad_out_weight: float32 [2097152], P(('dp', 'seq'))
The draws below stay inside these ranges and needn't reach their ends.
Inputs may be any that keep to these rules, and one draw needn't show every extreme that they name: `lengths`: of the 2 sequences of each index of dp, one, drawn from the seed, fills all 2048 slots; the others are drawn evenly.
All inputs are finite; a program needn't handle non-finite values.
Results may differ from the reference program's by a relative error of at most 0.0003.
Values sent between devices are 32-bit elements; how exact they have to be, the bound alone decides.
No kernel may reach another device: no remote copies, remote signals or barrier semaphores. Data moves between devices by JAX's collectives and lax.ppermute only.
A program may use at most 256 MiB of HBM per device.

```python
import jax
import jax.numpy as jnp
from jax import lax

D = 1024
DI = 2048
HEADS = 32
HDIM = 64
STATE = 128
CONV = 4
SPAN = 256
SEQ_DEV = 2
MIXED = 2304
PROJ = 4384
LENGTH = 2048
SEQS = 8


def head_windows(key):
    head_key = jax.random.fold_in(key, 11)
    factor_key = jax.random.fold_in(key, 13)
    upper_end = jnp.log(16.0 * LENGTH)
    lower_end = jnp.log(40.0)
    fraction = jax.random.uniform(head_key, (HEADS,), jnp.float32)
    window = jnp.exp(lower_end + (upper_end - lower_end) * fraction)
    factor = jnp.exp(jnp.log(0.7) + (jnp.log(2.0) - jnp.log(0.7)) * jax.random.uniform(factor_key, (HEADS,), jnp.float32))
    target = factor * 5.0 / jnp.minimum(window, 1.0 * LENGTH)
    return (window, target)


def draw_dt_bias(key, part):
    window, target = head_windows(key)
    return jnp.log(jnp.expm1(target))


def draw_a_log(key, part):
    window, target = head_windows(key)
    return -jnp.log(target * window)


def draw_lengths(key, part):
    groups = SEQS // SEQ_DEV
    sampled = jax.random.randint(jax.random.fold_in(key, 3), (groups, SEQ_DEV), LENGTH // 4, LENGTH + 1)
    chosen = jax.random.randint(jax.random.fold_in(key, 5), (groups, 1), 0, SEQ_DEV)
    position = jnp.arange(SEQ_DEV, dtype=jnp.int32)[None, :]
    filled = jnp.where(position == chosen, LENGTH, sampled)
    return filled.reshape(SEQS).astype(jnp.int32)


def block_scale(key, dims, shards, low, top_value):
    def one(dim, shards_of):
        heights = jax.random.uniform(jax.random.fold_in(jax.random.fold_in(key, 6), dim), (shards_of,), jnp.float32, low / len(shards), top_value / len(shards))
        return jnp.repeat(jnp.exp(heights), dims[dim] // shards_of).reshape((-1,) + (1,) * (len(dims) - dim - 1))

    factor_of = one(*shards[0])
    for cut in shards[1:]:
        factor_of = factor_of * one(*cut)
    return factor_of


def centred(key, extent, scale, most, split=(), held_as=jnp.bfloat16):
    entries = jax.random.normal(key, extent, jnp.float32) * scale
    if len(split) > 0:
        entries = block_scale(key, extent, split, -0.22, 0.18) * entries
    return jnp.clip(entries, min=-most, max=most).astype(held_as)


def setup_inputs(seed: int = 0) -> dict:
    seeds = jax.random.split(jax.random.key(seed), 13)
    hidden_in = centred(seeds[0], (SEQS, LENGTH, D), 1.0, 6.0, ((0, 4), (1, 8)), jnp.float32)
    lengths = draw_lengths(jax.random.fold_in(seeds[12], 71), 0)
    norm_gain = jnp.clip(1.0 + 0.18 * jax.random.normal(seeds[2], (D,), jnp.float32), 0.1, 1.9)
    in_weight = centred(seeds[3], (D * PROJ,), D ** -0.5, 0.1875, ((0, 32),), jnp.float32)
    conv_weight = centred(seeds[4], (CONV * MIXED,), CONV ** -0.5, 3.0, ((0, 32),), jnp.float32)
    conv_bias = centred(seeds[5], (MIXED,), 0.5, 3.0, ((0, 32),), jnp.float32)
    dt_bias = draw_dt_bias(jax.random.fold_in(seeds[12], 71), 0)
    a_log = draw_a_log(jax.random.fold_in(seeds[12], 71), 0)
    skip_gain = jnp.clip(jax.random.uniform(seeds[8], (HEADS,), jnp.float32, 0.5, 2.0), 0.5, 2.0)
    gated_gain = jnp.clip(1.0 + 0.18 * jax.random.normal(seeds[9], (DI,), jnp.float32), 0.1, 1.9)
    out_weight = centred(seeds[10], (DI * D,), DI ** -0.5, 0.125, ((0, 32),), jnp.float32)
    cotangent = centred(seeds[11], (SEQS, LENGTH, D), 1.0, 6.0, ((0, 4), (1, 8)), jnp.float32)
    return {"hidden_in": hidden_in, "lengths": lengths, "norm_gain": norm_gain, "in_weight": in_weight, "conv_weight": conv_weight, "conv_bias": conv_bias, "dt_bias": dt_bias, "a_log": a_log, "skip_gain": skip_gain, "gated_gain": gated_gain, "out_weight": out_weight, "cotangent": cotangent}


@jax.custom_vjp
def low(v):
    return lax.optimization_barrier(v.astype(jnp.bfloat16)).astype(jnp.float32)

@jax.custom_vjp
def low_back(v):
    return v

def low_keep(v):
    return (low(v), None)

def low_pass(kept, grad):
    return (grad,)

def back_keep(v):
    return (v, None)

def back_low(kept, grad):
    return (low(grad),)
low.defvjp(low_keep, low_pass)
low_back.defvjp(back_keep, back_low)
epsilon = 1e-05
highest = lax.Precision.HIGHEST

def rms_scale(values, gain):
    return values * lax.rsqrt(lax.optimization_barrier(jnp.mean(values * values, axis=-1, keepdims=True)) + epsilon) * gain

def block_step(entering, block):
    heads_in, b_state, c_state, step_size, log_rate = block
    log_decay = jnp.cumsum(log_rate, axis=0).T
    lower = lax.iota(jnp.int32, SPAN)[:, None] >= lax.iota(jnp.int32, SPAN)[None, :]
    spread = log_decay[:, :, None] - log_decay[:, None, :]
    weights = jnp.where(lower, jnp.exp(jnp.where(lower, spread, 0.0)), 0.0)
    scores = jnp.dot(c_state, b_state.T, precision=highest)
    mixing = scores[None] * weights * step_size.T[:, None, :]
    inner = jnp.einsum('hts,shp->thp', mixing, heads_in, precision=highest)
    carried = jnp.exp(log_decay).T[:, :, None] * jnp.einsum('tn,hpn->thp', c_state, entering, precision=highest)
    tail = jnp.exp(log_decay[:, -1:] - log_decay).T * step_size
    weighted = tail[:, :, None] * heads_in
    leaving = jnp.exp(log_decay[:, -1])[:, None, None] * entering + jnp.einsum('shp,sn->hpn', weighted, b_state, precision=highest)
    return (leaving, inner + carried)

def sequence(hidden, length, norm_gain, w_in, taps, conv_bias, dt_bias, a_log, skip_gain, gated_gain, w_out):
    normed = rms_scale(hidden, norm_gain)
    projected = jnp.dot(normed, w_in, precision=highest)
    gate_in = projected[:, :DI]
    conv_in = projected[:, DI:DI + MIXED]
    rate_in = projected[:, DI + MIXED:]
    padded = jnp.concatenate([jnp.zeros((CONV - 1, MIXED), jnp.float32), conv_in], axis=0)
    conv_out = conv_bias + taps[0] * padded[0:LENGTH]
    for offset in range(1, CONV):
        conv_out = conv_out + taps[offset] * padded[offset:offset + LENGTH]
    active = jax.nn.silu(conv_out)
    heads_in = active[:, :DI].reshape(LENGTH, HEADS, HDIM)
    b_state = active[:, DI:DI + STATE]
    c_state = active[:, DI + STATE:]
    step_size = jax.nn.softplus(rate_in + dt_bias)
    log_rate = -jnp.exp(a_log) * step_size
    blocks = LENGTH // SPAN
    start_state = jnp.zeros((HEADS, HDIM, STATE), jnp.float32)
    stacked = (heads_in.reshape(blocks, SPAN, HEADS, HDIM), b_state.reshape(blocks, SPAN, STATE), c_state.reshape(blocks, SPAN, STATE), step_size.reshape(blocks, SPAN, HEADS), log_rate.reshape(blocks, SPAN, HEADS))
    _, pieces = lax.scan(jax.checkpoint(block_step), start_state, stacked)
    ssd = pieces.reshape(LENGTH, HEADS, HDIM) + skip_gain[:, None] * heads_in
    gated = ssd.reshape(LENGTH, DI) * jax.nn.silu(gate_in)
    normed_gate = rms_scale(gated, gated_gain)
    branch = jnp.dot(normed_gate, w_out, precision=highest)
    valid = (lax.iota(jnp.int32, LENGTH) < length).astype(jnp.float32)[:, None]
    return (hidden + branch) * valid

def reference(hidden_in, lengths, norm_gain, in_weight, conv_weight, conv_bias, dt_bias, a_log, skip_gain, gated_gain, out_weight, cotangent):

    def forward(hidden_all, gain_in, weight_in, weight_conv, bias_conv, bias_step, rate_log, gain_skip, gain_gated, weight_out):
        w_in = weight_in.reshape(D, PROJ)
        taps = weight_conv.reshape(CONV, MIXED)
        w_out = weight_out.reshape(DI, D)

        def one_seq(item):
            return sequence(item[0], item[1], gain_in, w_in, taps, bias_conv, bias_step, rate_log, gain_skip, gain_gated, w_out)
        return lax.map(jax.checkpoint(one_seq), (hidden_all, lengths))
    output, pullback = jax.vjp(forward, hidden_in, norm_gain, in_weight, conv_weight, conv_bias, dt_bias, a_log, skip_gain, gated_gain, out_weight)
    grads = pullback(cotangent)
    return (output, grads[0], grads[1], grads[2], grads[3], grads[4], grads[5], grads[6], grads[7], grads[8], grads[9])
```

```python
import functools

import jax
import jax.numpy as jnp
from jax import lax
from jax.experimental import pallas as pl
from jax.experimental.pallas import tpu as pltpu
from jax.sharding import Mesh
from jax.sharding import PartitionSpec as P

DI = 2048
HEADS = 32
HDIM = 64
STATE = 128
CONV = 4
MIXED = DI + 2 * STATE
RATED = MIXED + HEADS
CUT = 128
EDGE = 8
PAIR = 2 * HDIM
F32 = jnp.float32
BF16 = jnp.bfloat16
HIGH = lax.Precision.HIGH
EXACT = lax.Precision.HIGHEST
epsilon = 1e-05


def shift(block, axis, step=1):
    count = lax.axis_size(axis)
    return lax.ppermute(block, axis, [(i, (i + step) % count) for i in range(count)])


def gather_axis(block, axis):
    count, index = (lax.axis_size(axis), lax.axis_index(axis))
    whole = jnp.zeros((count,) + block.shape, block.dtype)
    whole = lax.dynamic_update_slice_in_dim(whole, block[None], index, 0)
    moving = block
    for k in range(1, count):
        moving = shift(moving, axis)
        whole = lax.dynamic_update_slice_in_dim(whole, moving[None], (index - k) % count, 0)
    return whole


AXES = ("y", "core", "zc", "p")


def gather_rows(piece, order):
    block = piece.reshape((1,) * len(AXES) + piece.shape)
    for axis in order:
        at = AXES.index(axis)
        block = jnp.moveaxis(gather_axis(block, axis), 0, at)
        block = block.reshape(block.shape[: at + 1] + block.shape[at + 2 :])
    return block.reshape(-1, piece.shape[-1])


def scatter_axis(parts, axis, dim):
    count, index = (lax.axis_size(axis), lax.axis_index(axis))
    moving = lax.dynamic_index_in_dim(parts, (index - 1) % count, dim, keepdims=False)
    for k in range(2, count + 1):
        moving = shift(moving, axis) + lax.dynamic_index_in_dim(
            parts, (index - k) % count, dim, keepdims=False
        )
    return moving


def scatter_rows(whole, order):
    left = list(AXES)
    block = whole.reshape([lax.axis_size(a) for a in AXES] + [-1, whole.shape[-1]])
    for axis in order:
        block = scatter_axis(block, axis, left.index(axis))
        left.remove(axis)
    return block


def gather_matrix(piece):
    half = piece.shape[1] // 256 * 128
    return (
        gather_rows(piece[:, :half], ("zc", "p", "y", "core")),
        gather_rows(piece[:, half:], ("zc", "y", "p", "core")),
    )


def scatter_matrix(whole):
    half = whole.shape[1] // 256 * 128
    return jnp.concatenate(
        [
            scatter_rows(whole[:, :half], ("core", "p", "y", "zc")),
            scatter_rows(whole[:, half:], ("core", "y", "p", "zc")),
        ],
        axis=1,
    )


def sum_everywhere(values):
    for axis in ("core", "p", "y", "zc"):
        if lax.axis_size(axis) == 2:
            values = values + shift(values, axis)
        else:
            values = jnp.sum(gather_axis(values, axis), axis=0)
    return values


def to_span(block, mine):
    keep = lax.dynamic_index_in_dim(block, mine, 0, keepdims=False)
    other = shift(lax.dynamic_index_in_dim(block, 1 - mine, 0, keepdims=False), "p")
    first = mine == 0
    return jnp.concatenate([jnp.where(first, keep, other), jnp.where(first, other, keep)], axis=0)


def from_span(span, mine):
    block = span.reshape(2, -1, span.shape[-1])
    keep = lax.dynamic_index_in_dim(block, mine, 0, keepdims=False)
    other = shift(lax.dynamic_index_in_dim(block, 1 - mine, 0, keepdims=False), "p")
    first = mine == 0
    return jnp.stack([jnp.where(first, keep, other), jnp.where(first, other, keep)], axis=0)


def chain(decay, leaving, reverse):
    count, index = (lax.axis_size("zc"), lax.axis_index("zc"))
    place = count - 1 - index if reverse else index
    route = [(i + 1, i) if reverse else (i, i + 1) for i in range(count - 1)]
    chunks = 4
    rows = leaving.shape[0] // chunks
    came, got = ([], None)
    for step in range(chunks + count - 2):
        at = jnp.clip(step - place, 0, chunks - 1) * rows
        send = lax.dynamic_slice_in_dim(leaving, at, rows, 0)
        if got is not None:
            send = send + decay * got
        got = lax.ppermute(send, "zc", route)
        came.append(got)
    return lax.dynamic_slice_in_dim(
        jnp.concatenate(came, axis=0), jnp.maximum(place - 1, 0) * rows, leaving.shape[0], 0
    )


def nn(a, b, precision=HIGH):
    return jnp.dot(a, b, precision=precision, preferred_element_type=F32)


def nt(a, b, precision=HIGH):
    return lax.dot_general(
        a, b, (((1,), (1,)), ((), ())), precision=precision, preferred_element_type=F32
    )


def tn(a, b, precision=HIGH):
    return lax.dot_general(
        a, b, (((0,), (0,)), ((), ())), precision=precision, preferred_element_type=F32
    )


def spread_heads(values, spreader):
    top = values.astype(BF16)
    rest = values - top.astype(F32)
    mid = rest.astype(BF16)
    low = (rest - mid.astype(F32)).astype(BF16)
    return jnp.dot(
        jnp.concatenate([top, mid, low], axis=1), spreader, preferred_element_type=F32
    )


def sum_heads(values, gatherer):
    top = values.astype(BF16)
    low = (values - top.astype(F32)).astype(BF16)
    return jnp.dot(top, gatherer, preferred_element_type=F32) + jnp.dot(
        low, gatherer, preferred_element_type=F32
    )


def order_mask(shape, kind):
    row, column = (lax.broadcasted_iota(jnp.int32, shape, d) for d in (0, 1))
    return {"ge": row >= column, "gt": row > column, "le": row <= column, "lt": row < column}[kind]


def triangle(kind):
    return jnp.where(order_mask((CUT, CUT), kind), 1.0, 0.0).astype(F32)


def conv_chunk(window_ref, taps_ref, bias_ref, cols):
    total = bias_ref[:, cols] + taps_ref[0:1, cols] * window_ref[EDGE - 3 : EDGE - 3 + CUT, cols]
    for k in range(1, CONV):
        at = EDGE - 3 + k
        total = total + taps_ref[k : k + 1, cols] * window_ref[at : at + CUT, cols]
    return total


def prepare_kernel(
    proj_ref,
    edge_ref,
    taps_ref,
    bias_ref,
    dtb_ref,
    alog_ref,
    spreader_ref,
    act_ref,
    step_ref,
    slope_ref,
    logd_ref,
    local_ref,
    before_ref,
    total_ref,
    window,
    state,
    logs,
):
    q = pl.program_id(0)

    @pl.when(q == 0)
    def _():
        window[0:EDGE, :] = edge_ref[:, 0:MIXED]
        state[...] = jnp.zeros_like(state)
        logs[...] = jnp.zeros_like(logs)

    @pl.when(q > 0)
    def _():
        window[0:EDGE, :] = window[CUT : CUT + EDGE, :]

    window[EDGE : EDGE + CUT, :] = proj_ref[:, 0:MIXED]

    def conv(c, carry):
        cols = pl.ds(pl.multiple_of(c * 256, 256), 256)
        out = conv_chunk(window, taps_ref, bias_ref, cols)
        act_ref[:, cols] = out * jax.nn.sigmoid(out)
        return carry

    lax.fori_loop(0, MIXED // 256, conv, 0)
    raw = proj_ref[:, MIXED:RATED] + dtb_ref[...]
    step = jnp.maximum(raw, 0.0) + jnp.log1p(jnp.exp(-jnp.abs(raw)))
    logd = nn(triangle("ge"), -jnp.exp(alog_ref[...]) * step, EXACT)
    step_ref[...] = step
    slope_ref[...] = jax.nn.sigmoid(raw)
    logd_ref[...] = logd
    last = logd[CUT - 1 : CUT, :]
    tail = spread_heads(jnp.exp(last - logd) * step, spreader_ref[...])
    added = tn(act_ref[:, DI : DI + STATE], act_ref[:, 0:DI] * tail)
    decay = spread_heads(jnp.broadcast_to(jnp.exp(last), (8, HEADS)), spreader_ref[...])
    state[...] = state[...] * decay[0:1, :] + added
    local_ref[0] = state[...]
    before_ref[...] = jnp.exp(logs[...])
    logs[...] = logs[...] + jnp.broadcast_to(last, (8, HEADS))
    total_ref[...] = jnp.exp(logs[...])


def full(shape):
    return pl.BlockSpec(shape, lambda i: (0,) * len(shape))


def params():
    return pltpu.CompilerParams(
        dimension_semantics=("arbitrary",), vmem_limit_bytes=52 * 1024 * 1024
    )


def prepare(proj, taps, bias, dt_bias, a_log, spreader):
    width = proj.shape[1]
    rows = proj.shape[0] - EDGE
    cuts = rows // CUT
    return pl.pallas_call(
        prepare_kernel,
        grid=(cuts,),
        in_specs=[
            pl.BlockSpec((CUT, width), lambda i: (i, 0)),
            pl.BlockSpec((EDGE, width), lambda i: (rows // EDGE, 0)),
            full((CONV, MIXED)),
            full((1, MIXED)),
            full((1, HEADS)),
            full((1, HEADS)),
            full((3 * HEADS, DI)),
        ],
        out_specs=[
            pl.BlockSpec((CUT, MIXED), lambda i: (i, 0)),
            pl.BlockSpec((CUT, HEADS), lambda i: (i, 0)),
            pl.BlockSpec((CUT, HEADS), lambda i: (i, 0)),
            pl.BlockSpec((CUT, HEADS), lambda i: (i, 0)),
            pl.BlockSpec((1, STATE, DI), lambda i: (i, 0, 0)),
            pl.BlockSpec((8, HEADS), lambda i: (i, 0)),
            full((8, HEADS)),
        ],
        out_shape=[
            jax.ShapeDtypeStruct((rows, MIXED), F32),
            jax.ShapeDtypeStruct((rows, HEADS), F32),
            jax.ShapeDtypeStruct((rows, HEADS), F32),
            jax.ShapeDtypeStruct((rows, HEADS), F32),
            jax.ShapeDtypeStruct((cuts, STATE, DI), F32),
            jax.ShapeDtypeStruct((8 * cuts, HEADS), F32),
            jax.ShapeDtypeStruct((8, HEADS), F32),
        ],
        scratch_shapes=[
            pltpu.VMEM((CUT + EDGE, MIXED), F32),
            pltpu.VMEM((STATE, DI), F32),
            pltpu.VMEM((8, HEADS), F32),
        ],
        compiler_params=params(),
        cost_estimate=pl.CostEstimate(
            flops=6 * rows * STATE * DI, bytes_accessed=24_000_000, transcendentals=rows * MIXED
        ),
        name="prepare",
    )(proj, proj, taps, bias, dt_bias, a_log, spreader)


def both_columns(pair, left):
    turned = pltpu.roll(pair, HDIM, 1)
    return (jnp.where(left, pair, turned), jnp.where(left, turned, pair))


def stacked_pair(pair, left):
    zero = jnp.zeros_like(pair)
    return jnp.concatenate([jnp.where(left, pair, zero), jnp.where(left, zero, pair)], axis=0)


def mixer_kernel(
    act_ref,
    step_ref,
    logd_ref,
    gate_ref,
    dng_ref,
    local_ref,
    enter_ref,
    before_ref,
    skip_ref,
    ggain_ref,
    spreader_ref,
    ng_ref,
    dy_ref,
    dz_ref,
    gin_ref,
    ggrad_ref,
    skipg_ref,
    logx,
    weighted,
    out,
    log_rows,
    gstate,
    scores,
):
    i = pl.program_id(0)
    q = pl.num_programs(0) - 1 - i
    spreader = spreader_ref[...]

    @pl.when(i == 0)
    def _():
        gstate[...] = jnp.zeros_like(gstate)
        ggrad_ref[...] = jnp.zeros_like(ggrad_ref)
        skipg_ref[...] = jnp.zeros_like(skipg_ref)

    logd = logd_ref[...]
    logx[...] = spread_heads(logd, spreader)
    log_rows[...] = logd.T
    heads_in = act_ref[:, 0:DI]
    weighted[...] = heads_in * spread_heads(step_ref[...], spreader)
    before = spread_heads(before_ref[...], spreader)[0:1, :]
    entering = enter_ref[...] * before + jnp.where(q == 0, 0.0, local_ref[0])
    b_state = act_ref[:, DI : DI + STATE]
    c_state = act_ref[:, DI + STATE : MIXED]
    out[...] = jnp.exp(logx[...]) * nn(c_state, entering) + skip_ref[...] * heads_in
    scores[...] = nt(c_state, b_state)

    def pair(j, carry):
        cols = pl.ds(pl.multiple_of(j * PAIR, PAIR), PAIR)
        left = lax.broadcasted_iota(jnp.int32, (CUT, PAIR), 1) < HDIM
        mask = order_mask((CUT, CUT), "ge")
        mixes = []
        for side, column in enumerate(both_columns(logx[:, cols], left)):
            row = log_rows[pl.ds(2 * j + side, 1), :]
            mixes.append(jnp.exp(jnp.where(mask, column - row, -1e30)) * scores[...])
        out[:, cols] += nn(
            jnp.concatenate(mixes, axis=1), stacked_pair(weighted[:, cols], left)
        )
        return carry

    lax.fori_loop(0, HEADS // 2, pair, 0)

    def gate(k, carry):
        rows = pl.ds(pl.multiple_of(k * 8, 8), 8)
        ssd = out[rows, :]
        gate_in = gate_ref[rows, :]
        sg = jax.nn.sigmoid(gate_in)
        silu = gate_in * sg
        gated = ssd * silu
        scale = lax.rsqrt(jnp.mean(gated * gated, axis=1, keepdims=True) + epsilon)
        unit = gated * scale
        ng_ref[rows, :] = unit * ggain_ref[...]
        dng = dng_ref[rows, :]
        e = dng * ggain_ref[...]
        ggrad_ref[...] += dng * unit
        dgated = scale * (e - unit * jnp.mean(e * unit, axis=1, keepdims=True))
        dy = dgated * silu
        dy_ref[rows, :] = dy
        dz_ref[rows, :] = dgated * ssd * (sg * (1.0 + gate_in * (1.0 - sg)))
        skipg_ref[...] += dy * act_ref[rows, 0:DI]
        return carry

    lax.fori_loop(0, CUT // 8, gate, 0)
    decay = spread_heads(
        jnp.broadcast_to(jnp.exp(logd[CUT - 1 : CUT, :]), (8, HEADS)), spreader
    )[0:1, :]
    gstate[...] = gstate[...] * decay + tn(c_state, jnp.exp(logx[...]) * dy_ref[...])
    gin_ref[0] = gstate[...]


def mixer(act, step, logd, gate_in, dng, local, entering, before, skip, ggain, spreader):
    rows = act.shape[0]
    cuts = rows // CUT

    def back(width):
        return pl.BlockSpec((CUT, width), lambda i: (cuts - 1 - i, 0))

    wide = jax.ShapeDtypeStruct((rows, DI), F32)
    return pl.pallas_call(
        mixer_kernel,
        grid=(cuts,),
        in_specs=[
            back(MIXED),
            back(HEADS),
            back(HEADS),
            back(DI),
            back(DI),
            pl.BlockSpec((1, STATE, DI), lambda i: (jnp.maximum(cuts - 2 - i, 0), 0, 0)),
            full((STATE, DI)),
            pl.BlockSpec((8, HEADS), lambda i: (cuts - 1 - i, 0)),
            full((1, DI)),
            full((1, DI)),
            full((3 * HEADS, DI)),
        ],
        out_specs=[
            back(DI),
            back(DI),
            back(DI),
            pl.BlockSpec((1, STATE, DI), lambda i: (cuts - 1 - i, 0, 0)),
            full((8, DI)),
            full((8, DI)),
        ],
        out_shape=[
            wide,
            wide,
            wide,
            jax.ShapeDtypeStruct((cuts, STATE, DI), F32),
            jax.ShapeDtypeStruct((8, DI), F32),
            jax.ShapeDtypeStruct((8, DI), F32),
        ],
        scratch_shapes=[
            pltpu.VMEM((CUT, DI), F32),
            pltpu.VMEM((CUT, DI), F32),
            pltpu.VMEM((CUT, DI), F32),
            pltpu.VMEM((HEADS, CUT), F32),
            pltpu.VMEM((STATE, DI), F32),
            pltpu.VMEM((CUT, CUT), F32),
        ],
        compiler_params=params(),
        cost_estimate=pl.CostEstimate(
            flops=30 * rows * STATE * DI, bytes_accessed=38_000_000, transcendentals=rows * CUT * HEADS
        ),
        name="mixer",
    )(act, step, logd, gate_in, dng, local, entering, before, skip, ggain, spreader)


def back_kernel(
    act_ref,
    step_ref,
    slope_ref,
    logd_ref,
    dy_ref,
    local_ref,
    enter_ref,
    before_ref,
    gin_ref,
    gout_ref,
    proj_ref,
    halo_ref,
    taps_ref,
    bias_ref,
    alog_ref,
    skip_ref,
    spreader_ref,
    gatherer_ref,
    dproj_ref,
    dtaps_ref,
    dbias_ref,
    dlog_ref,
    ddtb_ref,
    logx,
    weighted,
    dweighted,
    log_rows,
    sum_rows,
    scores,
    dscores,
    sum_columns,
    dact,
    window,
    dwindow,
    after,
):
    i = pl.program_id(0)
    cuts = pl.num_programs(0)
    q = cuts - 1 - i
    spreader = spreader_ref[...]
    gatherer = gatherer_ref[...]

    @pl.when(i == 0)
    def _():
        after[...] = jnp.zeros_like(after)
        dwindow[...] = jnp.zeros_like(dwindow)
        for ref in (dtaps_ref, dbias_ref, dlog_ref, ddtb_ref):
            ref[...] = jnp.zeros_like(ref)

    @pl.when(i > 0)
    def _():
        dwindow[CUT : CUT + EDGE, :] = dwindow[0:EDGE, :]

    logd = logd_ref[...]
    step = step_ref[...]
    last = logd[CUT - 1 : CUT, :]
    logx[...] = spread_heads(logd, spreader)
    log_rows[...] = logd.T
    heads_in = act_ref[:, 0:DI]
    steps = spread_heads(step, spreader)
    weighted[...] = heads_in * steps
    before = spread_heads(before_ref[...], spreader)[0:1, :]
    entering = enter_ref[...] * before + jnp.where(q == 0, 0.0, local_ref[0])
    later = spread_heads(jnp.exp(after[...]), spreader)[0:1, :]
    gout = gout_ref[...] * later + jnp.where(i == 0, 0.0, gin_ref[0])
    after[...] = after[...] + jnp.broadcast_to(last, (8, HEADS))
    b_state = act_ref[:, DI : DI + STATE]
    c_state = act_ref[:, DI + STATE : MIXED]
    scores[...] = nt(b_state, c_state)
    dscores[...] = jnp.zeros_like(dscores)
    sum_columns[...] = jnp.zeros_like(sum_columns)

    def pair(j, carry):
        cols = pl.ds(pl.multiple_of(j * PAIR, PAIR), PAIR)
        left = lax.broadcasted_iota(jnp.int32, (CUT, PAIR), 1) < HDIM
        mask = order_mask((CUT, CUT), "le")
        strict = order_mask((CUT, CUT), "lt")
        dy = dy_ref[:, cols]
        dmix = nt(stacked_pair(weighted[:, cols], left), dy)
        mixes = []
        lane = lax.broadcasted_iota(jnp.int32, (CUT, CUT), 1)
        for side, column in enumerate(both_columns(logx[:, cols], left)):
            row = log_rows[pl.ds(2 * j + side, 1), :]
            weights = jnp.exp(jnp.where(mask, row - column, -1e30))
            mixes.append(weights * scores[...])
            part = dmix[side * CUT : (side + 1) * CUT, :] * weights
            dscores[...] += part
            moved = jnp.where(strict, part * scores[...], 0.0)
            sum_rows[pl.ds(2 * j + side, 1), :] = jnp.sum(moved, axis=0, keepdims=True)
            sum_columns[...] += jnp.where(
                lane == 2 * j + side, jnp.sum(moved, axis=1, keepdims=True), 0.0
            )
        dweighted[:, cols] = nn(jnp.concatenate(mixes, axis=1), stacked_pair(dy, left))
        return carry

    lax.fori_loop(0, HEADS // 2, pair, 0)
    tail = jnp.exp(logx[CUT - 1 : CUT, :] - logx[...])
    from_state = tail * nn(b_state, gout)
    left_part = weighted[...] * from_state
    dweighted[...] += from_state
    carried = jnp.exp(logx[...]) * dy_ref[...]
    dact[:, DI : DI + STATE] = nn(dscores[...], c_state) + nt(tail * weighted[...], gout)
    dact[:, DI + STATE : MIXED] = tn(dscores[...], b_state) + nt(carried, entering)
    dact[:, 0:DI] = dweighted[...] * steps + skip_ref[...] * dy_ref[...]
    moved = (
        log_rows_to_columns(sum_rows)
        - sum_columns[:, 0:HEADS]
        + sum_heads(carried * nn(c_state, entering), gatherer)
    )
    kept = sum_heads(
        jnp.broadcast_to(jnp.sum(gout * entering, axis=0, keepdims=True), (8, DI)), gatherer
    )[0:1, :]
    dlog = (
        nn(triangle("le"), moved, EXACT)
        + nn(triangle("gt"), sum_heads(left_part, gatherer), EXACT)
        + jnp.exp(last) * kept
    )
    rate = -jnp.exp(alog_ref[...])
    dlog_ref[...] += jnp.broadcast_to(
        jnp.sum(dlog * step, axis=0, keepdims=True) * rate, (8, HEADS)
    )
    draw = (sum_heads(heads_in * dweighted[...], gatherer) + dlog * rate) * slope_ref[...]
    ddtb_ref[...] += jnp.broadcast_to(jnp.sum(draw, axis=0, keepdims=True), (8, HEADS))
    here = pl.ds(pl.multiple_of(q * CUT, CUT), CUT)
    width = dproj_ref.shape[1]
    dproj_ref[here, MIXED:width] = jnp.concatenate(
        [draw, jnp.zeros((CUT, width - RATED), F32)], axis=1
    )

    window[0:EDGE, :] = halo_ref[:, 0:MIXED]
    window[EDGE : EDGE + CUT, :] = proj_ref[:, 0:MIXED]

    def conv(c, carry):
        cols = pl.ds(pl.multiple_of(c * 256, 256), 256)
        out = conv_chunk(window, taps_ref, bias_ref, cols)
        sg = jax.nn.sigmoid(out)
        dout = dact[:, cols] * (sg * (1.0 + out * (1.0 - sg)))
        dwindow[0:CUT, cols] = dout
        dbias_ref[:, cols] += jnp.sum(dout.reshape(CUT // 8, 8, 256), axis=0)
        for k in range(CONV):
            at = EDGE - 3 + k
            dtaps_ref[8 * k : 8 * k + 8, cols] += jnp.sum(
                (dout * window[at : at + CUT, cols]).reshape(CUT // 8, 8, 256), axis=0
            )
        din = taps_ref[CONV - 1 : CONV, cols] * dout
        for k in range(CONV - 1):
            din = din + taps_ref[k : k + 1, cols] * dwindow[3 - k : 3 - k + CUT, cols]
        dproj_ref[here, cols] = din
        return carry

    lax.fori_loop(0, MIXED // 256, conv, 0)

    @pl.when(q == 0)
    def _():
        rows = cuts * CUT
        window[0:EDGE, :] = jnp.zeros((EDGE, MIXED), F32)
        window[EDGE : 2 * EDGE, :] = dwindow[0:EDGE, :]
        din = taps_ref[CONV - 1 : CONV, :] * window[0:EDGE, :]
        for k in range(CONV - 1):
            din = din + taps_ref[k : k + 1, :] * window[3 - k : 3 - k + EDGE, :]
        dproj_ref[rows : rows + EDGE, 0:MIXED] = din
        dproj_ref[rows : rows + EDGE, MIXED:width] = jnp.zeros((EDGE, width - MIXED), F32)


def log_rows_to_columns(ref):
    return ref[...].T


def back(
    act, step, slope, logd, dy, local, entering, before, gin, gout, proj, taps, bias, a_log, skip,
    spreader, gatherer,
):
    rows = act.shape[0]
    cuts = rows // CUT
    width = proj.shape[1]

    def at(size):
        return pl.BlockSpec((CUT, size), lambda i: (cuts - 1 - i, 0))

    def halo(i):
        q = cuts - 1 - i
        return (jnp.where(q == 0, rows // EDGE, q * (CUT // EDGE) - 1), 0)

    return pl.pallas_call(
        back_kernel,
        grid=(cuts,),
        in_specs=[
            at(MIXED),
            at(HEADS),
            at(HEADS),
            at(HEADS),
            at(DI),
            pl.BlockSpec((1, STATE, DI), lambda i: (jnp.maximum(cuts - 2 - i, 0), 0, 0)),
            full((STATE, DI)),
            pl.BlockSpec((8, HEADS), lambda i: (cuts - 1 - i, 0)),
            pl.BlockSpec((1, STATE, DI), lambda i: (jnp.minimum(cuts - i, cuts - 1), 0, 0)),
            full((STATE, DI)),
            at(width),
            pl.BlockSpec((EDGE, width), halo),
            full((CONV, MIXED)),
            full((1, MIXED)),
            full((1, HEADS)),
            full((1, DI)),
            full((3 * HEADS, DI)),
            full((DI, HEADS)),
        ],
        out_specs=[
            full((rows + EDGE, width)),
            full((8 * CONV, MIXED)),
            full((8, MIXED)),
            full((8, HEADS)),
            full((8, HEADS)),
        ],
        out_shape=[
            jax.ShapeDtypeStruct((rows + EDGE, width), F32),
            jax.ShapeDtypeStruct((8 * CONV, MIXED), F32),
            jax.ShapeDtypeStruct((8, MIXED), F32),
            jax.ShapeDtypeStruct((8, HEADS), F32),
            jax.ShapeDtypeStruct((8, HEADS), F32),
        ],
        scratch_shapes=[
            pltpu.VMEM((CUT, DI), F32),
            pltpu.VMEM((CUT, DI), F32),
            pltpu.VMEM((CUT, DI), F32),
            pltpu.VMEM((HEADS, CUT), F32),
            pltpu.VMEM((HEADS, CUT), F32),
            pltpu.VMEM((CUT, CUT), F32),
            pltpu.VMEM((CUT, CUT), F32),
            pltpu.VMEM((CUT, CUT), F32),
            pltpu.VMEM((CUT, MIXED), F32),
            pltpu.VMEM((CUT + EDGE, MIXED), F32),
            pltpu.VMEM((CUT + EDGE, MIXED), F32),
            pltpu.VMEM((8, HEADS), F32),
        ],
        compiler_params=params(),
        cost_estimate=pl.CostEstimate(
            flops=60 * rows * STATE * DI, bytes_accessed=40_000_000, transcendentals=rows * CUT * HEADS
        ),
        name="back",
    )(
        act, step, slope, logd, dy, local, entering, before, gin, gout, proj, proj, taps, bias,
        a_log, skip, spreader, gatherer,
    )


def head_spreader():
    head = lax.broadcasted_iota(jnp.int32, (3 * HEADS, DI), 0) % HEADS
    return (head == lax.broadcasted_iota(jnp.int32, (3 * HEADS, DI), 1) // HDIM).astype(BF16)


def head_gatherer():
    channel = lax.broadcasted_iota(jnp.int32, (DI, HEADS), 0) // HDIM
    return (channel == lax.broadcasted_iota(jnp.int32, (DI, HEADS), 1)).astype(BF16)


def per_device(
    hidden_in,
    lengths,
    norm_gain,
    in_weight,
    conv_weight,
    conv_bias,
    dt_bias,
    a_log,
    skip_gain,
    gated_gain,
    out_weight,
    cotangent,
):
    width = hidden_in.shape[-1]
    devices = 1
    for axis in AXES:
        devices *= lax.axis_size(axis)
    mine, place = (lax.axis_index("p"), lax.axis_index("zc"))
    hidden = to_span(hidden_in, mine)
    rows = hidden.shape[0]
    own_rows = width // devices

    in_piece = in_weight.reshape(own_rows, -1)
    small = jnp.concatenate([conv_weight, conv_bias])
    extra = -(-small.shape[0] // own_rows)
    padded = jnp.pad(small, (0, extra * own_rows - small.shape[0])).reshape(own_rows, extra)
    w_conv = jnp.concatenate(
        gather_matrix(jnp.concatenate([in_piece[:, DI:], padded], axis=1)), axis=1
    )
    w_gate = jnp.concatenate(gather_matrix(in_piece[:, :DI]), axis=1)
    w_out = jnp.concatenate(gather_matrix(out_weight.reshape(-1, width)), axis=1)
    smalls = w_conv[:, RATED:].reshape(devices, own_rows * extra)
    taps = smalls[:, : conv_weight.shape[0]].reshape(CONV, MIXED)
    bias = smalls[:, conv_weight.shape[0] : small.shape[0]].reshape(1, MIXED)

    count = lax.axis_size("zc")
    edge = lax.ppermute(hidden[rows - EDGE :], "zc", [(i, i + 1) for i in range(count - 1)])
    extended = jnp.concatenate([hidden, edge], axis=0)
    scale = lax.rsqrt(jnp.mean(extended * extended, axis=1, keepdims=True) + epsilon)
    unit = extended * scale
    normed = unit * norm_gain
    spreader, gatherer = (head_spreader(), head_gatherer())
    dt_row, alog_row = (dt_bias.reshape(1, -1), a_log.reshape(1, -1))
    proj = nn(normed, w_conv)
    act, step, slope, logd, local, before, total = prepare(
        proj, taps, bias, dt_row, alog_row, spreader
    )
    total_row = jnp.repeat(total[0], HDIM).reshape(1, DI)
    entering = chain(total_row, local[-1], False)
    gate_in = nn(normed[:rows], w_gate)
    positions = place * rows + lax.iota(jnp.int32, rows)
    length = lax.dynamic_index_in_dim(lengths, mine, 0, keepdims=False)
    valid = (positions < length).astype(F32)[:, None]
    grad_out = to_span(cotangent, mine) * valid
    dng = nt(grad_out, w_out)
    skip_row = jnp.repeat(skip_gain, HDIM).reshape(1, DI)
    ng, dy, dz, gin, ggrad, skipg = mixer(
        act, step, logd, gate_in, dng, local, entering, before, skip_row,
        gated_gain.reshape(1, DI), spreader,
    )
    gout = chain(total_row, gin[0], True)
    grad_wout = scatter_matrix(tn(ng, grad_out))
    output = from_span((hidden + nn(ng, w_out)) * valid, mine)
    grad_wgate = scatter_matrix(tn(normed[:rows], dz))
    dproj, dtaps, dbias, dlog, ddtb = back(
        act, step, slope, logd, dy, local, entering, before, gin, gout, proj, taps, bias,
        alog_row, skip_row, spreader, gatherer,
    )
    dtaps = jnp.sum(dtaps.reshape(CONV, 8, MIXED), axis=1).reshape(devices, -1)
    dbias = jnp.sum(dbias, axis=0).reshape(devices, -1)
    dsmall = jnp.concatenate([dtaps, dbias], axis=1)
    dsmall = jnp.pad(dsmall, ((0, 0), (0, extra * own_rows - small.shape[0])))
    grad_wconv = scatter_matrix(
        jnp.concatenate([tn(normed, dproj)[:, :RATED], dsmall.reshape(width, extra)], axis=1)
    )
    dnormed = nt(dproj[:, :RATED], w_conv[:, :RATED])
    returned = lax.ppermute(dnormed[rows:], "zc", [(i + 1, i) for i in range(count - 1)])
    dnormed = dnormed[:rows] + nt(dz, w_gate)
    dnormed = jnp.concatenate([dnormed[: rows - EDGE], dnormed[rows - EDGE :] + returned], axis=0)
    unit = unit[:rows]
    dunit = dnormed * norm_gain
    dhidden = scale[:rows] * (dunit - unit * jnp.mean(dunit * unit, axis=1, keepdims=True))
    grad_input = from_span(grad_out + dhidden, mine)
    grad_skip = jnp.sum(jnp.sum(skipg, axis=0).reshape(HEADS, HDIM), axis=1)
    sums = jnp.concatenate(
        [
            jnp.sum(dnormed * unit, axis=0),
            jnp.sum(ggrad, axis=0),
            ddtb[0],
            dlog[0],
            grad_skip,
        ]
    )
    sums = sum_everywhere(jnp.pad(sums, (0, -sums.shape[0] % 128)).reshape(-1, 128)).reshape(-1)
    parts = []
    for size in (width, DI, HEADS, HEADS, HEADS):
        parts.append(sums[:size])
        sums = sums[size:]
    small_grad = grad_wconv[:, RATED:].reshape(-1)
    return (
        output,
        grad_input,
        parts[0],
        jnp.concatenate([grad_wgate, grad_wconv[:, :RATED]], axis=1).reshape(-1),
        small_grad[: conv_weight.shape[0]],
        small_grad[conv_weight.shape[0] : small.shape[0]],
        parts[2],
        parts[3],
        parts[4],
        parts[1],
        grad_wout.reshape(-1),
    )


def solution(mesh):
    dp, seq = (mesh.shape["dp"], mesh.shape["seq"])
    finer = Mesh(mesh.devices.reshape(dp // 2, 2, seq // 2, 2), AXES)
    over_dp, over_seq = (("y", "core"), ("zc", "p"))
    tokens = P(over_dp, over_seq, None)
    in_specs = (
        tokens, P(over_dp), P(), P(AXES), P(AXES), P(AXES), P(), P(), P(), P(), P(AXES), tokens,
    )
    out_specs = (
        tokens, tokens, P(), P(AXES), P(AXES), P(AXES), P(), P(), P(), P(), P(AXES),
    )
    return jax.shard_map(
        per_device, mesh=finer, in_specs=in_specs, out_specs=out_specs, check_vma=False
    )
```

```python
import functools

import jax
import jax.numpy as jnp
from jax import lax
from jax.experimental import pallas as pl
from jax.experimental.pallas import tpu as pltpu
from jax.sharding import Mesh
from jax.sharding import PartitionSpec as P

DI = 2048
HEADS = 32
HDIM = 64
STATE = 128
CONV = 4
MIXED = DI + 2 * STATE
RATED = MIXED + HEADS
CUT = 128
EDGE = 8
PAIR = 2 * HDIM
SPARE = 128 - HEADS
WIDE = RATED + SPARE
STRIP = 128
BLOCK = 512
F32 = jnp.float32
BF16 = jnp.bfloat16
HIGH = lax.Precision.HIGH
EXACT = lax.Precision.HIGHEST
epsilon = 1e-05
FREE = pl.CostEstimate(flops=0, bytes_accessed=0, transcendentals=0)


def shift(block, axis, step=1):
    count = lax.axis_size(axis)
    return lax.ppermute(block, axis, [(i, (i + step) % count) for i in range(count)])


AXES = ("y", "core", "zc", "p")


def offsets(block, axis):
    count = lax.axis_size(axis)
    return [block] + [shift(block, axis, k) for k in range(1, count)]


def ring(block, axis):
    held = [block]
    for _ in range(1, lax.axis_size(axis)):
        held.append(shift(held[-1], axis))
    return held


def after(value, *others):
    return lax.optimization_barrier((value,) + others)[0]


def place_kernel(count, own_rows, where_ref, *refs):
    blocks, whole = (refs[:count], refs[count])
    spot = 0
    for block in blocks:
        for k in range(block.shape[0] // own_rows):
            at = pl.multiple_of(where_ref[spot] * own_rows, own_rows)
            whole[pl.ds(at, own_rows), :] = block[k * own_rows : (k + 1) * own_rows, :]
            spot += 1


def place(blocks, own_rows):
    sizes = {axis: lax.axis_size(axis) for axis in AXES}
    index = {axis: lax.axis_index(axis) for axis in AXES}
    devices = 1
    for axis in AXES:
        devices *= sizes[axis]
    where = []
    for slot, lines, _ in blocks:
        for k in lines:
            at = 0
            for axis in AXES:
                back = k if axis == "zc" else slot.get(axis, 0)
                at = at * sizes[axis] + (index[axis] - back) % sizes[axis]
            where.append(at)
    arrays = [block for _, _, block in blocks]
    cols = arrays[0].shape[1]
    if own_rows % 8:
        whole = jnp.zeros((devices, own_rows, cols), F32)
        spots = iter(where)
        for block in arrays:
            for k in range(block.shape[0] // own_rows):
                whole = lax.dynamic_update_slice_in_dim(
                    whole, block[None, k * own_rows : (k + 1) * own_rows], next(spots), 0
                )
        return whole.reshape(devices * own_rows, cols)
    return pl.pallas_call(
        functools.partial(place_kernel, len(blocks), own_rows),
        in_specs=[pl.BlockSpec(memory_space=pltpu.SMEM)]
        + [pl.BlockSpec(memory_space=pltpu.VMEM)] * len(blocks),
        out_specs=pl.BlockSpec(memory_space=pltpu.VMEM),
        out_shape=jax.ShapeDtypeStruct((devices * own_rows, cols), F32),
        compiler_params=pltpu.CompilerParams(vmem_limit_bytes=32 * 1024 * 1024),
        cost_estimate=FREE,
        name="place",
    )(jnp.stack(where).astype(jnp.int32), *arrays)


def tied(values, *others):
    return list(lax.optimization_barrier((tuple(values), tuple(others)))[0])


class Gather:
    def __init__(self, piece):
        self.piece, self.rows = (piece, piece.shape[0])

    def line(self, *tie):
        (piece,) = tied([self.piece], *tie)
        self.lines = list(range(lax.axis_size("zc")))
        self.block = jnp.concatenate(offsets(piece, "zc"), axis=0)

    def line_at_once(self, *tie):
        (piece,) = tied([self.piece], *tie)
        count, index = (lax.axis_size("zc"), lax.axis_index("zc"))
        whole = lax.all_to_all(jnp.broadcast_to(piece, (count,) + piece.shape), "zc", 0, 0)
        self.lines = [index - k for k in range(count)]
        self.block = whole.reshape(-1, piece.shape[1])

    def near(self, *tie):
        (block,) = tied([self.block], *tie)
        self.rings = {axis: ring(block, axis)[1:] for axis in ("p", "y")}
        return [b for r in self.rings.values() for b in r]

    def far(self, *tie):
        middle = len(self.lines) // 2
        cut = middle * self.rows
        sides = {"p": [b[:cut] for b in self.rings["p"]], "y": [b[cut:] for b in self.rings["y"]]}
        other = {"p": "y", "y": "p"}
        self.corners = []
        for axis, blocks in sides.items():
            lines = self.lines[:middle] if axis == "p" else self.lines[middle:]
            blocks = tied(blocks, *tie)
            for k, block in enumerate(blocks):
                for n, moved in enumerate(ring(block, other[axis])[1:]):
                    self.corners.append(({axis: k + 1, other[axis]: n + 1}, lines, moved))
        return [b for _, _, b in self.corners]

    def held_near(self):
        near = [
            ({axis: k + 1}, self.lines, b) for axis, r in self.rings.items() for k, b in enumerate(r)
        ]
        return [({}, self.lines, self.block)] + near

    def held(self):
        return self.held_near() + self.corners

    def across(self, blocks, *tie):
        arrays = tied([b for _, _, b in blocks], *tie)
        return [
            ({**slot, "core": 1}, lines, shift(b, "core"))
            for (slot, lines, _), b in zip(blocks, arrays)
        ]


def indexed(addends, at, dim):
    total = None
    for addend in addends:
        part = lax.dynamic_index_in_dim(addend, at, dim, keepdims=False)
        total = part if total is None else total + part
    return total


class Scatter:
    def __init__(self, send, keep):
        self.shape = [lax.axis_size(a) for a in ("y", "zc", "p")] + [-1, keep.shape[-1]]
        moved = shift(send, "core")
        self.came = [moved]
        both = [keep.reshape(self.shape), moved.reshape(self.shape)]
        middle = self.shape[1] // 2
        self.parts = [
            ([v[:, :middle] for v in both], ["y", "zc", "p"]),
            ([v[:, middle:] for v in both], ["y", "zc", "p"]),
        ]

    def stage(self, axes, *tie):
        self.came, parts = ([], [])
        for (addends, left), axis in zip(self.parts, axes):
            count, index, dim = (lax.axis_size(axis), lax.axis_index(axis), left.index(axis))
            came = []
            for k in range(1, count):
                moving = indexed(addends, (index + k) % count, dim)
                if tie:
                    moving = after(moving, *tie)
                came.append(shift(moving, axis, k))
            kept = [lax.dynamic_index_in_dim(v, index, dim, keepdims=False) for v in addends]
            parts.append((kept + came, [a for a in left if a != axis]))
            self.came += came
        self.parts = parts

    def last(self, *tie):
        count, index = (lax.axis_size("zc"), lax.axis_index("zc"))
        line = jnp.concatenate([functools.reduce(jnp.add, v) for v, _ in self.parts], axis=0)
        if tie:
            line = after(line, *tie)
        self.came = [
            shift(lax.dynamic_index_in_dim(line, (index + k) % count, 0, keepdims=False), "zc", k)
            for k in range(1, count)
        ]
        self.kept = lax.dynamic_index_in_dim(line, index, 0, keepdims=False)

    def last_at_once(self, *tie):
        line = jnp.concatenate([functools.reduce(jnp.add, v) for v, _ in self.parts], axis=0)
        (line,) = tied([line], *tie)
        line = lax.all_to_all(line, "zc", 0, 0)
        self.came, self.kept = ([line[k] for k in range(1, line.shape[0])], line[0])

    def result(self):
        return functools.reduce(jnp.add, self.came, self.kept)


def sum_everywhere(values):
    for axis in ("core", "p", "y", "zc"):
        count, index = (lax.axis_size(axis), lax.axis_index(axis))
        if count == 2:
            values = values + shift(values, axis)
        else:
            held = jnp.stack(offsets(values, axis))
            total = None
            for k in range(count):
                part = lax.dynamic_index_in_dim(held, (index - k) % count, 0, keepdims=False)
                total = part if total is None else total + part
            values = total
    return values


def to_span(block, mine):
    keep = lax.dynamic_index_in_dim(block, mine, 0, keepdims=False)
    other = shift(lax.dynamic_index_in_dim(block, 1 - mine, 0, keepdims=False), "p")
    first = mine == 0
    return jnp.concatenate([jnp.where(first, keep, other), jnp.where(first, other, keep)], axis=0)


def from_span(span, mine):
    block = span.reshape(2, -1, span.shape[-1])
    keep = lax.dynamic_index_in_dim(block, mine, 0, keepdims=False)
    other = shift(lax.dynamic_index_in_dim(block, 1 - mine, 0, keepdims=False), "p")
    first = mine == 0
    return jnp.stack([jnp.where(first, keep, other), jnp.where(first, other, keep)], axis=0)


class States:
    chunks = 1

    def __init__(self, decay, added, reverse):
        self.count, self.reverse, self.distance = (lax.axis_size("zc"), reverse, 1)
        rows = added.shape[0] // self.chunks
        decay = jnp.broadcast_to(decay, (8, added.shape[1]))
        self.decay = decay
        self.added = [added[k * rows : (k + 1) * rows] for k in range(self.chunks)]
        self.held = [None] * self.chunks
        self.span = None

    def send(self, *tie):
        w = self.distance
        pairs = [(i, i + w) for i in range(self.count - w)]
        route = [(b, a) if self.reverse else (a, b) for a, b in pairs]
        came = []
        for k in range(self.chunks):
            block = self.added[k]
            if self.held[k] is not None:
                block = block + self.decay[0:1] * self.held[k]
            if k == 0 and 2 * w < self.count:
                span = self.decay if self.span is None else self.decay * self.span
                block = jnp.concatenate([block, span], axis=0)
            if tie:
                block = after(block, *tie)
            came.append(lax.ppermute(block, "zc", route))
        rows = self.added[0].shape[0]
        for k in range(self.chunks):
            new = came[k][:rows]
            if self.held[k] is not None:
                new = self.held[k] + self.span[0:1] * new
            self.held[k] = new
        if 2 * w < self.count:
            span = came[0][rows:]
            self.span = span if self.span is None else self.span * span
        self.distance = 2 * w
        return came

    def result(self, *tie):
        while self.distance < self.count:
            self.send(*tie)
        return jnp.concatenate(self.held, axis=0)


def nn(a, b, precision=HIGH):
    return jnp.dot(a, b, precision=precision, preferred_element_type=F32)


def nt(a, b, precision=HIGH):
    return lax.dot_general(
        a, b, (((1,), (1,)), ((), ())), precision=precision, preferred_element_type=F32
    )


def tn(a, b, precision=HIGH):
    return lax.dot_general(
        a, b, (((0,), (0,)), ((), ())), precision=precision, preferred_element_type=F32
    )


def bf16_dot(a, b):
    return jnp.dot(a, b, preferred_element_type=F32)


def split_heads(values):
    top = values.astype(BF16)
    rest = values - top.astype(F32)
    mid = rest.astype(BF16)
    low = (rest - mid.astype(F32)).astype(BF16)
    return jnp.concatenate([top, mid, low], axis=1)


def spread_heads(values, spreader):
    return bf16_dot(split_heads(values), spreader)


def sum_heads(values, gatherer):
    top = values.astype(BF16)
    low = (values - top.astype(F32)).astype(BF16)
    return jnp.dot(top, gatherer, preferred_element_type=F32) + jnp.dot(
        low, gatherer, preferred_element_type=F32
    )


def order_mask(shape, kind):
    row, column = (lax.broadcasted_iota(jnp.int32, shape, d) for d in (0, 1))
    return {"ge": row >= column, "gt": row > column, "le": row <= column, "lt": row < column}[kind]


def triangle(kind):
    return jnp.where(order_mask((CUT, CUT), kind), 1.0, 0.0).astype(F32)


def conv_chunk(window_ref, taps_ref, bias_ref, cols):
    total = bias_ref[:, cols] + taps_ref[0:1, cols] * window_ref[EDGE - 3 : EDGE - 3 + CUT, cols]
    for k in range(1, CONV):
        at = EDGE - 3 + k
        total = total + taps_ref[k : k + 1, cols] * window_ref[at : at + CUT, cols]
    return total


def prepare_kernel(
    proj_ref,
    edge_ref,
    taps_ref,
    bias_ref,
    dtb_ref,
    alog_ref,
    spreader_ref,
    act_ref,
    step_ref,
    slope_ref,
    logd_ref,
    local_ref,
    before_ref,
    total_ref,
    window,
    state,
    logs,
):
    q = pl.program_id(0)

    @pl.when(q == 0)
    def _():
        window[0:EDGE, :] = edge_ref[:, 0:MIXED]
        state[...] = jnp.zeros_like(state)
        logs[...] = jnp.zeros_like(logs)

    @pl.when(q > 0)
    def _():
        window[0:EDGE, :] = window[CUT : CUT + EDGE, :]

    window[EDGE : EDGE + CUT, :] = proj_ref[:, 0:MIXED]

    def conv(c, carry):
        cols = pl.ds(pl.multiple_of(c * STRIP, STRIP), STRIP)
        out = conv_chunk(window, taps_ref, bias_ref, cols)
        act_ref[:, cols] = out * jax.nn.sigmoid(out)
        return carry

    lax.fori_loop(0, MIXED // STRIP, conv, 0, unroll=3)
    raw = proj_ref[:, MIXED:RATED] + dtb_ref[...]
    step = jnp.maximum(raw, 0.0) + jnp.log1p(jnp.exp(-jnp.abs(raw)))
    logd = nn(triangle("ge"), -jnp.exp(alog_ref[...]) * step, EXACT)
    step_ref[...] = step
    slope_ref[...] = jax.nn.sigmoid(raw)
    logd_ref[...] = logd
    last = logd[CUT - 1 : CUT, :]
    tail = spread_heads(jnp.exp(last - logd) * step, spreader_ref[...])
    added = tn(act_ref[:, DI : DI + STATE], act_ref[:, 0:DI] * tail)
    decay = spread_heads(jnp.broadcast_to(jnp.exp(last), (8, HEADS)), spreader_ref[...])
    state[...] = state[...] * decay[0:1, :] + added
    local_ref[0] = state[...]
    before_ref[...] = jnp.exp(logs[...])
    logs[...] = logs[...] + jnp.broadcast_to(last, (8, HEADS))
    total_ref[...] = jnp.exp(logs[...])


def full(shape):
    return pl.BlockSpec(shape, lambda i: (0,) * len(shape))


def params():
    return pltpu.CompilerParams(
        dimension_semantics=("arbitrary",), vmem_limit_bytes=52 * 1024 * 1024
    )


def prepare(proj, taps, bias, dt_bias, a_log, spreader):
    rows = proj.shape[0] - EDGE
    cuts = rows // CUT
    return pl.pallas_call(
        prepare_kernel,
        grid=(cuts,),
        in_specs=[
            pl.BlockSpec((CUT, WIDE), lambda i: (i, 0)),
            pl.BlockSpec((EDGE, WIDE), lambda i: (rows // EDGE, 0)),
            full((CONV, MIXED)),
            full((1, MIXED)),
            full((1, HEADS)),
            full((1, HEADS)),
            full((3 * HEADS, DI)),
        ],
        out_specs=[
            pl.BlockSpec((CUT, MIXED), lambda i: (i, 0)),
            pl.BlockSpec((CUT, HEADS), lambda i: (i, 0)),
            pl.BlockSpec((CUT, HEADS), lambda i: (i, 0)),
            pl.BlockSpec((CUT, HEADS), lambda i: (i, 0)),
            pl.BlockSpec((1, STATE, DI), lambda i: (i, 0, 0)),
            pl.BlockSpec((8, HEADS), lambda i: (i, 0)),
            full((8, HEADS)),
        ],
        out_shape=[
            jax.ShapeDtypeStruct((rows, MIXED), F32),
            jax.ShapeDtypeStruct((rows, HEADS), F32),
            jax.ShapeDtypeStruct((rows, HEADS), F32),
            jax.ShapeDtypeStruct((rows, HEADS), F32),
            jax.ShapeDtypeStruct((cuts, STATE, DI), F32),
            jax.ShapeDtypeStruct((8 * cuts, HEADS), F32),
            jax.ShapeDtypeStruct((8, HEADS), F32),
        ],
        scratch_shapes=[
            pltpu.VMEM((CUT + EDGE, MIXED), F32),
            pltpu.VMEM((STATE, DI), F32),
            pltpu.VMEM((8, HEADS), F32),
        ],
        compiler_params=params(),
        cost_estimate=FREE,
        name="prepare",
    )(proj, proj, taps, bias, dt_bias, a_log, spreader)


def both_columns(pair, left):
    turned = pltpu.roll(pair, HDIM, 1)
    return (jnp.where(left, pair, turned), jnp.where(left, turned, pair))


def stacked_pair(pair, left):
    zero = jnp.zeros_like(pair)
    return jnp.concatenate([jnp.where(left, pair, zero), jnp.where(left, zero, pair)], axis=0)


UNROLL = 8


def intra_kernel(
    act_ref, step_ref, logd_ref, skip_ref, spreader_ref, out_ref, logx, weighted, log_rows, scores
):
    spreader = spreader_ref[...]
    logd = logd_ref[...]
    logx[...] = spread_heads(logd, spreader)
    log_rows[...] = logd.T
    heads_in = act_ref[:, 0:DI]
    weighted[...] = heads_in * spread_heads(step_ref[...], spreader)
    scores[...] = nt(act_ref[:, DI + STATE : MIXED], act_ref[:, DI : DI + STATE])

    def pair(j, carry):
        cols = pl.ds(pl.multiple_of(j * PAIR, PAIR), PAIR)
        left = lax.broadcasted_iota(jnp.int32, (CUT, PAIR), 1) < HDIM
        mask = order_mask((CUT, CUT), "ge")
        mixes = []
        for side, column in enumerate(both_columns(logx[:, cols], left)):
            row = log_rows[pl.ds(2 * j + side, 1), :]
            mixes.append(jnp.exp(jnp.where(mask, column - row, -1e30)) * scores[...])
        out_ref[:, cols] = skip_ref[:, cols] * act_ref[:, cols] + nn(
            jnp.concatenate(mixes, axis=1), stacked_pair(weighted[:, cols], left)
        )
        return carry

    lax.fori_loop(0, HEADS // 2, pair, 0, unroll=UNROLL)


def intra(act, step, logd, skip, spreader):
    rows = act.shape[0]

    def at(width):
        return pl.BlockSpec((CUT, width), lambda i: (i, 0))

    return pl.pallas_call(
        intra_kernel,
        grid=(rows // CUT,),
        in_specs=[at(MIXED), at(HEADS), at(HEADS), full((1, DI)), full((3 * HEADS, DI))],
        out_specs=at(DI),
        out_shape=jax.ShapeDtypeStruct((rows, DI), F32),
        scratch_shapes=[
            pltpu.VMEM((CUT, DI), F32),
            pltpu.VMEM((CUT, DI), F32),
            pltpu.VMEM((HEADS, CUT), F32),
            pltpu.VMEM((CUT, CUT), F32),
        ],
        compiler_params=params(),
        cost_estimate=FREE,
        name="intra",
    )(act, step, logd, skip, spreader)


def mixer_kernel(
    act_ref,
    logd_ref,
    inner_ref,
    gate_ref,
    dng_ref,
    local_ref,
    enter_ref,
    before_ref,
    ggain_ref,
    spreader_ref,
    ng_ref,
    dy_ref,
    dz_ref,
    gin_ref,
    ggrad_ref,
    skipg_ref,
    grown,
    out,
    gstate,
):
    i = pl.program_id(0)
    q = pl.num_programs(0) - 1 - i
    spreader = spreader_ref[...]

    @pl.when(i == 0)
    def _():
        gstate[...] = jnp.zeros_like(gstate)
        ggrad_ref[...] = jnp.zeros_like(ggrad_ref)
        skipg_ref[...] = jnp.zeros_like(skipg_ref)

    logd = logd_ref[...]
    grown[...] = spread_heads(jnp.exp(logd), spreader)
    before = spread_heads(before_ref[...], spreader)[0:1, :]
    entering = enter_ref[...] * before + jnp.where(q == 0, 0.0, local_ref[0])
    c_state = act_ref[:, DI + STATE : MIXED]
    out[...] = grown[...] * nn(c_state, entering) + inner_ref[...]

    def gate(k, carry):
        rows = pl.ds(pl.multiple_of(k * 8, 8), 8)
        ssd = out[rows, :]
        gate_in = gate_ref[rows, :]
        sg = jax.nn.sigmoid(gate_in)
        silu = gate_in * sg
        gated = ssd * silu
        scale = lax.rsqrt(jnp.mean(gated * gated, axis=1, keepdims=True) + epsilon)
        unit = gated * scale
        ng_ref[rows, :] = unit * ggain_ref[...]
        dng = dng_ref[rows, :]
        e = dng * ggain_ref[...]
        ggrad_ref[...] += dng * unit
        dgated = scale * (e - unit * jnp.mean(e * unit, axis=1, keepdims=True))
        dy = dgated * silu
        dy_ref[rows, :] = dy
        dz_ref[rows, :] = dgated * ssd * (sg * (1.0 + gate_in * (1.0 - sg)))
        skipg_ref[...] += dy * act_ref[rows, 0:DI]
        return carry

    lax.fori_loop(0, CUT // 8, gate, 0, unroll=GATE_UNROLL)
    gstate[...] = gstate[...] * grown[CUT - 1 : CUT, :] + tn(c_state, grown[...] * dy_ref[...])
    gin_ref[0] = gstate[...]


GATE_UNROLL = 4


def mixer(act, logd, inner, gate_in, dng, local, entering, before, ggain, spreader):
    rows = act.shape[0]
    cuts = rows // CUT

    def back(width):
        return pl.BlockSpec((CUT, width), lambda i: (cuts - 1 - i, 0))

    wide = jax.ShapeDtypeStruct((rows, DI), F32)
    return pl.pallas_call(
        mixer_kernel,
        grid=(cuts,),
        in_specs=[
            back(MIXED),
            back(HEADS),
            back(DI),
            back(DI),
            back(DI),
            pl.BlockSpec((1, STATE, DI), lambda i: (jnp.maximum(cuts - 2 - i, 0), 0, 0)),
            full((STATE, DI)),
            pl.BlockSpec((8, HEADS), lambda i: (cuts - 1 - i, 0)),
            full((1, DI)),
            full((3 * HEADS, DI)),
        ],
        out_specs=[
            back(DI),
            back(DI),
            back(DI),
            pl.BlockSpec((1, STATE, DI), lambda i: (cuts - 1 - i, 0, 0)),
            full((8, DI)),
            full((8, DI)),
        ],
        out_shape=[
            wide,
            wide,
            wide,
            jax.ShapeDtypeStruct((cuts, STATE, DI), F32),
            jax.ShapeDtypeStruct((8, DI), F32),
            jax.ShapeDtypeStruct((8, DI), F32),
        ],
        scratch_shapes=[
            pltpu.VMEM((CUT, DI), F32),
            pltpu.VMEM((CUT, DI), F32),
            pltpu.VMEM((STATE, DI), F32),
        ],
        compiler_params=params(),
        cost_estimate=FREE,
        name="mixer",
    )(act, logd, inner, gate_in, dng, local, entering, before, ggain, spreader)


def back_intra_kernel(
    act_ref,
    step_ref,
    logd_ref,
    dy_ref,
    spreader_ref,
    dweighted_ref,
    dstates_ref,
    moved_ref,
    logx,
    weighted,
    log_rows,
    sum_rows,
    scores,
    dscores,
    sum_columns,
):
    spreader = spreader_ref[...]
    logd = logd_ref[...]
    logx[...] = spread_heads(logd, spreader)
    log_rows[...] = logd.T
    weighted[...] = act_ref[:, 0:DI] * spread_heads(step_ref[...], spreader)
    b_state = act_ref[:, DI : DI + STATE]
    c_state = act_ref[:, DI + STATE : MIXED]
    scores[...] = nt(b_state, c_state)
    dscores[...] = jnp.zeros_like(dscores)
    sum_columns[...] = jnp.zeros_like(sum_columns)

    def pair(j, carry):
        cols = pl.ds(pl.multiple_of(j * PAIR, PAIR), PAIR)
        left = lax.broadcasted_iota(jnp.int32, (CUT, PAIR), 1) < HDIM
        mask = order_mask((CUT, CUT), "le")
        strict = order_mask((CUT, CUT), "lt")
        dy = dy_ref[:, cols]
        dmix = nt(stacked_pair(weighted[:, cols], left), dy)
        mixes = []
        lane = lax.broadcasted_iota(jnp.int32, (CUT, CUT), 1)
        for side, column in enumerate(both_columns(logx[:, cols], left)):
            row = log_rows[pl.ds(2 * j + side, 1), :]
            weights = jnp.exp(jnp.where(mask, row - column, -1e30))
            mixes.append(weights * scores[...])
            part = dmix[side * CUT : (side + 1) * CUT, :] * weights
            dscores[...] += part
            moved = jnp.where(strict, part * scores[...], 0.0)
            sum_rows[pl.ds(2 * j + side, 1), :] = jnp.sum(moved, axis=0, keepdims=True)
            sum_columns[...] += jnp.where(
                lane == 2 * j + side, jnp.sum(moved, axis=1, keepdims=True), 0.0
            )
        dweighted_ref[:, cols] = nn(jnp.concatenate(mixes, axis=1), stacked_pair(dy, left))
        return carry

    lax.fori_loop(0, HEADS // 2, pair, 0, unroll=BACK_UNROLL)
    dstates_ref[:, 0:STATE] = nn(dscores[...], c_state)
    dstates_ref[:, STATE : 2 * STATE] = tn(dscores[...], b_state)
    moved_ref[...] = sum_rows[...].T - sum_columns[:, 0:HEADS]


BACK_UNROLL = 4


def back_intra(act, step, logd, dy, spreader):
    rows = act.shape[0]

    def at(width):
        return pl.BlockSpec((CUT, width), lambda i: (i, 0))

    return pl.pallas_call(
        back_intra_kernel,
        grid=(rows // CUT,),
        in_specs=[at(MIXED), at(HEADS), at(HEADS), at(DI), full((3 * HEADS, DI))],
        out_specs=[at(DI), at(2 * STATE), at(HEADS)],
        out_shape=[
            jax.ShapeDtypeStruct((rows, DI), F32),
            jax.ShapeDtypeStruct((rows, 2 * STATE), F32),
            jax.ShapeDtypeStruct((rows, HEADS), F32),
        ],
        scratch_shapes=[
            pltpu.VMEM((CUT, DI), F32),
            pltpu.VMEM((CUT, DI), F32),
            pltpu.VMEM((HEADS, CUT), F32),
            pltpu.VMEM((HEADS, CUT), F32),
            pltpu.VMEM((CUT, CUT), F32),
            pltpu.VMEM((CUT, CUT), F32),
            pltpu.VMEM((CUT, CUT), F32),
        ],
        compiler_params=params(),
        cost_estimate=FREE,
        name="back_intra",
    )(act, step, logd, dy, spreader)


def back_kernel(
    act_ref,
    step_ref,
    slope_ref,
    logd_ref,
    dy_ref,
    dweighted_ref,
    dstates_ref,
    moved_ref,
    local_ref,
    enter_ref,
    before_ref,
    gin_ref,
    gout_ref,
    proj_ref,
    halo_ref,
    taps_ref,
    bias_ref,
    alog_ref,
    skip_ref,
    spreader_ref,
    gatherer_ref,
    dproj_ref,
    dtaps_ref,
    dbias_ref,
    dlog_ref,
    ddtb_ref,
    dact,
    window,
    dwindow,
    after,
):
    i = pl.program_id(0)
    cuts = pl.num_programs(0)
    q = cuts - 1 - i

    @pl.when(i == 0)
    def _():
        after[...] = jnp.zeros_like(after)
        dwindow[...] = jnp.zeros_like(dwindow)
        for ref in (dtaps_ref, dbias_ref, dlog_ref, ddtb_ref):
            ref[...] = jnp.zeros_like(ref)

    @pl.when(i > 0)
    def _():
        dwindow[CUT : CUT + EDGE, :] = dwindow[0:EDGE, :]

    logd = logd_ref[...]
    step = step_ref[...]
    last = logd[CUT - 1 : CUT, :]
    b_state = act_ref[:, DI : DI + STATE]
    c_state = act_ref[:, DI + STATE : MIXED]
    grow_parts = split_heads(jnp.exp(logd))
    tail_parts = split_heads(jnp.exp(last - logd))
    step_parts = split_heads(step)
    before_parts = split_heads(before_ref[...])
    later_parts = split_heads(jnp.exp(after[...]))
    after[...] = after[...] + jnp.broadcast_to(last, (8, HEADS))
    db = dstates_ref[:, 0:STATE]
    dc = dstates_ref[:, STATE : 2 * STATE]
    moved = moved_ref[...]
    lost = jnp.zeros((CUT, HEADS), F32)
    dstep = jnp.zeros((CUT, HEADS), F32)
    kept = jnp.zeros((8, HEADS), F32)
    for c in range(DI // BLOCK):
        cols = slice(c * BLOCK, (c + 1) * BLOCK)
        spreader = spreader_ref[:, cols]
        gatherer = gatherer_ref[cols, :]
        entering = enter_ref[:, cols] * bf16_dot(before_parts, spreader)[0:1, :]
        entering = entering + jnp.where(q == 0, 0.0, local_ref[0, :, cols])
        gout = gout_ref[:, cols] * bf16_dot(later_parts, spreader)[0:1, :]
        gout = gout + jnp.where(i == 0, 0.0, gin_ref[0, :, cols])
        tail = bf16_dot(tail_parts, spreader)
        steps = bf16_dot(step_parts, spreader)
        heads_in = act_ref[:, cols]
        dy = dy_ref[:, cols]
        from_state = tail * nn(b_state, gout)
        stepped = heads_in * steps
        dweighted = dweighted_ref[:, cols] + from_state
        carried = bf16_dot(grow_parts, spreader) * dy
        db = db + nt(tail * stepped, gout)
        dc = dc + nt(carried, entering)
        dact[:, cols] = dweighted * steps + skip_ref[:, cols] * dy
        moved = moved + sum_heads(carried * nn(c_state, entering), gatherer)
        lost = lost + sum_heads(stepped * from_state, gatherer)
        dstep = dstep + sum_heads(heads_in * dweighted, gatherer)
        kept = kept + sum_heads(
            jnp.broadcast_to(jnp.sum(gout * entering, axis=0, keepdims=True), (8, BLOCK)), gatherer
        )
    dact[:, DI : DI + STATE] = db
    dact[:, DI + STATE : MIXED] = dc
    dlog = (
        nn(triangle("le"), moved, EXACT)
        + nn(triangle("gt"), lost, EXACT)
        + jnp.exp(last) * kept[0:1, :]
    )
    rate = -jnp.exp(alog_ref[...])
    dlog_ref[...] += jnp.broadcast_to(
        jnp.sum(dlog * step, axis=0, keepdims=True) * rate, (8, HEADS)
    )
    draw = (dstep + dlog * rate) * slope_ref[...]
    ddtb_ref[...] += jnp.broadcast_to(jnp.sum(draw, axis=0, keepdims=True), (8, HEADS))
    here = pl.ds(pl.multiple_of(q * CUT, CUT), CUT)
    dproj_ref[here, MIXED:WIDE] = jnp.concatenate([draw, jnp.zeros((CUT, SPARE), F32)], axis=1)
    window[0:EDGE, :] = halo_ref[:, 0:MIXED]
    window[EDGE : EDGE + CUT, :] = proj_ref[:, 0:MIXED]

    def conv(c, carry):
        cols = pl.ds(pl.multiple_of(c * STRIP, STRIP), STRIP)
        out = conv_chunk(window, taps_ref, bias_ref, cols)
        sg = jax.nn.sigmoid(out)
        dout = dact[:, cols] * (sg * (1.0 + out * (1.0 - sg)))
        dwindow[0:CUT, cols] = dout
        dbias_ref[:, cols] += jnp.sum(dout.reshape(CUT // 8, 8, STRIP), axis=0)
        for k in range(CONV):
            at = EDGE - 3 + k
            dtaps_ref[8 * k : 8 * k + 8, cols] += jnp.sum(
                (dout * window[at : at + CUT, cols]).reshape(CUT // 8, 8, STRIP), axis=0
            )
        din = taps_ref[CONV - 1 : CONV, cols] * dout
        for k in range(CONV - 1):
            din = din + taps_ref[k : k + 1, cols] * dwindow[3 - k : 3 - k + CUT, cols]
        dproj_ref[here, cols] = din
        return carry

    lax.fori_loop(0, MIXED // STRIP, conv, 0, unroll=3)

    @pl.when(q == 0)
    def _():
        rows = cuts * CUT
        window[0:EDGE, :] = jnp.zeros((EDGE, MIXED), F32)
        window[EDGE : 2 * EDGE, :] = dwindow[0:EDGE, :]
        din = taps_ref[CONV - 1 : CONV, :] * window[0:EDGE, :]
        for k in range(CONV - 1):
            din = din + taps_ref[k : k + 1, :] * window[3 - k : 3 - k + EDGE, :]
        dproj_ref[rows : rows + EDGE, 0:MIXED] = din
        dproj_ref[rows : rows + EDGE, MIXED:WIDE] = jnp.zeros((EDGE, WIDE - MIXED), F32)


def back(
    act, step, slope, logd, dy, dweighted, dstates, moved, local, entering, before, gin, gout, proj, taps, bias, a_log,
    skip, spreader, gatherer,
):
    rows = act.shape[0]
    cuts = rows // CUT

    def at(size):
        return pl.BlockSpec((CUT, size), lambda i: (cuts - 1 - i, 0))

    def halo(i):
        q = cuts - 1 - i
        return (jnp.where(q == 0, rows // EDGE, q * (CUT // EDGE) - 1), 0)

    return pl.pallas_call(
        back_kernel,
        grid=(cuts,),
        in_specs=[
            at(MIXED),
            at(HEADS),
            at(HEADS),
            at(HEADS),
            at(DI),
            at(DI),
            at(2 * STATE),
            at(HEADS),
            pl.BlockSpec((1, STATE, DI), lambda i: (jnp.maximum(cuts - 2 - i, 0), 0, 0)),
            full((STATE, DI)),
            pl.BlockSpec((8, HEADS), lambda i: (cuts - 1 - i, 0)),
            pl.BlockSpec((1, STATE, DI), lambda i: (jnp.minimum(cuts - i, cuts - 1), 0, 0)),
            full((STATE, DI)),
            at(WIDE),
            pl.BlockSpec((EDGE, WIDE), halo),
            full((CONV, MIXED)),
            full((1, MIXED)),
            full((1, HEADS)),
            full((1, DI)),
            full((3 * HEADS, DI)),
            full((DI, HEADS)),
        ],
        out_specs=[
            full((rows + EDGE, WIDE)),
            full((8 * CONV, MIXED)),
            full((8, MIXED)),
            full((8, HEADS)),
            full((8, HEADS)),
        ],
        out_shape=[
            jax.ShapeDtypeStruct((rows + EDGE, WIDE), F32),
            jax.ShapeDtypeStruct((8 * CONV, MIXED), F32),
            jax.ShapeDtypeStruct((8, MIXED), F32),
            jax.ShapeDtypeStruct((8, HEADS), F32),
            jax.ShapeDtypeStruct((8, HEADS), F32),
        ],
        scratch_shapes=[
            pltpu.VMEM((CUT, MIXED), F32),
            pltpu.VMEM((CUT + EDGE, MIXED), F32),
            pltpu.VMEM((CUT + EDGE, MIXED), F32),
            pltpu.VMEM((8, HEADS), F32),
        ],
        compiler_params=params(),
        cost_estimate=FREE,
        name="back",
    )(
        act, step, slope, logd, dy, dweighted, dstates, moved, local, entering, before, gin, gout, proj, proj,
        taps, bias, a_log, skip, spreader, gatherer,
    )


def head_spreader():
    head = lax.broadcasted_iota(jnp.int32, (3 * HEADS, DI), 0) % HEADS
    return (head == lax.broadcasted_iota(jnp.int32, (3 * HEADS, DI), 1) // HDIM).astype(BF16)


def head_gatherer():
    channel = lax.broadcasted_iota(jnp.int32, (DI, HEADS), 0) // HDIM
    return (channel == lax.broadcasted_iota(jnp.int32, (DI, HEADS), 1)).astype(BF16)


def per_device(
    hidden_in,
    lengths,
    norm_gain,
    in_weight,
    conv_weight,
    conv_bias,
    dt_bias,
    a_log,
    skip_gain,
    gated_gain,
    out_weight,
    cotangent,
):
    width = hidden_in.shape[-1]
    devices = 1
    for axis in AXES:
        devices *= lax.axis_size(axis)
    mine, spot, count = (lax.axis_index("p"), lax.axis_index("zc"), lax.axis_size("zc"))
    own_rows = width // devices

    in_piece = in_weight.reshape(own_rows, -1)
    small = jnp.concatenate([conv_weight, conv_bias])
    padded = jnp.pad(small, (0, SPARE * own_rows - small.shape[0])).reshape(own_rows, SPARE)
    conv = Gather(jnp.concatenate([in_piece[:, DI:], padded], axis=1))
    gate = Gather(in_piece[:, :DI])
    out = Gather(out_weight.reshape(-1, width))
    conv.line()
    hidden = to_span(hidden_in, mine)
    rows = hidden.shape[0]
    near = conv.near()
    conv_over = conv.across(conv.held_near()[:1], conv.block)
    far = conv.far(hidden)
    conv_over += conv.across(conv.held_near()[1:])
    gate.line_at_once(conv.block)
    other = to_span(tied([cotangent], *near)[0], mine)
    conv_over += conv.across(conv.corners)
    w_conv = place(conv.held() + conv_over, conv.rows)
    gate_near = gate.near(*far)
    out.line_at_once(gate.block, *far)
    edge = lax.ppermute(
        tied([hidden[rows - EDGE :]], *near)[0], "zc", [(i, i + 1) for i in range(count - 1)]
    )
    smalls = w_conv[:, RATED:].reshape(devices, own_rows * SPARE)
    taps = smalls[:, : conv_weight.shape[0]].reshape(CONV, MIXED)
    bias = smalls[:, conv_weight.shape[0] : small.shape[0]].reshape(1, MIXED)

    extended = jnp.concatenate([hidden, edge], axis=0)
    scale = lax.rsqrt(jnp.mean(extended * extended, axis=1, keepdims=True) + epsilon)
    unit = extended * scale
    normed = unit * norm_gain
    inner = normed[:rows]
    spreader, gatherer = (head_spreader(), head_gatherer())
    dt_row, alog_row = (dt_bias.reshape(1, -1), a_log.reshape(1, -1))
    skip_row = jnp.repeat(skip_gain, HDIM).reshape(1, DI)
    positions = spot * rows + lax.iota(jnp.int32, rows)
    length = lax.dynamic_index_in_dim(lengths, mine, 0, keepdims=False)
    valid = (positions < length).astype(F32)[:, None]
    proj = nn(normed, w_conv)
    act, step, slope, logd, local, before, total = prepare(
        proj, taps, bias, dt_row, alog_row, spreader
    )
    total_row = jnp.repeat(total[0], HDIM).reshape(1, DI)
    states = States(total_row, local[-1], False)
    came = states.send(*gate_near)
    gate_far = gate.far(act)
    gate_over = gate.across(gate.held_near(), act)
    within = intra(act, step, logd, skip_row, spreader)
    out_near = out.near(within, *gate_far)
    while states.distance < count:
        came = states.send()
    gate_over += gate.across(gate.corners, within)
    w_gate = place(gate.held() + gate_over, gate.rows)
    gate_in = nn(tied([inner], within)[0], w_gate)
    out_far = out.far(gate_in)
    out_over = out.across(out.held_near(), gate_in) + out.across(out.corners)
    w_out = place(out.held() + out_over, out.rows)
    grad_out = other * valid
    dng = nt(grad_out, w_out)
    entering = states.result()
    ng, dy, dz, gin, ggrad, skipg = mixer(
        act, logd, within, gate_in, dng, local, entering, before, gated_gain.reshape(1, DI), spreader
    )
    ng_keep, ng_send = core_columns(ng)
    in_keep, in_send = core_columns(normed)
    grads = States(total_row, gin[0], True)
    came = grads.send()
    first = tn(ng_send, grad_out)
    (turn,) = tied([grad_out], first)
    second = tn(ng_keep, turn)
    grad_wout = Scatter(first, second)
    branch = nn(tied([ng], second)[0], w_out)
    (send_from,) = tied([dz], branch, *grad_wout.came)
    grad_wout.stage(("p", "y"))
    first = tn(in_send[:rows], send_from)
    (turn,) = tied([send_from], first)
    second = tn(in_keep[:rows], turn)
    grad_wgate = Scatter(first, second)
    back_parts = back_intra(tied([act], second, *came)[0], step, logd, dy, spreader)
    while grads.distance < count:
        came = grads.send()
    (turn,) = tied([dz], back_parts[1], *grad_wgate.came, *grad_wout.came)
    grad_wout.stage(("y", "p"))
    dgate_normed = nt(turn, w_gate)
    grad_wgate.stage(("p", "y"))
    gout = grads.result()
    dproj, dtaps, dbias, dlog, ddtb = back(
        tied([act], dgate_normed, *grad_wout.came)[0], step, slope, logd, dy, *back_parts, local,
        entering, before, gin, gout, proj, taps, bias, alog_row, skip_row, spreader, gatherer,
    )
    grad_wout.last_at_once()
    dtaps = jnp.sum(dtaps.reshape(CONV, 8, MIXED), axis=1).reshape(devices, -1)
    dbias = jnp.sum(dbias, axis=0).reshape(devices, -1)
    dsmall = jnp.concatenate([dtaps, dbias], axis=1)
    dsmall = jnp.pad(dsmall, ((0, 0), (0, SPARE * own_rows - small.shape[0])))
    dsmall = jnp.pad(dsmall.reshape(width, SPARE), ((0, 0), (RATED, 0)))
    small_keep, small_send = (core_rows(dsmall, k) for k in (0, 1))
    first = tn(in_send, dproj) + small_send
    (turn,) = tied([dproj], first, *grad_wgate.came)
    second = tn(in_keep, turn) + small_keep
    grad_wconv = Scatter(first, second)
    grad_wgate.stage(("y", "p"))
    (turn,) = tied([dproj], second)
    dnormed = nt(turn, w_conv)
    (dnormed,) = tied([dnormed], *grad_wconv.came, *grad_wgate.came)
    grad_wgate.last_at_once()
    grad_wconv.stage(("p", "y"))
    returned = lax.ppermute(dnormed[rows:], "zc", [(i + 1, i) for i in range(count - 1)])
    near = grad_wconv.came
    output = from_span((hidden + branch) * valid, mine)
    grad_wconv.stage(("y", "p"))
    grad_wconv.last()
    dnormed = dnormed[:rows] + dgate_normed
    dnormed = dnormed + jnp.pad(returned, ((rows - EDGE, 0), (0, 0)))
    unit = unit[:rows]
    dunit = dnormed * norm_gain
    dhidden = scale[:rows] * (dunit - unit * jnp.mean(dunit * unit, axis=1, keepdims=True))
    grad_input = from_span(tied([grad_out + dhidden], *near)[0], mine)
    grad_skip = jnp.sum(jnp.sum(skipg, axis=0).reshape(HEADS, HDIM), axis=1)
    sums = jnp.concatenate(
        [
            jnp.sum(dnormed * unit, axis=0),
            jnp.sum(ggrad, axis=0),
            ddtb[0],
            dlog[0],
            grad_skip,
        ]
    )
    (sums,) = tied([jnp.pad(sums, (0, -sums.shape[0] % 128)).reshape(-1, 128)], *near)
    sums = sum_everywhere(sums).reshape(-1)
    parts = []
    for size in (width, DI, HEADS, HEADS, HEADS):
        parts.append(sums[:size])
        sums = sums[size:]
    conv_grad = grad_wconv.result()
    small_grad = conv_grad[:, RATED:].reshape(-1)
    return (
        output,
        grad_input,
        parts[0],
        jnp.concatenate([grad_wgate.result(), conv_grad[:, :RATED]], axis=1).reshape(-1),
        small_grad[: conv_weight.shape[0]],
        small_grad[conv_weight.shape[0] : small.shape[0]],
        parts[2],
        parts[3],
        parts[4],
        parts[1],
        grad_wout.result().reshape(-1),
    )


def core_columns(values):
    size = values.shape[1] // (2 * lax.axis_size("y"))
    core = lax.axis_index("core")
    return [
        jnp.concatenate(
            [
                lax.dynamic_slice_in_dim(values, (2 * y + (core + k) % 2) * size, size, 1)
                for y in range(lax.axis_size("y"))
            ],
            axis=1,
        )
        for k in (0, 1)
    ]


def core_rows(values, k):
    size = values.shape[0] // (2 * lax.axis_size("y"))
    core = lax.axis_index("core")
    return jnp.concatenate(
        [
            lax.dynamic_slice_in_dim(values, (2 * y + (core + k) % 2) * size, size, 0)
            for y in range(lax.axis_size("y"))
        ],
        axis=0,
    )


def solution(mesh):
    dp, seq = (mesh.shape["dp"], mesh.shape["seq"])
    finer = Mesh(mesh.devices.reshape(dp // 2, 2, seq // 2, 2), AXES)
    over_dp, over_seq = (("y", "core"), ("zc", "p"))
    tokens = P(over_dp, over_seq, None)
    in_specs = (
        tokens, P(over_dp), P(), P(AXES), P(AXES), P(AXES), P(), P(), P(), P(), P(AXES), tokens,
    )
    out_specs = (
        tokens, tokens, P(), P(AXES), P(AXES), P(AXES), P(), P(), P(), P(), P(AXES),
    )
    return jax.shard_map(
        per_device, mesh=finer, in_specs=in_specs, out_specs=out_specs, check_vma=False
    )
```

```python
import functools

import jax
import jax.numpy as jnp
from jax import lax
from jax.experimental import pallas as pl
from jax.experimental.pallas import tpu as pltpu
from jax.sharding import Mesh
from jax.sharding import PartitionSpec as P

DI = 2048
HEADS = 32
HDIM = 64
STATE = 128
CONV = 4
MIXED = DI + 2 * STATE
RATED = MIXED + HEADS
CUT = 128
EDGE = 8
PAIR = 2 * HDIM
SPARE = 128 - HEADS
WIDE = RATED + SPARE
STRIP = 128
BLOCK = 512
F32 = jnp.float32
BF16 = jnp.bfloat16
HIGH = lax.Precision.HIGH
EXACT = lax.Precision.HIGHEST
epsilon = 1e-05
FREE = pl.CostEstimate(flops=0, bytes_accessed=0, transcendentals=0)


def shift(block, axis, step=1):
    count = lax.axis_size(axis)
    return lax.ppermute(block, axis, [(i, (i + step) % count) for i in range(count)])


AXES = ("y", "core", "zc", "p")


def offsets(block, axis):
    count = lax.axis_size(axis)
    return [block] + [shift(block, axis, k) for k in range(1, count)]


def ring(block, axis):
    held = [block]
    for _ in range(1, lax.axis_size(axis)):
        held.append(shift(held[-1], axis))
    return held


def after(value, *others):
    return lax.optimization_barrier((value,) + others)[0]


def place_kernel(count, own_rows, parts, where_ref, *refs):
    blocks, wholes = (refs[:count], refs[count:])
    spot = 0
    for block in blocks:
        for k in range(block.shape[0] // own_rows):
            for whole, cuts in zip(wholes, parts):
                for n, (start, stop) in enumerate(cuts):
                    row = (where_ref[spot] * len(cuts) + n) * own_rows
                    whole[pl.ds(pl.multiple_of(row, own_rows), own_rows), :] = block[
                        k * own_rows : (k + 1) * own_rows, start:stop
                    ]
            spot += 1


def place(blocks, own_rows, parts):
    sizes = {axis: lax.axis_size(axis) for axis in AXES}
    index = {axis: lax.axis_index(axis) for axis in AXES}
    devices = 1
    for axis in AXES:
        devices *= sizes[axis]
    where = []
    for slot, lines, _ in blocks:
        for k in lines:
            at = 0
            for axis in AXES:
                back = k if axis == "zc" else slot.get(axis, 0)
                at = at * sizes[axis] + (index[axis] - back) % sizes[axis]
            where.append(at)
    arrays = [block for _, _, block in blocks]
    shapes = [(devices * own_rows * len(cuts), cuts[0][1] - cuts[0][0]) for cuts in parts]
    if own_rows % 8:
        whole = jnp.zeros((devices, own_rows, arrays[0].shape[1]), F32)
        spots = iter(where)
        for block in arrays:
            for k in range(block.shape[0] // own_rows):
                whole = lax.dynamic_update_slice_in_dim(
                    whole, block[None, k * own_rows : (k + 1) * own_rows], next(spots), 0
                )
        return [
            jnp.concatenate([whole[:, :, a:b] for a, b in cuts], axis=1).reshape(shape)
            for cuts, shape in zip(parts, shapes)
        ]
    return pl.pallas_call(
        functools.partial(place_kernel, len(blocks), own_rows, parts),
        in_specs=[pl.BlockSpec(memory_space=pltpu.SMEM)]
        + [pl.BlockSpec(memory_space=pltpu.VMEM)] * len(blocks),
        out_specs=[pl.BlockSpec(memory_space=pltpu.VMEM)] * len(parts),
        out_shape=[jax.ShapeDtypeStruct(shape, F32) for shape in shapes],
        compiler_params=pltpu.CompilerParams(vmem_limit_bytes=48 * 1024 * 1024),
        cost_estimate=FREE,
        name="place",
    )(jnp.stack(where).astype(jnp.int32), *arrays)


def tied(values, *others):
    return list(lax.optimization_barrier((tuple(values), tuple(others)))[0])


class Gather:
    def __init__(self, piece, share):
        self.piece, self.rows, self.share = (piece, piece.shape[0], share)

    def line(self, *tie):
        (piece,) = tied([self.piece], *tie)
        self.lines = list(range(lax.axis_size("zc")))
        self.block = jnp.concatenate(offsets(piece, "zc"), axis=0)

    def line_at_once(self, *tie):
        (piece,) = tied([self.piece], *tie)
        count, index = (lax.axis_size("zc"), lax.axis_index("zc"))
        whole = lax.all_to_all(jnp.broadcast_to(piece, (count,) + piece.shape), "zc", 0, 0)
        self.lines = [index - k for k in range(count)]
        self.block = whole.reshape(-1, piece.shape[1])

    def near(self, *tie):
        (block,) = tied([self.block], *tie)
        self.rings = {axis: ring(block, axis)[1:] for axis in ("p", "y")}
        return [b for r in self.rings.values() for b in r]

    def keep_near(self, *others):
        self.rings = {axis: tied(r, *others) for axis, r in self.rings.items()}

    def keep_far(self, *others):
        arrays = tied([b for _, _, b in self.corners], *others)
        self.corners = [(slot, lines, b) for (slot, lines, _), b in zip(self.corners, arrays)]

    def far(self, *tie):
        middle = int(len(self.lines) * self.share)
        cut = middle * self.rows
        sides = {"p": [b[:cut] for b in self.rings["p"]], "y": [b[cut:] for b in self.rings["y"]]}
        other = {"p": "y", "y": "p"}
        self.corners = []
        for axis, blocks in sides.items():
            lines = self.lines[:middle] if axis == "p" else self.lines[middle:]
            blocks = tied(blocks, *tie)
            for k, block in enumerate(blocks):
                for n, moved in enumerate(ring(block, other[axis])[1:]):
                    self.corners.append(({axis: k + 1, other[axis]: n + 1}, lines, moved))
        return [b for _, _, b in self.corners]

    def held_near(self):
        near = [
            ({axis: k + 1}, self.lines, b) for axis, r in self.rings.items() for k, b in enumerate(r)
        ]
        return [({}, self.lines, self.block)] + near

    def held(self):
        return self.held_near() + self.corners

    def across(self, blocks, *tie):
        arrays = tied([b for _, _, b in blocks], *tie)
        return [
            ({**slot, "core": 1}, lines, shift(b, "core"))
            for (slot, lines, _), b in zip(blocks, arrays)
        ]


def indexed(addends, at, dim):
    total = None
    for addend in addends:
        part = lax.dynamic_index_in_dim(addend, at, dim, keepdims=False)
        total = part if total is None else total + part
    return total


class Scatter:
    def __init__(self, send, keep):
        self.shape = [lax.axis_size(a) for a in ("y", "zc", "p")] + [-1, keep.shape[-1]]
        moved = shift(send, "core")
        self.came = [moved]
        both = [keep.reshape(self.shape), moved.reshape(self.shape)]
        middle = self.shape[1] // 2
        self.parts = [
            ([v[:, :middle] for v in both], ["y", "zc", "p"]),
            ([v[:, middle:] for v in both], ["y", "zc", "p"]),
        ]

    def stage(self, axes):
        self.came, self.sends, parts = ([], [], [])
        for (addends, left), axis in zip(self.parts, axes):
            count, index, dim = (lax.axis_size(axis), lax.axis_index(axis), left.index(axis))
            came = []
            for k in range(1, count):
                moving = indexed(addends, (index + k) % count, dim)
                self.sends.append(moving)
                came.append(shift(moving, axis, k))
            kept = [lax.dynamic_index_in_dim(v, index, dim, keepdims=False) for v in addends]
            parts.append((kept + came, [a for a in left if a != axis]))
            self.came += came
            self.fresh = len(came)
        self.parts = parts

    def keep(self, *others):
        parts = []
        for addends, left in self.parts:
            fresh = self.fresh if left != ["y", "zc", "p"] else 1
            parts.append((addends[:-fresh] + tied(addends[-fresh:], *others), left))
        self.parts = parts

    def last(self, *tie):
        count, index = (lax.axis_size("zc"), lax.axis_index("zc"))
        line = jnp.concatenate([functools.reduce(jnp.add, v) for v, _ in self.parts], axis=0)
        if tie:
            line = after(line, *tie)
        self.came = [
            shift(lax.dynamic_index_in_dim(line, (index + k) % count, 0, keepdims=False), "zc", k)
            for k in range(1, count)
        ]
        self.kept = lax.dynamic_index_in_dim(line, index, 0, keepdims=False)

    def last_at_once(self):
        line = jnp.concatenate([functools.reduce(jnp.add, v) for v, _ in self.parts], axis=0)
        self.sends = [line]
        line = lax.all_to_all(line, "zc", 0, 0)
        self.came, self.kept = ([line[k] for k in range(1, line.shape[0])], line[0])

    def result(self):
        return functools.reduce(jnp.add, self.came, self.kept)


def sum_everywhere(values):
    for axis in ("core", "p", "y", "zc"):
        count, index = (lax.axis_size(axis), lax.axis_index(axis))
        if count == 2:
            values = values + shift(values, axis)
        else:
            held = jnp.stack(offsets(values, axis))
            values = functools.reduce(
                jnp.add,
                [
                    lax.dynamic_index_in_dim(held, (index - k) % count, 0, keepdims=False)
                    for k in range(count)
                ],
            )
    return values


class Exchange:
    def __init__(self, block, mine):
        self.mine = mine
        self.keep = lax.dynamic_index_in_dim(block, mine, 0, keepdims=False)
        self.other = shift(lax.dynamic_index_in_dim(block, 1 - mine, 0, keepdims=False), "p")

    def result(self, join, *others):
        (other,) = tied([self.other], *others)
        first = self.mine == 0
        return join([jnp.where(first, self.keep, other), jnp.where(first, other, self.keep)], axis=0)


def before_span(block, mine):
    count = lax.axis_size("zc")
    routes = [[(2 * i + 1, 2 * i + 2 + k) for i in range(count - 1)] for k in (0, 1)]
    ends = [lax.ppermute(block[k, -EDGE:], ("zc", "p"), routes[k]) for k in (0, 1)]
    return jnp.where(mine == 0, ends[0], ends[1])


def halves(span):
    return span.reshape(2, -1, span.shape[-1])


class States:
    chunks = 1

    def __init__(self, decay, added, reverse):
        self.count, self.reverse, self.distance = (lax.axis_size("zc"), reverse, 1)
        rows = added.shape[0] // self.chunks
        decay = jnp.broadcast_to(decay, (8, added.shape[1]))
        self.decay = decay
        self.added = [added[k * rows : (k + 1) * rows] for k in range(self.chunks)]
        self.held = [None] * self.chunks
        self.span = None

    def send(self):
        w = self.distance
        pairs = [(i, i + w) for i in range(self.count - w)]
        route = [(b, a) if self.reverse else (a, b) for a, b in pairs]
        self.came, self.sends = ([], [])
        for k in range(self.chunks):
            block = self.added[k]
            if self.held[k] is not None:
                block = block + self.decay[0:1] * self.held[k]
            if k == 0 and 2 * w < self.count:
                span = self.decay if self.span is None else self.decay * self.span
                block = jnp.concatenate([block, span], axis=0)
            self.sends.append(block)
            self.came.append(lax.ppermute(block, "zc", route))

    def absorb(self, *others):
        w, rows = (self.distance, self.added[0].shape[0])
        came = tied(self.came, *others) if others else self.came
        for k in range(self.chunks):
            new = came[k][:rows]
            if self.held[k] is not None:
                new = self.held[k] + self.span[0:1] * new
            self.held[k] = new
        if 2 * w < self.count:
            span = came[0][rows:]
            self.span = span if self.span is None else self.span * span
        self.distance = 2 * w

    def go_on(self, *others):
        self.absorb(*others)
        while self.distance < self.count:
            self.send()
            if 2 * self.distance >= self.count:
                return
            self.absorb()

    def result(self, *others):
        if self.distance < self.count:
            self.absorb(*others)
        return jnp.concatenate(self.held, axis=0)


def nn(a, b, precision=HIGH):
    return jnp.dot(a, b, precision=precision, preferred_element_type=F32)


def nt(a, b, precision=HIGH):
    return lax.dot_general(
        a, b, (((1,), (1,)), ((), ())), precision=precision, preferred_element_type=F32
    )


def tn(a, b, precision=HIGH):
    return lax.dot_general(
        a, b, (((0,), (0,)), ((), ())), precision=precision, preferred_element_type=F32
    )


def bf16_dot(a, b):
    return jnp.dot(a, b, preferred_element_type=F32)


def split_heads(values):
    top = values.astype(BF16)
    rest = values - top.astype(F32)
    mid = rest.astype(BF16)
    low = (rest - mid.astype(F32)).astype(BF16)
    return jnp.concatenate([top, mid, low], axis=1)


def spread_heads(values, spreader):
    return bf16_dot(split_heads(values), spreader)


def sum_heads(values, gatherer):
    top = values.astype(BF16)
    low = (values - top.astype(F32)).astype(BF16)
    return jnp.dot(top, gatherer, preferred_element_type=F32) + jnp.dot(
        low, gatherer, preferred_element_type=F32
    )


def order_mask(shape, kind):
    row, column = (lax.broadcasted_iota(jnp.int32, shape, d) for d in (0, 1))
    return {"ge": row >= column, "gt": row > column, "le": row <= column, "lt": row < column}[kind]


def triangle(kind):
    return jnp.where(order_mask((CUT, CUT), kind), 1.0, 0.0).astype(F32)


def conv_chunk(window_ref, taps_ref, bias_ref, cols):
    total = bias_ref[:, cols] + taps_ref[0:1, cols] * window_ref[EDGE - 3 : EDGE - 3 + CUT, cols]
    for k in range(1, CONV):
        at = EDGE - 3 + k
        total = total + taps_ref[k : k + 1, cols] * window_ref[at : at + CUT, cols]
    return total


def prepare_kernel(
    proj_ref,
    edge_ref,
    taps_ref,
    bias_ref,
    dtb_ref,
    alog_ref,
    spreader_ref,
    act_ref,
    step_ref,
    slope_ref,
    logd_ref,
    local_ref,
    before_ref,
    total_ref,
    window,
    state,
    logs,
):
    q = pl.program_id(0)

    @pl.when(q == 0)
    def _():
        window[0:EDGE, :] = edge_ref[:, 0:MIXED]
        state[...] = jnp.zeros_like(state)
        logs[...] = jnp.zeros_like(logs)

    @pl.when(q > 0)
    def _():
        window[0:EDGE, :] = window[CUT : CUT + EDGE, :]

    window[EDGE : EDGE + CUT, :] = proj_ref[:, 0:MIXED]

    def conv(c, carry):
        cols = pl.ds(pl.multiple_of(c * STRIP, STRIP), STRIP)
        out = conv_chunk(window, taps_ref, bias_ref, cols)
        act_ref[:, cols] = out * jax.nn.sigmoid(out)
        return carry

    lax.fori_loop(0, MIXED // STRIP, conv, 0, unroll=3)
    raw = proj_ref[:, MIXED:RATED] + dtb_ref[...]
    step = jnp.maximum(raw, 0.0) + jnp.log1p(jnp.exp(-jnp.abs(raw)))
    logd = nn(triangle("ge"), -jnp.exp(alog_ref[...]) * step, EXACT)
    step_ref[...] = step
    slope_ref[...] = jax.nn.sigmoid(raw)
    logd_ref[...] = logd
    last = logd[CUT - 1 : CUT, :]
    tail = spread_heads(jnp.exp(last - logd) * step, spreader_ref[...])
    added = tn(act_ref[:, DI : DI + STATE], act_ref[:, 0:DI] * tail)
    decay = spread_heads(jnp.broadcast_to(jnp.exp(last), (8, HEADS)), spreader_ref[...])
    state[...] = state[...] * decay[0:1, :] + added
    local_ref[0] = state[...]
    before_ref[...] = jnp.exp(logs[...])
    logs[...] = logs[...] + jnp.broadcast_to(last, (8, HEADS))
    total_ref[...] = jnp.exp(logs[...])


def full(shape):
    return pl.BlockSpec(shape, lambda i: (0,) * len(shape))


def params():
    return pltpu.CompilerParams(
        dimension_semantics=("arbitrary",), vmem_limit_bytes=52 * 1024 * 1024
    )


def prepare(proj, taps, bias, dt_bias, a_log, spreader):
    rows = proj.shape[0] - EDGE
    cuts = rows // CUT
    return pl.pallas_call(
        prepare_kernel,
        grid=(cuts,),
        in_specs=[
            pl.BlockSpec((CUT, WIDE), lambda i: (i, 0)),
            pl.BlockSpec((EDGE, WIDE), lambda i: (rows // EDGE, 0)),
            full((CONV, MIXED)),
            full((1, MIXED)),
            full((1, HEADS)),
            full((1, HEADS)),
            full((3 * HEADS, DI)),
        ],
        out_specs=[
            pl.BlockSpec((CUT, MIXED), lambda i: (i, 0)),
            pl.BlockSpec((CUT, HEADS), lambda i: (i, 0)),
            pl.BlockSpec((CUT, HEADS), lambda i: (i, 0)),
            pl.BlockSpec((CUT, HEADS), lambda i: (i, 0)),
            pl.BlockSpec((1, STATE, DI), lambda i: (i, 0, 0)),
            pl.BlockSpec((8, HEADS), lambda i: (i, 0)),
            full((8, HEADS)),
        ],
        out_shape=[
            jax.ShapeDtypeStruct((rows, MIXED), F32),
            jax.ShapeDtypeStruct((rows, HEADS), F32),
            jax.ShapeDtypeStruct((rows, HEADS), F32),
            jax.ShapeDtypeStruct((rows, HEADS), F32),
            jax.ShapeDtypeStruct((cuts, STATE, DI), F32),
            jax.ShapeDtypeStruct((8 * cuts, HEADS), F32),
            jax.ShapeDtypeStruct((8, HEADS), F32),
        ],
        scratch_shapes=[
            pltpu.VMEM((CUT + EDGE, MIXED), F32),
            pltpu.VMEM((STATE, DI), F32),
            pltpu.VMEM((8, HEADS), F32),
        ],
        compiler_params=params(),
        cost_estimate=FREE,
        name="prepare",
    )(proj, proj, taps, bias, dt_bias, a_log, spreader)


def both_columns(pair, left):
    turned = pltpu.roll(pair, HDIM, 1)
    return (jnp.where(left, pair, turned), jnp.where(left, turned, pair))


def stacked_pair(pair, left):
    zero = jnp.zeros_like(pair)
    return jnp.concatenate([jnp.where(left, pair, zero), jnp.where(left, zero, pair)], axis=0)


UNROLL = 8


def intra_kernel(
    act_ref, step_ref, logd_ref, skip_ref, spreader_ref, out_ref, logx, weighted, log_rows, scores
):
    spreader = spreader_ref[...]
    logd = logd_ref[...]
    logx[...] = spread_heads(logd, spreader)
    log_rows[...] = logd.T
    heads_in = act_ref[:, 0:DI]
    weighted[...] = heads_in * spread_heads(step_ref[...], spreader)
    scores[...] = nt(act_ref[:, DI + STATE : MIXED], act_ref[:, DI : DI + STATE])

    def pair(j, carry):
        cols = pl.ds(pl.multiple_of(j * PAIR, PAIR), PAIR)
        left = lax.broadcasted_iota(jnp.int32, (CUT, PAIR), 1) < HDIM
        mask = order_mask((CUT, CUT), "ge")
        mixes = []
        for side, column in enumerate(both_columns(logx[:, cols], left)):
            row = log_rows[pl.ds(2 * j + side, 1), :]
            mixes.append(jnp.exp(jnp.where(mask, column - row, -1e30)) * scores[...])
        out_ref[:, cols] = skip_ref[:, cols] * act_ref[:, cols] + nn(
            jnp.concatenate(mixes, axis=1), stacked_pair(weighted[:, cols], left)
        )
        return carry

    lax.fori_loop(0, HEADS // 2, pair, 0, unroll=UNROLL)


def intra(act, step, logd, skip, spreader):
    rows = act.shape[0]

    def at(width):
        return pl.BlockSpec((CUT, width), lambda i: (i, 0))

    return pl.pallas_call(
        intra_kernel,
        grid=(rows // CUT,),
        in_specs=[at(MIXED), at(HEADS), at(HEADS), full((1, DI)), full((3 * HEADS, DI))],
        out_specs=at(DI),
        out_shape=jax.ShapeDtypeStruct((rows, DI), F32),
        scratch_shapes=[
            pltpu.VMEM((CUT, DI), F32),
            pltpu.VMEM((CUT, DI), F32),
            pltpu.VMEM((HEADS, CUT), F32),
            pltpu.VMEM((CUT, CUT), F32),
        ],
        compiler_params=params(),
        cost_estimate=FREE,
        name="intra",
    )(act, step, logd, skip, spreader)


def mixer_kernel(
    act_ref,
    logd_ref,
    inner_ref,
    gate_left_ref,
    gate_right_ref,
    dng_ref,
    local_ref,
    enter_ref,
    before_ref,
    ggain_ref,
    spreader_ref,
    ng_ref,
    dy_ref,
    dz_ref,
    gin_ref,
    ggrad_ref,
    skipg_ref,
    grown,
    out,
    gstate,
):
    i = pl.program_id(0)
    q = pl.num_programs(0) - 1 - i
    spreader = spreader_ref[...]

    @pl.when(i == 0)
    def _():
        gstate[...] = jnp.zeros_like(gstate)
        ggrad_ref[...] = jnp.zeros_like(ggrad_ref)
        skipg_ref[...] = jnp.zeros_like(skipg_ref)

    logd = logd_ref[...]
    grown[...] = spread_heads(jnp.exp(logd), spreader)
    before = spread_heads(before_ref[...], spreader)[0:1, :]
    entering = enter_ref[...] * before + jnp.where(q == 0, 0.0, local_ref[0])
    c_state = act_ref[:, DI + STATE : MIXED]
    out[...] = grown[...] * nn(c_state, entering) + inner_ref[...]

    def gate(k, carry):
        rows = pl.ds(pl.multiple_of(k * 8, 8), 8)
        ssd = out[rows, :]
        gate_in = jnp.concatenate([gate_left_ref[rows, :], gate_right_ref[rows, :]], axis=1)
        sg = jax.nn.sigmoid(gate_in)
        silu = gate_in * sg
        gated = ssd * silu
        scale = lax.rsqrt(jnp.mean(gated * gated, axis=1, keepdims=True) + epsilon)
        unit = gated * scale
        ng_ref[rows, :] = unit * ggain_ref[...]
        dng = dng_ref[rows, :]
        e = dng * ggain_ref[...]
        ggrad_ref[...] += dng * unit
        dgated = scale * (e - unit * jnp.mean(e * unit, axis=1, keepdims=True))
        dy = dgated * silu
        dy_ref[rows, :] = dy
        dz_ref[rows, :] = dgated * ssd * (sg * (1.0 + gate_in * (1.0 - sg)))
        skipg_ref[...] += dy * act_ref[rows, 0:DI]
        return carry

    lax.fori_loop(0, CUT // 8, gate, 0, unroll=GATE_UNROLL)
    gstate[...] = gstate[...] * grown[CUT - 1 : CUT, :] + tn(c_state, grown[...] * dy_ref[...])
    gin_ref[0] = gstate[...]


GATE_UNROLL = 4


def mixer(act, logd, inner, gates, dng, local, entering, before, ggain, spreader):
    rows = act.shape[0]
    cuts = rows // CUT

    def back(width):
        return pl.BlockSpec((CUT, width), lambda i: (cuts - 1 - i, 0))

    wide = jax.ShapeDtypeStruct((rows, DI), F32)
    return pl.pallas_call(
        mixer_kernel,
        grid=(cuts,),
        in_specs=[
            back(MIXED),
            back(HEADS),
            back(DI),
            back(DI // 2),
            back(DI // 2),
            back(DI),
            pl.BlockSpec((1, STATE, DI), lambda i: (jnp.maximum(cuts - 2 - i, 0), 0, 0)),
            full((STATE, DI)),
            pl.BlockSpec((8, HEADS), lambda i: (cuts - 1 - i, 0)),
            full((1, DI)),
            full((3 * HEADS, DI)),
        ],
        out_specs=[
            back(DI),
            back(DI),
            back(DI),
            pl.BlockSpec((1, STATE, DI), lambda i: (cuts - 1 - i, 0, 0)),
            full((8, DI)),
            full((8, DI)),
        ],
        out_shape=[
            wide,
            wide,
            wide,
            jax.ShapeDtypeStruct((cuts, STATE, DI), F32),
            jax.ShapeDtypeStruct((8, DI), F32),
            jax.ShapeDtypeStruct((8, DI), F32),
        ],
        scratch_shapes=[
            pltpu.VMEM((CUT, DI), F32),
            pltpu.VMEM((CUT, DI), F32),
            pltpu.VMEM((STATE, DI), F32),
        ],
        compiler_params=params(),
        cost_estimate=FREE,
        name="mixer",
    )(act, logd, inner, *gates, dng, local, entering, before, ggain, spreader)


def back_intra_kernel(
    act_ref,
    step_ref,
    logd_ref,
    dy_ref,
    spreader_ref,
    dweighted_ref,
    dstates_ref,
    moved_ref,
    logx,
    weighted,
    log_rows,
    sum_rows,
    scores,
    dscores,
    sum_columns,
):
    spreader = spreader_ref[...]
    logd = logd_ref[...]
    logx[...] = spread_heads(logd, spreader)
    log_rows[...] = logd.T
    weighted[...] = act_ref[:, 0:DI] * spread_heads(step_ref[...], spreader)
    b_state = act_ref[:, DI : DI + STATE]
    c_state = act_ref[:, DI + STATE : MIXED]
    scores[...] = nt(b_state, c_state)
    dscores[...] = jnp.zeros_like(dscores)
    sum_columns[...] = jnp.zeros_like(sum_columns)

    def pair(j, carry):
        cols = pl.ds(pl.multiple_of(j * PAIR, PAIR), PAIR)
        left = lax.broadcasted_iota(jnp.int32, (CUT, PAIR), 1) < HDIM
        mask = order_mask((CUT, CUT), "le")
        strict = order_mask((CUT, CUT), "lt")
        dy = dy_ref[:, cols]
        dmix = nt(stacked_pair(weighted[:, cols], left), dy)
        mixes = []
        lane = lax.broadcasted_iota(jnp.int32, (CUT, CUT), 1)
        for side, column in enumerate(both_columns(logx[:, cols], left)):
            row = log_rows[pl.ds(2 * j + side, 1), :]
            weights = jnp.exp(jnp.where(mask, row - column, -1e30))
            mixes.append(weights * scores[...])
            part = dmix[side * CUT : (side + 1) * CUT, :] * weights
            dscores[...] += part
            moved = jnp.where(strict, part * scores[...], 0.0)
            sum_rows[pl.ds(2 * j + side, 1), :] = jnp.sum(moved, axis=0, keepdims=True)
            sum_columns[...] += jnp.where(
                lane == 2 * j + side, jnp.sum(moved, axis=1, keepdims=True), 0.0
            )
        dweighted_ref[:, cols] = nn(jnp.concatenate(mixes, axis=1), stacked_pair(dy, left))
        return carry

    lax.fori_loop(0, HEADS // 2, pair, 0, unroll=BACK_UNROLL)
    dstates_ref[:, 0:STATE] = nn(dscores[...], c_state)
    dstates_ref[:, STATE : 2 * STATE] = tn(dscores[...], b_state)
    moved_ref[...] = sum_rows[...].T - sum_columns[:, 0:HEADS]


BACK_UNROLL = 4


def back_intra(act, step, logd, dy, spreader):
    rows = act.shape[0]

    def at(width):
        return pl.BlockSpec((CUT, width), lambda i: (i, 0))

    return pl.pallas_call(
        back_intra_kernel,
        grid=(rows // CUT,),
        in_specs=[at(MIXED), at(HEADS), at(HEADS), at(DI), full((3 * HEADS, DI))],
        out_specs=[at(DI), at(2 * STATE), at(HEADS)],
        out_shape=[
            jax.ShapeDtypeStruct((rows, DI), F32),
            jax.ShapeDtypeStruct((rows, 2 * STATE), F32),
            jax.ShapeDtypeStruct((rows, HEADS), F32),
        ],
        scratch_shapes=[
            pltpu.VMEM((CUT, DI), F32),
            pltpu.VMEM((CUT, DI), F32),
            pltpu.VMEM((HEADS, CUT), F32),
            pltpu.VMEM((HEADS, CUT), F32),
            pltpu.VMEM((CUT, CUT), F32),
            pltpu.VMEM((CUT, CUT), F32),
            pltpu.VMEM((CUT, CUT), F32),
        ],
        compiler_params=params(),
        cost_estimate=FREE,
        name="back_intra",
    )(act, step, logd, dy, spreader)


def back_kernel(
    act_ref,
    step_ref,
    slope_ref,
    logd_ref,
    dy_ref,
    dweighted_ref,
    dstates_ref,
    moved_ref,
    local_ref,
    enter_ref,
    before_ref,
    gin_ref,
    gout_ref,
    proj_ref,
    halo_ref,
    taps_ref,
    bias_ref,
    alog_ref,
    skip_ref,
    spreader_ref,
    gatherer_ref,
    dproj_ref,
    dtaps_ref,
    dbias_ref,
    dlog_ref,
    ddtb_ref,
    dact,
    window,
    dwindow,
    after,
):
    i = pl.program_id(0)
    cuts = pl.num_programs(0)
    q = cuts - 1 - i

    @pl.when(i == 0)
    def _():
        after[...] = jnp.zeros_like(after)
        dwindow[...] = jnp.zeros_like(dwindow)
        for ref in (dtaps_ref, dbias_ref, dlog_ref, ddtb_ref):
            ref[...] = jnp.zeros_like(ref)

    @pl.when(i > 0)
    def _():
        dwindow[CUT : CUT + EDGE, :] = dwindow[0:EDGE, :]

    logd = logd_ref[...]
    step = step_ref[...]
    last = logd[CUT - 1 : CUT, :]
    b_state = act_ref[:, DI : DI + STATE]
    c_state = act_ref[:, DI + STATE : MIXED]
    grow_parts = split_heads(jnp.exp(logd))
    tail_parts = split_heads(jnp.exp(last - logd))
    step_parts = split_heads(step)
    before_parts = split_heads(before_ref[...])
    later_parts = split_heads(jnp.exp(after[...]))
    after[...] = after[...] + jnp.broadcast_to(last, (8, HEADS))
    db = dstates_ref[:, 0:STATE]
    dc = dstates_ref[:, STATE : 2 * STATE]
    moved = moved_ref[...]
    lost = jnp.zeros((CUT, HEADS), F32)
    dstep = jnp.zeros((CUT, HEADS), F32)
    kept = jnp.zeros((8, HEADS), F32)
    for c in range(DI // BLOCK):
        cols = slice(c * BLOCK, (c + 1) * BLOCK)
        spreader = spreader_ref[:, cols]
        gatherer = gatherer_ref[cols, :]
        entering = enter_ref[:, cols] * bf16_dot(before_parts, spreader)[0:1, :]
        entering = entering + jnp.where(q == 0, 0.0, local_ref[0, :, cols])
        gout = gout_ref[:, cols] * bf16_dot(later_parts, spreader)[0:1, :]
        gout = gout + jnp.where(i == 0, 0.0, gin_ref[0, :, cols])
        tail = bf16_dot(tail_parts, spreader)
        steps = bf16_dot(step_parts, spreader)
        heads_in = act_ref[:, cols]
        dy = dy_ref[:, cols]
        from_state = tail * nn(b_state, gout)
        stepped = heads_in * steps
        dweighted = dweighted_ref[:, cols] + from_state
        carried = bf16_dot(grow_parts, spreader) * dy
        db = db + nt(tail * stepped, gout)
        dc = dc + nt(carried, entering)
        dact[:, cols] = dweighted * steps + skip_ref[:, cols] * dy
        moved = moved + sum_heads(carried * nn(c_state, entering), gatherer)
        lost = lost + sum_heads(stepped * from_state, gatherer)
        dstep = dstep + sum_heads(heads_in * dweighted, gatherer)
        kept = kept + sum_heads(
            jnp.broadcast_to(jnp.sum(gout * entering, axis=0, keepdims=True), (8, BLOCK)), gatherer
        )
    dact[:, DI : DI + STATE] = db
    dact[:, DI + STATE : MIXED] = dc
    dlog = (
        nn(triangle("le"), moved, EXACT)
        + nn(triangle("gt"), lost, EXACT)
        + jnp.exp(last) * kept[0:1, :]
    )
    rate = -jnp.exp(alog_ref[...])
    dlog_ref[...] += jnp.broadcast_to(
        jnp.sum(dlog * step, axis=0, keepdims=True) * rate, (8, HEADS)
    )
    draw = (dstep + dlog * rate) * slope_ref[...]
    ddtb_ref[...] += jnp.broadcast_to(jnp.sum(draw, axis=0, keepdims=True), (8, HEADS))
    here = pl.ds(pl.multiple_of(q * CUT, CUT), CUT)
    dproj_ref[here, MIXED:WIDE] = jnp.concatenate([draw, jnp.zeros((CUT, SPARE), F32)], axis=1)
    window[0:EDGE, :] = halo_ref[:, 0:MIXED]
    window[EDGE : EDGE + CUT, :] = proj_ref[:, 0:MIXED]

    def conv(c, carry):
        cols = pl.ds(pl.multiple_of(c * STRIP, STRIP), STRIP)
        out = conv_chunk(window, taps_ref, bias_ref, cols)
        sg = jax.nn.sigmoid(out)
        dout = dact[:, cols] * (sg * (1.0 + out * (1.0 - sg)))
        dwindow[0:CUT, cols] = dout
        dbias_ref[:, cols] += jnp.sum(dout.reshape(CUT // 8, 8, STRIP), axis=0)
        for k in range(CONV):
            at = EDGE - 3 + k
            dtaps_ref[8 * k : 8 * k + 8, cols] += jnp.sum(
                (dout * window[at : at + CUT, cols]).reshape(CUT // 8, 8, STRIP), axis=0
            )
        din = taps_ref[CONV - 1 : CONV, cols] * dout
        for k in range(CONV - 1):
            din = din + taps_ref[k : k + 1, cols] * dwindow[3 - k : 3 - k + CUT, cols]
        dproj_ref[here, cols] = din
        return carry

    lax.fori_loop(0, MIXED // STRIP, conv, 0, unroll=3)

    @pl.when(q == 0)
    def _():
        rows = cuts * CUT
        window[0:EDGE, :] = jnp.zeros((EDGE, MIXED), F32)
        window[EDGE : 2 * EDGE, :] = dwindow[0:EDGE, :]
        din = taps_ref[CONV - 1 : CONV, :] * window[0:EDGE, :]
        for k in range(CONV - 1):
            din = din + taps_ref[k : k + 1, :] * window[3 - k : 3 - k + EDGE, :]
        dproj_ref[rows : rows + EDGE, 0:MIXED] = din
        dproj_ref[rows : rows + EDGE, MIXED:WIDE] = jnp.zeros((EDGE, WIDE - MIXED), F32)


def back(
    act, step, slope, logd, dy, dweighted, dstates, moved, local, entering, before, gin, gout, proj, taps, bias, a_log,
    skip, spreader, gatherer,
):
    rows = act.shape[0]
    cuts = rows // CUT

    def at(size):
        return pl.BlockSpec((CUT, size), lambda i: (cuts - 1 - i, 0))

    def halo(i):
        q = cuts - 1 - i
        return (jnp.where(q == 0, rows // EDGE, q * (CUT // EDGE) - 1), 0)

    return pl.pallas_call(
        back_kernel,
        grid=(cuts,),
        in_specs=[
            at(MIXED),
            at(HEADS),
            at(HEADS),
            at(HEADS),
            at(DI),
            at(DI),
            at(2 * STATE),
            at(HEADS),
            pl.BlockSpec((1, STATE, DI), lambda i: (jnp.maximum(cuts - 2 - i, 0), 0, 0)),
            full((STATE, DI)),
            pl.BlockSpec((8, HEADS), lambda i: (cuts - 1 - i, 0)),
            pl.BlockSpec((1, STATE, DI), lambda i: (jnp.minimum(cuts - i, cuts - 1), 0, 0)),
            full((STATE, DI)),
            at(WIDE),
            pl.BlockSpec((EDGE, WIDE), halo),
            full((CONV, MIXED)),
            full((1, MIXED)),
            full((1, HEADS)),
            full((1, DI)),
            full((3 * HEADS, DI)),
            full((DI, HEADS)),
        ],
        out_specs=[
            full((rows + EDGE, WIDE)),
            full((8 * CONV, MIXED)),
            full((8, MIXED)),
            full((8, HEADS)),
            full((8, HEADS)),
        ],
        out_shape=[
            jax.ShapeDtypeStruct((rows + EDGE, WIDE), F32),
            jax.ShapeDtypeStruct((8 * CONV, MIXED), F32),
            jax.ShapeDtypeStruct((8, MIXED), F32),
            jax.ShapeDtypeStruct((8, HEADS), F32),
            jax.ShapeDtypeStruct((8, HEADS), F32),
        ],
        scratch_shapes=[
            pltpu.VMEM((CUT, MIXED), F32),
            pltpu.VMEM((CUT + EDGE, MIXED), F32),
            pltpu.VMEM((CUT + EDGE, MIXED), F32),
            pltpu.VMEM((8, HEADS), F32),
        ],
        compiler_params=params(),
        cost_estimate=FREE,
        name="back",
    )(
        act, step, slope, logd, dy, dweighted, dstates, moved, local, entering, before, gin, gout, proj, proj,
        taps, bias, a_log, skip, spreader, gatherer,
    )


COLUMNS = 512


def right_kernel(x_ref, w_ref, added_ref, scale_ref, out_ref):
    out_ref[...] = (nn(x_ref[...], w_ref[...]) + added_ref[...]) * scale_ref[...]


def right(x, w, added, scale):
    (rows, depth), cols = (x.shape, w.shape[1])
    tile = pl.BlockSpec((rows, COLUMNS), lambda j: (0, j))
    return pl.pallas_call(
        right_kernel,
        grid=(cols // COLUMNS,),
        in_specs=[
            full((rows, depth)), pl.BlockSpec((depth, COLUMNS), lambda j: (0, j)), tile, full((rows, 1)),
        ],
        out_specs=tile,
        out_shape=jax.ShapeDtypeStruct((rows, cols), F32),
        compiler_params=params(),
        cost_estimate=FREE,
        name="right",
    )(x, w, added, scale)


def right_back_kernel(x_ref, *refs):
    *w_refs, out_ref = refs
    total, at = (None, 0)
    for w_ref in w_refs:
        part = nt(x_ref[:, at : at + w_ref.shape[1]], w_ref[...])
        total, at = (part if total is None else total + part, at + w_ref.shape[1])
    out_ref[...] = total


def right_back(x, weights):
    rows, cols = (x.shape[0], weights[0].shape[0])
    return pl.pallas_call(
        right_back_kernel,
        grid=(cols // COLUMNS,),
        in_specs=[full(x.shape)]
        + [pl.BlockSpec((COLUMNS, w.shape[1]), lambda j: (j, 0)) for w in weights],
        out_specs=pl.BlockSpec((rows, COLUMNS), lambda j: (0, j)),
        out_shape=jax.ShapeDtypeStruct((rows, cols), F32),
        compiler_params=params(),
        cost_estimate=FREE,
        name="right_back",
    )(x, *weights)


def head_spreader():
    head = lax.broadcasted_iota(jnp.int32, (3 * HEADS, DI), 0) % HEADS
    return (head == lax.broadcasted_iota(jnp.int32, (3 * HEADS, DI), 1) // HDIM).astype(BF16)


def head_gatherer():
    channel = lax.broadcasted_iota(jnp.int32, (DI, HEADS), 0) // HDIM
    return (channel == lax.broadcasted_iota(jnp.int32, (DI, HEADS), 1)).astype(BF16)


def per_device(
    hidden_in,
    lengths,
    norm_gain,
    in_weight,
    conv_weight,
    conv_bias,
    dt_bias,
    a_log,
    skip_gain,
    gated_gain,
    out_weight,
    cotangent,
):
    width = hidden_in.shape[-1]
    devices = 1
    for axis in AXES:
        devices *= lax.axis_size(axis)
    mine, spot, count = (lax.axis_index("p"), lax.axis_index("zc"), lax.axis_size("zc"))
    own_rows = width // devices

    in_piece = in_weight.reshape(own_rows, -1)
    small = jnp.concatenate([conv_weight, conv_bias])
    padded = jnp.pad(small, (0, SPARE * own_rows - small.shape[0])).reshape(own_rows, SPARE)
    conv = Gather(jnp.concatenate([in_piece[:, DI:], padded], axis=1), 0.5)
    edge = before_span(hidden_in, mine)
    conv.line()
    trade = Exchange(hidden_in, mine)
    hidden = trade.result(jnp.concatenate)
    rows = hidden.shape[0]
    out_piece = out_weight.reshape(-1, width)
    rest = jnp.concatenate([in_piece[:, :width], in_piece[:, width:DI], out_piece], axis=0)
    rest = lax.all_gather(rest, AXES, axis=0).reshape(devices, -1, width)
    w_gates = [
        rest[:, k * own_rows : (k + 1) * own_rows].reshape(width, width) for k in range(DI // width)
    ]
    w_out = rest[:, DI // width * own_rows :].reshape(DI, width)
    near = conv.near(trade.other)
    conv_over = conv.across(conv.held_near()[:1], conv.block)
    far = conv.far()
    conv_over += conv.across(conv.held_near()[1:])
    conv_over += conv.across(conv.corners)
    (w_conv,) = place(conv.held() + conv_over, conv.rows, [[(0, WIDE)]])
    other = Exchange(tied([cotangent], *far)[0], mine)
    smalls = w_conv[:, RATED:].reshape(devices, own_rows * SPARE)
    taps = smalls[:, : conv_weight.shape[0]].reshape(CONV, MIXED)
    bias = smalls[:, conv_weight.shape[0] : small.shape[0]].reshape(1, MIXED)

    extended = jnp.concatenate([hidden, edge], axis=0)
    scale = lax.rsqrt(jnp.mean(extended * extended, axis=1, keepdims=True) + epsilon)
    unit = extended * scale
    normed = unit * norm_gain
    inner = normed[:rows]
    spreader, gatherer = (head_spreader(), head_gatherer())
    dt_row, alog_row = (dt_bias.reshape(1, -1), a_log.reshape(1, -1))
    skip_row = jnp.repeat(skip_gain, HDIM).reshape(1, DI)
    positions = spot * rows + lax.iota(jnp.int32, rows)
    length = lax.dynamic_index_in_dim(lengths, mine, 0, keepdims=False)
    valid = (positions < length).astype(F32)[:, None]
    proj = nn(normed, w_conv)
    act, step, slope, logd, local, before, total = prepare(
        proj, taps, bias, dt_row, alog_row, spreader
    )
    total_row = jnp.repeat(total[0], HDIM).reshape(1, DI)
    states = States(total_row, local[-1], False)
    states.send()
    within = intra(tied([act], *states.sends)[0], step, logd, skip_row, spreader)
    (turn,) = tied([inner], within)
    gates = [nn(turn, w) for w in w_gates]
    states.go_on(*gates)
    grad_out = other.result(jnp.concatenate, within) * valid
    dng = nt(tied([grad_out], *gates, *states.sends)[0], w_out)
    entering = states.result(dng)
    ng, dy, dz, gin, ggrad, skipg = mixer(
        act, logd, within, gates, dng, local, entering, before, gated_gain.reshape(1, DI), spreader
    )
    ng_keep, ng_send = core_columns(ng)
    in_keep, in_send = core_columns(normed)
    grads = States(total_row, gin[0], True)
    grads.send()
    (turn,) = tied([ng_send], *grads.sends)
    first = tn(turn, grad_out)
    (turn,) = tied([grad_out], first)
    second = tn(ng_keep, turn)
    grad_wout = Scatter(first, second)
    branch = right(tied([ng], second)[0], w_out, hidden, valid)
    grads.go_on(branch)
    grad_wout.keep(branch)
    grad_wout.stage(("p", "y"))
    (turn,) = tied([dz], branch, *grads.sends, *grad_wout.sends)
    first = tn(in_send[:rows], turn)
    (turn,) = tied([turn], first)
    second = tn(in_keep[:rows], turn)
    grad_wgate = Scatter(first, second)
    back_parts = back_intra(tied([act], second)[0], step, logd, dy, spreader)
    grad_wout.keep(back_parts[1])
    grad_wgate.keep(back_parts[1])
    grad_wout.stage(("y", "p"))
    grad_wgate.stage(("p", "y"))
    (turn,) = tied([dz], back_parts[1], *grad_wout.sends, *grad_wgate.sends)
    dgate_normed = right_back(turn, w_gates)
    grad_wout.keep(dgate_normed)
    grad_wout.last_at_once()
    gout = grads.result(dgate_normed)
    dproj, dtaps, dbias, dlog, ddtb = back(
        tied([act], dgate_normed, *grad_wout.sends)[0], step, slope, logd, dy, *back_parts, local,
        entering, before, gin, gout, proj, taps, bias, alog_row, skip_row, spreader, gatherer,
    )
    dtaps = jnp.sum(dtaps.reshape(CONV, 8, MIXED), axis=1).reshape(devices, -1)
    dbias = jnp.sum(dbias, axis=0).reshape(devices, -1)
    dsmall = jnp.concatenate([dtaps, dbias], axis=1)
    dsmall = jnp.pad(dsmall, ((0, 0), (0, SPARE * own_rows - small.shape[0])))
    dsmall = jnp.pad(dsmall.reshape(width, SPARE), ((0, 0), (RATED, 0)))
    small_keep, small_send = (core_rows(dsmall, k) for k in (0, 1))
    grad_wgate.keep(ddtb)
    grad_wgate.stage(("y", "p"))
    (turn,) = tied([dproj], *grad_wgate.sends)
    first = tn(in_send, turn) + small_send
    (turn,) = tied([dproj], first)
    second = tn(in_keep, turn) + small_keep
    grad_wconv = Scatter(first, second)
    grad_wconv.keep(second)
    grad_wconv.stage(("p", "y"))
    traded = Exchange(halves(tied([branch], ddtb)[0]), mine)
    dnormed = nt(tied([dproj], second, *grad_wconv.sends)[0], w_conv)
    grad_wgate.keep(dnormed)
    grad_wgate.last_at_once()
    near = grad_wconv.came
    (dnormed,) = tied([dnormed], *grad_wgate.sends)
    output = traded.result(jnp.stack, dnormed)
    returned = lax.ppermute(dnormed[rows:], "zc", [(i + 1, i) for i in range(count - 1)])
    dnormed = dnormed[:rows] + dgate_normed
    dnormed = dnormed + jnp.pad(returned, ((rows - EDGE, 0), (0, 0)))
    unit = unit[:rows]
    dunit = dnormed * norm_gain
    dhidden = scale[:rows] * (dunit - unit * jnp.mean(dunit * unit, axis=1, keepdims=True))
    grad_input = Exchange(halves(tied([grad_out + dhidden], *near)[0]), mine).result(jnp.stack)
    grad_skip = jnp.sum(jnp.sum(skipg, axis=0).reshape(HEADS, HDIM), axis=1)
    sums = jnp.concatenate(
        [
            jnp.sum(dnormed * unit, axis=0),
            jnp.sum(ggrad, axis=0),
            ddtb[0],
            dlog[0],
            grad_skip,
        ]
    )
    (sums,) = tied([jnp.pad(sums, (0, -sums.shape[0] % 128)).reshape(-1, 128)], *near)
    sums = sum_everywhere(sums).reshape(-1)
    grad_wconv.stage(("y", "p"))
    grad_wconv.last()
    parts = []
    for size in (width, DI, HEADS, HEADS, HEADS):
        parts.append(sums[:size])
        sums = sums[size:]
    conv_grad = grad_wconv.result()
    small_grad = conv_grad[:, RATED:].reshape(-1)
    return (
        output,
        grad_input,
        parts[0],
        jnp.concatenate([grad_wgate.result(), conv_grad[:, :RATED]], axis=1).reshape(-1),
        small_grad[: conv_weight.shape[0]],
        small_grad[conv_weight.shape[0] : small.shape[0]],
        parts[2],
        parts[3],
        parts[4],
        parts[1],
        grad_wout.result().reshape(-1),
    )


def core_columns(values):
    size = values.shape[1] // (2 * lax.axis_size("y"))
    core = lax.axis_index("core")
    return [
        jnp.concatenate(
            [
                lax.dynamic_slice_in_dim(values, (2 * y + (core + k) % 2) * size, size, 1)
                for y in range(lax.axis_size("y"))
            ],
            axis=1,
        )
        for k in (0, 1)
    ]


def core_rows(values, k):
    size = values.shape[0] // (2 * lax.axis_size("y"))
    core = lax.axis_index("core")
    return jnp.concatenate(
        [
            lax.dynamic_slice_in_dim(values, (2 * y + (core + k) % 2) * size, size, 0)
            for y in range(lax.axis_size("y"))
        ],
        axis=0,
    )


def solution(mesh):
    dp, seq = (mesh.shape["dp"], mesh.shape["seq"])
    finer = Mesh(mesh.devices.reshape(dp // 2, 2, seq // 2, 2), AXES)
    over_dp, over_seq = (("y", "core"), ("zc", "p"))
    tokens = P(over_dp, over_seq, None)
    in_specs = (
        tokens, P(over_dp), P(), P(AXES), P(AXES), P(AXES), P(), P(), P(), P(), P(AXES), tokens,
    )
    out_specs = (
        tokens, tokens, P(), P(AXES), P(AXES), P(AXES), P(), P(), P(), P(), P(AXES),
    )
    return jax.shard_map(
        per_device, mesh=finer, in_specs=in_specs, out_specs=out_specs, check_vma=False
    )
```

```python
import functools

import jax
import jax.numpy as jnp
from jax import lax
from jax.experimental import pallas as pl
from jax.experimental.pallas import tpu as pltpu
from jax.sharding import Mesh
from jax.sharding import PartitionSpec as P

DI = 2048
HEADS = 32
HDIM = 64
STATE = 128
CONV = 4
MIXED = DI + 2 * STATE
RATED = MIXED + HEADS
CUT = 128
EDGE = 8
PAIR = 2 * HDIM
SPARE = 128 - HEADS
WIDE = RATED + SPARE
STRIP = 128
BLOCK = 1024
F32 = jnp.float32
BF16 = jnp.bfloat16
HIGH = lax.Precision.HIGH
EXACT = lax.Precision.HIGHEST
epsilon = 1e-05
FREE = pl.CostEstimate(flops=0, bytes_accessed=0, transcendentals=0)


def shift(block, axis, step=1):
    count = lax.axis_size(axis)
    return lax.ppermute(block, axis, [(i, (i + step) % count) for i in range(count)])


AXES = ("y", "core", "zc", "p")


def offsets(block, axis):
    count = lax.axis_size(axis)
    return [block] + [shift(block, axis, k) for k in range(1, count)]


def ring(block, axis):
    held = [block]
    for _ in range(1, lax.axis_size(axis)):
        held.append(shift(held[-1], axis))
    return held


def after(value, *others):
    return lax.optimization_barrier((value,) + others)[0]


def place_kernel(count, own_rows, parts, where_ref, *refs):
    blocks, wholes = (refs[:count], refs[count:])
    spot = 0
    for block in blocks:
        for k in range(block.shape[0] // own_rows):
            for whole, cuts in zip(wholes, parts):
                for n, (start, stop) in enumerate(cuts):
                    row = (where_ref[spot] * len(cuts) + n) * own_rows
                    whole[pl.ds(pl.multiple_of(row, own_rows), own_rows), :] = block[
                        k * own_rows : (k + 1) * own_rows, start:stop
                    ]
            spot += 1


def place(blocks, own_rows, parts):
    sizes = {axis: lax.axis_size(axis) for axis in AXES}
    index = {axis: lax.axis_index(axis) for axis in AXES}
    devices = 1
    for axis in AXES:
        devices *= sizes[axis]
    where = []
    for slot, lines, _ in blocks:
        for k in lines:
            at = 0
            for axis in AXES:
                back = k if axis == "zc" else slot.get(axis, 0)
                at = at * sizes[axis] + (index[axis] - back) % sizes[axis]
            where.append(at)
    arrays = [block for _, _, block in blocks]
    shapes = [(devices * own_rows * len(cuts), cuts[0][1] - cuts[0][0]) for cuts in parts]
    if own_rows % 8:
        whole = jnp.zeros((devices, own_rows, arrays[0].shape[1]), F32)
        spots = iter(where)
        for block in arrays:
            for k in range(block.shape[0] // own_rows):
                whole = lax.dynamic_update_slice_in_dim(
                    whole, block[None, k * own_rows : (k + 1) * own_rows], next(spots), 0
                )
        return [
            jnp.concatenate([whole[:, :, a:b] for a, b in cuts], axis=1).reshape(shape)
            for cuts, shape in zip(parts, shapes)
        ]
    return pl.pallas_call(
        functools.partial(place_kernel, len(blocks), own_rows, parts),
        in_specs=[pl.BlockSpec(memory_space=pltpu.SMEM)]
        + [pl.BlockSpec(memory_space=pltpu.VMEM)] * len(blocks),
        out_specs=[pl.BlockSpec(memory_space=pltpu.VMEM)] * len(parts),
        out_shape=[jax.ShapeDtypeStruct(shape, F32) for shape in shapes],
        compiler_params=pltpu.CompilerParams(vmem_limit_bytes=48 * 1024 * 1024),
        cost_estimate=FREE,
        name="place",
    )(jnp.stack(where).astype(jnp.int32), *arrays)


def tied(values, *others):
    return list(lax.optimization_barrier((tuple(values), tuple(others)))[0])


class Gather:
    def __init__(self, piece, share):
        self.piece, self.rows, self.share = (piece, piece.shape[0], share)

    def line(self, *tie):
        (piece,) = tied([self.piece], *tie)
        self.lines = list(range(lax.axis_size("zc")))
        self.block = jnp.concatenate(offsets(piece, "zc"), axis=0)

    def line_at_once(self, *tie):
        (piece,) = tied([self.piece], *tie)
        count, index = (lax.axis_size("zc"), lax.axis_index("zc"))
        whole = lax.all_to_all(jnp.broadcast_to(piece, (count,) + piece.shape), "zc", 0, 0)
        self.lines = [index - k for k in range(count)]
        self.block = whole.reshape(-1, piece.shape[1])

    def near(self, *tie):
        (block,) = tied([self.block], *tie)
        self.rings = {axis: ring(block, axis)[1:] for axis in ("p", "y")}
        return [b for r in self.rings.values() for b in r]

    def keep_near(self, *others):
        self.rings = {axis: tied(r, *others) for axis, r in self.rings.items()}

    def keep_far(self, *others):
        arrays = tied([b for _, _, b in self.corners], *others)
        self.corners = [(slot, lines, b) for (slot, lines, _), b in zip(self.corners, arrays)]

    def far(self, *tie):
        middle = int(len(self.lines) * self.share)
        cut = middle * self.rows
        sides = {"p": [b[:cut] for b in self.rings["p"]], "y": [b[cut:] for b in self.rings["y"]]}
        other = {"p": "y", "y": "p"}
        self.corners = []
        for axis, blocks in sides.items():
            lines = self.lines[:middle] if axis == "p" else self.lines[middle:]
            blocks = tied(blocks, *tie)
            for k, block in enumerate(blocks):
                for n, moved in enumerate(ring(block, other[axis])[1:]):
                    self.corners.append(({axis: k + 1, other[axis]: n + 1}, lines, moved))
        return [b for _, _, b in self.corners]

    def held_near(self):
        near = [
            ({axis: k + 1}, self.lines, b) for axis, r in self.rings.items() for k, b in enumerate(r)
        ]
        return [({}, self.lines, self.block)] + near

    def held(self):
        return self.held_near() + self.corners

    def across(self, blocks, *tie):
        arrays = tied([b for _, _, b in blocks], *tie)
        return [
            ({**slot, "core": 1}, lines, shift(b, "core"))
            for (slot, lines, _), b in zip(blocks, arrays)
        ]


def indexed(addends, at, dim):
    total = None
    for addend in addends:
        part = lax.dynamic_index_in_dim(addend, at, dim, keepdims=False)
        total = part if total is None else total + part
    return total


class Scatter:
    def __init__(self, send, keep):
        self.shape = [lax.axis_size(a) for a in ("y", "zc", "p")] + [-1, keep.shape[-1]]
        moved = shift(send, "core")
        self.came = [moved]
        both = [keep.reshape(self.shape), moved.reshape(self.shape)]
        middle = self.shape[1] // 2
        self.parts = [
            ([v[:, :middle] for v in both], ["y", "zc", "p"]),
            ([v[:, middle:] for v in both], ["y", "zc", "p"]),
        ]

    def stage(self, axes):
        self.came, self.sends, parts = ([], [], [])
        for (addends, left), axis in zip(self.parts, axes):
            count, index, dim = (lax.axis_size(axis), lax.axis_index(axis), left.index(axis))
            came = []
            for k in range(1, count):
                moving = indexed(addends, (index + k) % count, dim)
                self.sends.append(moving)
                came.append(shift(moving, axis, k))
            kept = [lax.dynamic_index_in_dim(v, index, dim, keepdims=False) for v in addends]
            parts.append((kept + came, [a for a in left if a != axis]))
            self.came += came
            self.fresh = len(came)
        self.parts = parts

    def keep(self, *others):
        parts = []
        for addends, left in self.parts:
            fresh = self.fresh if left != ["y", "zc", "p"] else 1
            parts.append((addends[:-fresh] + tied(addends[-fresh:], *others), left))
        self.parts = parts

    def last(self, *tie):
        count, index = (lax.axis_size("zc"), lax.axis_index("zc"))
        line = jnp.concatenate([functools.reduce(jnp.add, v) for v, _ in self.parts], axis=0)
        if tie:
            line = after(line, *tie)
        self.came = [
            shift(lax.dynamic_index_in_dim(line, (index + k) % count, 0, keepdims=False), "zc", k)
            for k in range(1, count)
        ]
        self.kept = lax.dynamic_index_in_dim(line, index, 0, keepdims=False)

    def last_at_once(self):
        line = jnp.concatenate([functools.reduce(jnp.add, v) for v, _ in self.parts], axis=0)
        self.sends = [line]
        self.line = lax.all_to_all(line, "zc", 0, 0)

    def settle(self, *others):
        (line,) = tied([self.line], *others) if others else [self.line]
        self.came, self.kept = ([line[k] for k in range(1, line.shape[0])], line[0])

    def result(self):
        return functools.reduce(jnp.add, self.came, self.kept)


def sum_everywhere(values):
    for axis in ("core", "p", "y", "zc"):
        count, index = (lax.axis_size(axis), lax.axis_index(axis))
        if count == 2:
            values = values + shift(values, axis)
        else:
            held = jnp.stack(offsets(values, axis))
            values = functools.reduce(
                jnp.add,
                [
                    lax.dynamic_index_in_dim(held, (index - k) % count, 0, keepdims=False)
                    for k in range(count)
                ],
            )
    return values


class Exchange:
    def __init__(self, block, mine):
        self.mine = mine
        self.keep = lax.dynamic_index_in_dim(block, mine, 0, keepdims=False)
        self.other = shift(lax.dynamic_index_in_dim(block, 1 - mine, 0, keepdims=False), "p")

    def result(self, join, *others):
        (other,) = tied([self.other], *others)
        first = self.mine == 0
        return join([jnp.where(first, self.keep, other), jnp.where(first, other, self.keep)], axis=0)


def before_span(block, mine):
    count = lax.axis_size("zc")
    routes = [[(2 * i + 1, 2 * i + 2 + k) for i in range(count - 1)] for k in (0, 1)]
    ends = [lax.ppermute(block[k, -EDGE:], ("zc", "p"), routes[k]) for k in (0, 1)]
    return jnp.where(mine == 0, ends[0], ends[1])


def halves(span):
    return span.reshape(2, -1, span.shape[-1])


class States:
    chunks = 1

    def __init__(self, decay, added, reverse):
        self.count, self.reverse, self.distance = (lax.axis_size("zc"), reverse, 1)
        rows = added.shape[0] // self.chunks
        decay = jnp.broadcast_to(decay, (8, added.shape[1]))
        self.decay = decay
        self.added = [added[k * rows : (k + 1) * rows] for k in range(self.chunks)]
        self.held = [None] * self.chunks
        self.span = None

    def send(self):
        w = self.distance
        pairs = [(i, i + w) for i in range(self.count - w)]
        route = [(b, a) if self.reverse else (a, b) for a, b in pairs]
        self.came, self.sends = ([], [])
        for k in range(self.chunks):
            block = self.added[k]
            if self.held[k] is not None:
                block = block + self.decay[0:1] * self.held[k]
            if k == 0 and 2 * w < self.count:
                span = self.decay if self.span is None else self.decay * self.span
                block = jnp.concatenate([block, span], axis=0)
            self.sends.append(block)
            self.came.append(lax.ppermute(block, "zc", route))

    def absorb(self, *others):
        w, rows = (self.distance, self.added[0].shape[0])
        came = tied(self.came, *others) if others else self.came
        for k in range(self.chunks):
            new = came[k][:rows]
            if self.held[k] is not None:
                new = self.held[k] + self.span[0:1] * new
            self.held[k] = new
        if 2 * w < self.count:
            span = came[0][rows:]
            self.span = span if self.span is None else self.span * span
        self.distance = 2 * w

    def go_on(self, *others):
        self.absorb(*others)
        while self.distance < self.count:
            self.send()
            if 2 * self.distance >= self.count:
                return
            self.absorb()

    def result(self, *others):
        if self.distance < self.count:
            self.absorb(*others)
        return jnp.concatenate(self.held, axis=0)


def nn(a, b, precision=HIGH):
    return jnp.dot(a, b, precision=precision, preferred_element_type=F32)


def nt(a, b, precision=HIGH):
    return lax.dot_general(
        a, b, (((1,), (1,)), ((), ())), precision=precision, preferred_element_type=F32
    )


def tn(a, b, precision=HIGH):
    return lax.dot_general(
        a, b, (((0,), (0,)), ((), ())), precision=precision, preferred_element_type=F32
    )


def bf16_dot(a, b):
    return jnp.dot(a, b, preferred_element_type=F32)


def split_heads(values):
    top = values.astype(BF16)
    rest = values - top.astype(F32)
    mid = rest.astype(BF16)
    low = (rest - mid.astype(F32)).astype(BF16)
    return jnp.concatenate([top, mid, low], axis=1)


def spread_heads(values, spreader):
    return bf16_dot(split_heads(values), spreader)


def sum_heads(values, gatherer):
    top = values.astype(BF16)
    low = (values - top.astype(F32)).astype(BF16)
    return jnp.dot(top, gatherer, preferred_element_type=F32) + jnp.dot(
        low, gatherer, preferred_element_type=F32
    )


def order_mask(shape, kind):
    row, column = (lax.broadcasted_iota(jnp.int32, shape, d) for d in (0, 1))
    return {"ge": row >= column, "gt": row > column, "le": row <= column, "lt": row < column}[kind]


def triangle(kind):
    return jnp.where(order_mask((CUT, CUT), kind), 1.0, 0.0).astype(F32)


def conv_chunk(window_ref, taps_ref, bias_ref, cols):
    total = bias_ref[:, cols] + taps_ref[0:1, cols] * window_ref[EDGE - 3 : EDGE - 3 + CUT, cols]
    for k in range(1, CONV):
        at = EDGE - 3 + k
        total = total + taps_ref[k : k + 1, cols] * window_ref[at : at + CUT, cols]
    return total


def prepare_kernel(
    proj_ref,
    edge_ref,
    taps_ref,
    bias_ref,
    dtb_ref,
    alog_ref,
    spreader_ref,
    act_ref,
    step_ref,
    slope_ref,
    logd_ref,
    local_ref,
    before_ref,
    total_ref,
    window,
    state,
    logs,
):
    q = pl.program_id(0)

    @pl.when(q == 0)
    def _():
        window[0:EDGE, :] = edge_ref[:, 0:MIXED]
        state[...] = jnp.zeros_like(state)
        logs[...] = jnp.zeros_like(logs)

    @pl.when(q > 0)
    def _():
        window[0:EDGE, :] = window[CUT : CUT + EDGE, :]

    window[EDGE : EDGE + CUT, :] = proj_ref[:, 0:MIXED]

    def conv(c, carry):
        cols = pl.ds(pl.multiple_of(c * STRIP, STRIP), STRIP)
        out = conv_chunk(window, taps_ref, bias_ref, cols)
        act_ref[:, cols] = out * jax.nn.sigmoid(out)
        return carry

    lax.fori_loop(0, MIXED // STRIP, conv, 0, unroll=3)
    raw = proj_ref[:, MIXED:RATED] + dtb_ref[...]
    step = jnp.maximum(raw, 0.0) + jnp.log1p(jnp.exp(-jnp.abs(raw)))
    logd = nn(triangle("ge"), -jnp.exp(alog_ref[...]) * step, EXACT)
    step_ref[...] = step
    slope_ref[...] = jax.nn.sigmoid(raw)
    logd_ref[...] = logd
    last = logd[CUT - 1 : CUT, :]
    tail = spread_heads(jnp.exp(last - logd) * step, spreader_ref[...])
    added = tn(act_ref[:, DI : DI + STATE], act_ref[:, 0:DI] * tail)
    decay = spread_heads(jnp.broadcast_to(jnp.exp(last), (8, HEADS)), spreader_ref[...])
    state[...] = state[...] * decay[0:1, :] + added
    local_ref[0] = state[...]
    before_ref[...] = jnp.exp(logs[...])
    logs[...] = logs[...] + jnp.broadcast_to(last, (8, HEADS))
    total_ref[...] = jnp.exp(logs[...])


def full(shape):
    return pl.BlockSpec(shape, lambda i: (0,) * len(shape))


def params():
    return pltpu.CompilerParams(
        dimension_semantics=("arbitrary",), vmem_limit_bytes=52 * 1024 * 1024
    )


def prepare(proj, taps, bias, dt_bias, a_log, spreader):
    rows = proj.shape[0] - EDGE
    cuts = rows // CUT
    return pl.pallas_call(
        prepare_kernel,
        grid=(cuts,),
        in_specs=[
            pl.BlockSpec((CUT, WIDE), lambda i: (i, 0)),
            pl.BlockSpec((EDGE, WIDE), lambda i: (rows // EDGE, 0)),
            full((CONV, MIXED)),
            full((1, MIXED)),
            full((1, HEADS)),
            full((1, HEADS)),
            full((3 * HEADS, DI)),
        ],
        out_specs=[
            pl.BlockSpec((CUT, MIXED), lambda i: (i, 0)),
            pl.BlockSpec((CUT, HEADS), lambda i: (i, 0)),
            pl.BlockSpec((CUT, HEADS), lambda i: (i, 0)),
            pl.BlockSpec((CUT, HEADS), lambda i: (i, 0)),
            pl.BlockSpec((1, STATE, DI), lambda i: (i, 0, 0)),
            pl.BlockSpec((8, HEADS), lambda i: (i, 0)),
            full((8, HEADS)),
        ],
        out_shape=[
            jax.ShapeDtypeStruct((rows, MIXED), F32),
            jax.ShapeDtypeStruct((rows, HEADS), F32),
            jax.ShapeDtypeStruct((rows, HEADS), F32),
            jax.ShapeDtypeStruct((rows, HEADS), F32),
            jax.ShapeDtypeStruct((cuts, STATE, DI), F32),
            jax.ShapeDtypeStruct((8 * cuts, HEADS), F32),
            jax.ShapeDtypeStruct((8, HEADS), F32),
        ],
        scratch_shapes=[
            pltpu.VMEM((CUT + EDGE, MIXED), F32),
            pltpu.VMEM((STATE, DI), F32),
            pltpu.VMEM((8, HEADS), F32),
        ],
        compiler_params=params(),
        cost_estimate=FREE,
        name="prepare",
    )(proj, proj, taps, bias, dt_bias, a_log, spreader)


def both_columns(pair, left):
    turned = pltpu.roll(pair, HDIM, 1)
    return (jnp.where(left, pair, turned), jnp.where(left, turned, pair))


def stacked_pair(pair, left):
    zero = jnp.zeros_like(pair)
    return jnp.concatenate([jnp.where(left, pair, zero), jnp.where(left, zero, pair)], axis=0)


UNROLL = 8


def intra_kernel(
    act_ref, step_ref, logd_ref, skip_ref, spreader_ref, out_ref, logx, weighted, log_rows, scores
):
    spreader = spreader_ref[...]
    logd = logd_ref[...]
    logx[...] = spread_heads(logd, spreader)
    log_rows[...] = logd.T
    heads_in = act_ref[:, 0:DI]
    weighted[...] = heads_in * spread_heads(step_ref[...], spreader)
    scores[...] = nt(act_ref[:, DI + STATE : MIXED], act_ref[:, DI : DI + STATE])

    def pair(j, carry):
        cols = pl.ds(pl.multiple_of(j * PAIR, PAIR), PAIR)
        left = lax.broadcasted_iota(jnp.int32, (CUT, PAIR), 1) < HDIM
        mask = order_mask((CUT, CUT), "ge")
        mixes = []
        for side, column in enumerate(both_columns(logx[:, cols], left)):
            row = log_rows[pl.ds(2 * j + side, 1), :]
            mixes.append(jnp.exp(jnp.where(mask, column - row, -1e30)) * scores[...])
        out_ref[:, cols] = skip_ref[:, cols] * act_ref[:, cols] + nn(
            jnp.concatenate(mixes, axis=1), stacked_pair(weighted[:, cols], left)
        )
        return carry

    lax.fori_loop(0, HEADS // 2, pair, 0, unroll=UNROLL)


def intra(act, step, logd, skip, spreader):
    rows = act.shape[0]

    def at(width):
        return pl.BlockSpec((CUT, width), lambda i: (i, 0))

    return pl.pallas_call(
        intra_kernel,
        grid=(rows // CUT,),
        in_specs=[at(MIXED), at(HEADS), at(HEADS), full((1, DI)), full((3 * HEADS, DI))],
        out_specs=at(DI),
        out_shape=jax.ShapeDtypeStruct((rows, DI), F32),
        scratch_shapes=[
            pltpu.VMEM((CUT, DI), F32),
            pltpu.VMEM((CUT, DI), F32),
            pltpu.VMEM((HEADS, CUT), F32),
            pltpu.VMEM((CUT, CUT), F32),
        ],
        compiler_params=params(),
        cost_estimate=FREE,
        name="intra",
    )(act, step, logd, skip, spreader)


def mixer_kernel(
    act_ref,
    logd_ref,
    inner_ref,
    gate_left_ref,
    gate_right_ref,
    dng_ref,
    local_ref,
    enter_ref,
    before_ref,
    ggain_ref,
    spreader_ref,
    ng_ref,
    dy_ref,
    dz_ref,
    gin_ref,
    ggrad_ref,
    skipg_ref,
    grown,
    out,
    gstate,
):
    i = pl.program_id(0)
    q = pl.num_programs(0) - 1 - i
    spreader = spreader_ref[...]

    @pl.when(i == 0)
    def _():
        gstate[...] = jnp.zeros_like(gstate)
        ggrad_ref[...] = jnp.zeros_like(ggrad_ref)
        skipg_ref[...] = jnp.zeros_like(skipg_ref)

    logd = logd_ref[...]
    grown[...] = spread_heads(jnp.exp(logd), spreader)
    before = spread_heads(before_ref[...], spreader)[0:1, :]
    entering = enter_ref[...] * before + jnp.where(q == 0, 0.0, local_ref[0])
    c_state = act_ref[:, DI + STATE : MIXED]
    out[...] = grown[...] * nn(c_state, entering) + inner_ref[...]

    def gate(k, carry):
        rows = pl.ds(pl.multiple_of(k * 8, 8), 8)
        ssd = out[rows, :]
        gate_in = jnp.concatenate([gate_left_ref[rows, :], gate_right_ref[rows, :]], axis=1)
        sg = jax.nn.sigmoid(gate_in)
        silu = gate_in * sg
        gated = ssd * silu
        scale = lax.rsqrt(jnp.mean(gated * gated, axis=1, keepdims=True) + epsilon)
        unit = gated * scale
        ng_ref[rows, :] = unit * ggain_ref[...]
        dng = dng_ref[rows, :]
        e = dng * ggain_ref[...]
        ggrad_ref[...] += dng * unit
        dgated = scale * (e - unit * jnp.mean(e * unit, axis=1, keepdims=True))
        dy = dgated * silu
        dy_ref[rows, :] = dy
        dz_ref[rows, :] = dgated * ssd * (sg * (1.0 + gate_in * (1.0 - sg)))
        skipg_ref[...] += dy * act_ref[rows, 0:DI]
        return carry

    lax.fori_loop(0, CUT // 8, gate, 0, unroll=GATE_UNROLL)
    gstate[...] = gstate[...] * grown[CUT - 1 : CUT, :] + tn(c_state, grown[...] * dy_ref[...])
    gin_ref[0] = gstate[...]


GATE_UNROLL = 4


def mixer(act, logd, inner, gates, dng, local, entering, before, ggain, spreader):
    rows = act.shape[0]
    cuts = rows // CUT

    def back(width):
        return pl.BlockSpec((CUT, width), lambda i: (cuts - 1 - i, 0))

    wide = jax.ShapeDtypeStruct((rows, DI), F32)
    return pl.pallas_call(
        mixer_kernel,
        grid=(cuts,),
        in_specs=[
            back(MIXED),
            back(HEADS),
            back(DI),
            back(DI // 2),
            back(DI // 2),
            back(DI),
            pl.BlockSpec((1, STATE, DI), lambda i: (jnp.maximum(cuts - 2 - i, 0), 0, 0)),
            full((STATE, DI)),
            pl.BlockSpec((8, HEADS), lambda i: (cuts - 1 - i, 0)),
            full((1, DI)),
            full((3 * HEADS, DI)),
        ],
        out_specs=[
            back(DI),
            back(DI),
            back(DI),
            pl.BlockSpec((1, STATE, DI), lambda i: (cuts - 1 - i, 0, 0)),
            full((8, DI)),
            full((8, DI)),
        ],
        out_shape=[
            wide,
            wide,
            wide,
            jax.ShapeDtypeStruct((cuts, STATE, DI), F32),
            jax.ShapeDtypeStruct((8, DI), F32),
            jax.ShapeDtypeStruct((8, DI), F32),
        ],
        scratch_shapes=[
            pltpu.VMEM((CUT, DI), F32),
            pltpu.VMEM((CUT, DI), F32),
            pltpu.VMEM((STATE, DI), F32),
        ],
        compiler_params=params(),
        cost_estimate=FREE,
        name="mixer",
    )(act, logd, inner, *gates, dng, local, entering, before, ggain, spreader)


def back_intra_kernel(
    act_ref,
    step_ref,
    logd_ref,
    dy_ref,
    spreader_ref,
    dweighted_ref,
    dstates_ref,
    moved_ref,
    logx,
    weighted,
    log_rows,
    sum_rows,
    scores,
    dscores,
    sum_columns,
):
    spreader = spreader_ref[...]
    logd = logd_ref[...]
    logx[...] = spread_heads(logd, spreader)
    log_rows[...] = logd.T
    weighted[...] = act_ref[:, 0:DI] * spread_heads(step_ref[...], spreader)
    b_state = act_ref[:, DI : DI + STATE]
    c_state = act_ref[:, DI + STATE : MIXED]
    scores[...] = nt(b_state, c_state)
    dscores[...] = jnp.zeros_like(dscores)
    sum_columns[...] = jnp.zeros_like(sum_columns)

    def pair(j, carry):
        cols = pl.ds(pl.multiple_of(j * PAIR, PAIR), PAIR)
        left = lax.broadcasted_iota(jnp.int32, (CUT, PAIR), 1) < HDIM
        mask = order_mask((CUT, CUT), "le")
        strict = order_mask((CUT, CUT), "lt")
        dy = dy_ref[:, cols]
        dmix = nt(stacked_pair(weighted[:, cols], left), dy)
        mixes = []
        lane = lax.broadcasted_iota(jnp.int32, (CUT, CUT), 1)
        for side, column in enumerate(both_columns(logx[:, cols], left)):
            row = log_rows[pl.ds(2 * j + side, 1), :]
            weights = jnp.exp(jnp.where(mask, row - column, -1e30))
            mixes.append(weights * scores[...])
            part = dmix[side * CUT : (side + 1) * CUT, :] * weights
            dscores[...] += part
            moved = jnp.where(strict, part * scores[...], 0.0)
            sum_rows[pl.ds(2 * j + side, 1), :] = jnp.sum(moved, axis=0, keepdims=True)
            sum_columns[...] += jnp.where(
                lane == 2 * j + side, jnp.sum(moved, axis=1, keepdims=True), 0.0
            )
        dweighted_ref[:, cols] = nn(jnp.concatenate(mixes, axis=1), stacked_pair(dy, left))
        return carry

    lax.fori_loop(0, HEADS // 2, pair, 0, unroll=BACK_UNROLL)
    dstates_ref[:, 0:STATE] = nn(dscores[...], c_state)
    dstates_ref[:, STATE : 2 * STATE] = tn(dscores[...], b_state)
    moved_ref[...] = sum_rows[...].T - sum_columns[:, 0:HEADS]


BACK_UNROLL = 8


def back_intra(act, step, logd, dy, spreader):
    rows = act.shape[0]

    def at(width):
        return pl.BlockSpec((CUT, width), lambda i: (i, 0))

    return pl.pallas_call(
        back_intra_kernel,
        grid=(rows // CUT,),
        in_specs=[at(MIXED), at(HEADS), at(HEADS), at(DI), full((3 * HEADS, DI))],
        out_specs=[at(DI), at(2 * STATE), at(HEADS)],
        out_shape=[
            jax.ShapeDtypeStruct((rows, DI), F32),
            jax.ShapeDtypeStruct((rows, 2 * STATE), F32),
            jax.ShapeDtypeStruct((rows, HEADS), F32),
        ],
        scratch_shapes=[
            pltpu.VMEM((CUT, DI), F32),
            pltpu.VMEM((CUT, DI), F32),
            pltpu.VMEM((HEADS, CUT), F32),
            pltpu.VMEM((HEADS, CUT), F32),
            pltpu.VMEM((CUT, CUT), F32),
            pltpu.VMEM((CUT, CUT), F32),
            pltpu.VMEM((CUT, CUT), F32),
        ],
        compiler_params=params(),
        cost_estimate=FREE,
        name="back_intra",
    )(act, step, logd, dy, spreader)


def back_kernel(
    act_ref,
    step_ref,
    slope_ref,
    logd_ref,
    dy_ref,
    dweighted_ref,
    dstates_ref,
    moved_ref,
    local_ref,
    enter_ref,
    before_ref,
    gin_ref,
    gout_ref,
    proj_ref,
    halo_ref,
    taps_ref,
    bias_ref,
    alog_ref,
    skip_ref,
    spreader_ref,
    gatherer_ref,
    dproj_ref,
    dtaps_ref,
    dbias_ref,
    dlog_ref,
    ddtb_ref,
    dact,
    window,
    dwindow,
    after,
):
    i = pl.program_id(0)
    cuts = pl.num_programs(0)
    q = cuts - 1 - i

    @pl.when(i == 0)
    def _():
        after[...] = jnp.zeros_like(after)
        dwindow[...] = jnp.zeros_like(dwindow)
        for ref in (dtaps_ref, dbias_ref, dlog_ref, ddtb_ref):
            ref[...] = jnp.zeros_like(ref)

    @pl.when(i > 0)
    def _():
        dwindow[CUT : CUT + EDGE, :] = dwindow[0:EDGE, :]

    logd = logd_ref[...]
    step = step_ref[...]
    last = logd[CUT - 1 : CUT, :]
    b_state = act_ref[:, DI : DI + STATE]
    c_state = act_ref[:, DI + STATE : MIXED]
    grow_parts = split_heads(jnp.exp(logd))
    tail_parts = split_heads(jnp.exp(last - logd))
    step_parts = split_heads(step)
    before_parts = split_heads(before_ref[...])
    later_parts = split_heads(jnp.exp(after[...]))
    after[...] = after[...] + jnp.broadcast_to(last, (8, HEADS))
    db = dstates_ref[:, 0:STATE]
    dc = dstates_ref[:, STATE : 2 * STATE]
    moved = moved_ref[...]
    lost = jnp.zeros((CUT, HEADS), F32)
    dstep = jnp.zeros((CUT, HEADS), F32)
    kept = jnp.zeros((8, HEADS), F32)
    for c in range(DI // BLOCK):
        cols = slice(c * BLOCK, (c + 1) * BLOCK)
        spreader = spreader_ref[:, cols]
        gatherer = gatherer_ref[cols, :]
        entering = enter_ref[:, cols] * bf16_dot(before_parts, spreader)[0:1, :]
        entering = entering + jnp.where(q == 0, 0.0, local_ref[0, :, cols])
        gout = gout_ref[:, cols] * bf16_dot(later_parts, spreader)[0:1, :]
        gout = gout + jnp.where(i == 0, 0.0, gin_ref[0, :, cols])
        tail = bf16_dot(tail_parts, spreader)
        steps = bf16_dot(step_parts, spreader)
        heads_in = act_ref[:, cols]
        dy = dy_ref[:, cols]
        from_state = tail * nn(b_state, gout)
        stepped = heads_in * steps
        dweighted = dweighted_ref[:, cols] + from_state
        carried = bf16_dot(grow_parts, spreader) * dy
        db = db + nt(tail * stepped, gout)
        dc = dc + nt(carried, entering)
        dact[:, cols] = dweighted * steps + skip_ref[:, cols] * dy
        moved = moved + sum_heads(carried * nn(c_state, entering), gatherer)
        lost = lost + sum_heads(stepped * from_state, gatherer)
        dstep = dstep + sum_heads(heads_in * dweighted, gatherer)
        kept = kept + sum_heads(
            jnp.broadcast_to(jnp.sum(gout * entering, axis=0, keepdims=True), (8, BLOCK)), gatherer
        )
    dact[:, DI : DI + STATE] = db
    dact[:, DI + STATE : MIXED] = dc
    dlog = (
        nn(triangle("le"), moved, EXACT)
        + nn(triangle("gt"), lost, EXACT)
        + jnp.exp(last) * kept[0:1, :]
    )
    rate = -jnp.exp(alog_ref[...])
    dlog_ref[...] += jnp.broadcast_to(
        jnp.sum(dlog * step, axis=0, keepdims=True) * rate, (8, HEADS)
    )
    draw = (dstep + dlog * rate) * slope_ref[...]
    ddtb_ref[...] += jnp.broadcast_to(jnp.sum(draw, axis=0, keepdims=True), (8, HEADS))
    here = pl.ds(pl.multiple_of(q * CUT, CUT), CUT)
    dproj_ref[here, MIXED:WIDE] = jnp.concatenate([draw, jnp.zeros((CUT, SPARE), F32)], axis=1)
    window[0:EDGE, :] = halo_ref[:, 0:MIXED]
    window[EDGE : EDGE + CUT, :] = proj_ref[:, 0:MIXED]

    def conv(c, carry):
        cols = pl.ds(pl.multiple_of(c * STRIP, STRIP), STRIP)
        out = conv_chunk(window, taps_ref, bias_ref, cols)
        sg = jax.nn.sigmoid(out)
        dout = dact[:, cols] * (sg * (1.0 + out * (1.0 - sg)))
        dwindow[0:CUT, cols] = dout
        dbias_ref[:, cols] += jnp.sum(dout.reshape(CUT // 8, 8, STRIP), axis=0)
        for k in range(CONV):
            at = EDGE - 3 + k
            dtaps_ref[8 * k : 8 * k + 8, cols] += jnp.sum(
                (dout * window[at : at + CUT, cols]).reshape(CUT // 8, 8, STRIP), axis=0
            )
        din = taps_ref[CONV - 1 : CONV, cols] * dout
        for k in range(CONV - 1):
            din = din + taps_ref[k : k + 1, cols] * dwindow[3 - k : 3 - k + CUT, cols]
        dproj_ref[here, cols] = din
        return carry

    lax.fori_loop(0, MIXED // STRIP, conv, 0, unroll=3)

    @pl.when(q == 0)
    def _():
        rows = cuts * CUT
        window[0:EDGE, :] = jnp.zeros((EDGE, MIXED), F32)
        window[EDGE : 2 * EDGE, :] = dwindow[0:EDGE, :]
        din = taps_ref[CONV - 1 : CONV, :] * window[0:EDGE, :]
        for k in range(CONV - 1):
            din = din + taps_ref[k : k + 1, :] * window[3 - k : 3 - k + EDGE, :]
        dproj_ref[rows : rows + EDGE, 0:MIXED] = din
        dproj_ref[rows : rows + EDGE, MIXED:WIDE] = jnp.zeros((EDGE, WIDE - MIXED), F32)


def back(
    act, step, slope, logd, dy, dweighted, dstates, moved, local, entering, before, gin, gout, proj, taps, bias, a_log,
    skip, spreader, gatherer,
):
    rows = act.shape[0]
    cuts = rows // CUT

    def at(size):
        return pl.BlockSpec((CUT, size), lambda i: (cuts - 1 - i, 0))

    def halo(i):
        q = cuts - 1 - i
        return (jnp.where(q == 0, rows // EDGE, q * (CUT // EDGE) - 1), 0)

    return pl.pallas_call(
        back_kernel,
        grid=(cuts,),
        in_specs=[
            at(MIXED),
            at(HEADS),
            at(HEADS),
            at(HEADS),
            at(DI),
            at(DI),
            at(2 * STATE),
            at(HEADS),
            pl.BlockSpec((1, STATE, DI), lambda i: (jnp.maximum(cuts - 2 - i, 0), 0, 0)),
            full((STATE, DI)),
            pl.BlockSpec((8, HEADS), lambda i: (cuts - 1 - i, 0)),
            pl.BlockSpec((1, STATE, DI), lambda i: (jnp.minimum(cuts - i, cuts - 1), 0, 0)),
            full((STATE, DI)),
            at(WIDE),
            pl.BlockSpec((EDGE, WIDE), halo),
            full((CONV, MIXED)),
            full((1, MIXED)),
            full((1, HEADS)),
            full((1, DI)),
            full((3 * HEADS, DI)),
            full((DI, HEADS)),
        ],
        out_specs=[
            full((rows + EDGE, WIDE)),
            full((8 * CONV, MIXED)),
            full((8, MIXED)),
            full((8, HEADS)),
            full((8, HEADS)),
        ],
        out_shape=[
            jax.ShapeDtypeStruct((rows + EDGE, WIDE), F32),
            jax.ShapeDtypeStruct((8 * CONV, MIXED), F32),
            jax.ShapeDtypeStruct((8, MIXED), F32),
            jax.ShapeDtypeStruct((8, HEADS), F32),
            jax.ShapeDtypeStruct((8, HEADS), F32),
        ],
        scratch_shapes=[
            pltpu.VMEM((CUT, MIXED), F32),
            pltpu.VMEM((CUT + EDGE, MIXED), F32),
            pltpu.VMEM((CUT + EDGE, MIXED), F32),
            pltpu.VMEM((8, HEADS), F32),
        ],
        compiler_params=params(),
        cost_estimate=FREE,
        name="back",
    )(
        act, step, slope, logd, dy, dweighted, dstates, moved, local, entering, before, gin, gout, proj, proj,
        taps, bias, a_log, skip, spreader, gatherer,
    )


COLUMNS = 512


def right_kernel(x_ref, w_ref, added_ref, scale_ref, out_ref):
    out_ref[...] = (nn(x_ref[...], w_ref[...]) + added_ref[...]) * scale_ref[...]


def right(x, w, added, scale):
    (rows, depth), cols = (x.shape, w.shape[1])
    tile = pl.BlockSpec((rows, COLUMNS), lambda j: (0, j))
    return pl.pallas_call(
        right_kernel,
        grid=(cols // COLUMNS,),
        in_specs=[
            full((rows, depth)), pl.BlockSpec((depth, COLUMNS), lambda j: (0, j)), tile, full((rows, 1)),
        ],
        out_specs=tile,
        out_shape=jax.ShapeDtypeStruct((rows, cols), F32),
        compiler_params=params(),
        cost_estimate=FREE,
        name="right",
    )(x, w, added, scale)


def right_back_kernel(x_ref, *refs):
    *w_refs, out_ref = refs
    total, at = (None, 0)
    for w_ref in w_refs:
        part = nt(x_ref[:, at : at + w_ref.shape[1]], w_ref[...])
        total, at = (part if total is None else total + part, at + w_ref.shape[1])
    out_ref[...] = total


def right_back(x, weights):
    rows, cols = (x.shape[0], weights[0].shape[0])
    return pl.pallas_call(
        right_back_kernel,
        grid=(cols // COLUMNS,),
        in_specs=[full(x.shape)]
        + [pl.BlockSpec((COLUMNS, w.shape[1]), lambda j: (j, 0)) for w in weights],
        out_specs=pl.BlockSpec((rows, COLUMNS), lambda j: (0, j)),
        out_shape=jax.ShapeDtypeStruct((rows, cols), F32),
        compiler_params=params(),
        cost_estimate=FREE,
        name="right_back",
    )(x, *weights)


def head_spreader():
    head = lax.broadcasted_iota(jnp.int32, (3 * HEADS, DI), 0) % HEADS
    return (head == lax.broadcasted_iota(jnp.int32, (3 * HEADS, DI), 1) // HDIM).astype(BF16)


def head_gatherer():
    channel = lax.broadcasted_iota(jnp.int32, (DI, HEADS), 0) // HDIM
    return (channel == lax.broadcasted_iota(jnp.int32, (DI, HEADS), 1)).astype(BF16)


def per_device(
    hidden_in,
    lengths,
    norm_gain,
    in_weight,
    conv_weight,
    conv_bias,
    dt_bias,
    a_log,
    skip_gain,
    gated_gain,
    out_weight,
    cotangent,
):
    width = hidden_in.shape[-1]
    devices = 1
    for axis in AXES:
        devices *= lax.axis_size(axis)
    mine, spot, count = (lax.axis_index("p"), lax.axis_index("zc"), lax.axis_size("zc"))
    own_rows = width // devices

    in_piece = in_weight.reshape(own_rows, -1)
    small = jnp.concatenate([conv_weight, conv_bias])
    padded = jnp.pad(small, (0, SPARE * own_rows - small.shape[0])).reshape(own_rows, SPARE)
    conv = Gather(jnp.concatenate([in_piece[:, DI:], padded], axis=1), 0.5)
    edge = before_span(hidden_in, mine)
    conv.line()
    trade = Exchange(hidden_in, mine)
    hidden = trade.result(jnp.concatenate)
    rows = hidden.shape[0]
    out_piece = out_weight.reshape(-1, width)
    rest = jnp.concatenate([in_piece[:, :width], in_piece[:, width:DI], out_piece], axis=0)
    rest = lax.all_gather(rest, AXES, axis=0).reshape(devices, -1, width)
    w_gates = [
        rest[:, k * own_rows : (k + 1) * own_rows].reshape(width, width) for k in range(DI // width)
    ]
    w_out = rest[:, DI // width * own_rows :].reshape(DI, width)
    near = conv.near(trade.other)
    conv_over = conv.across(conv.held_near()[:1], conv.block)
    far = conv.far()
    conv_over += conv.across(conv.held_near()[1:])
    conv_over += conv.across(conv.corners)
    (w_conv,) = place(conv.held() + conv_over, conv.rows, [[(0, WIDE)]])
    other = Exchange(tied([cotangent], *far)[0], mine)
    smalls = w_conv[:, RATED:].reshape(devices, own_rows * SPARE)
    taps = smalls[:, : conv_weight.shape[0]].reshape(CONV, MIXED)
    bias = smalls[:, conv_weight.shape[0] : small.shape[0]].reshape(1, MIXED)

    extended = jnp.concatenate([hidden, edge], axis=0)
    scale = lax.rsqrt(jnp.mean(extended * extended, axis=1, keepdims=True) + epsilon)
    unit = extended * scale
    normed = unit * norm_gain
    inner = normed[:rows]
    spreader, gatherer = (head_spreader(), head_gatherer())
    dt_row, alog_row = (dt_bias.reshape(1, -1), a_log.reshape(1, -1))
    skip_row = jnp.repeat(skip_gain, HDIM).reshape(1, DI)
    positions = spot * rows + lax.iota(jnp.int32, rows)
    length = lax.dynamic_index_in_dim(lengths, mine, 0, keepdims=False)
    valid = (positions < length).astype(F32)[:, None]
    proj = nn(normed, w_conv)
    act, step, slope, logd, local, before, total = prepare(
        proj, taps, bias, dt_row, alog_row, spreader
    )
    total_row = jnp.repeat(total[0], HDIM).reshape(1, DI)
    states = States(total_row, local[-1], False)
    states.send()
    within = intra(tied([act], *states.sends)[0], step, logd, skip_row, spreader)
    (turn,) = tied([inner], within)
    gates = [nn(turn, w) for w in w_gates]
    states.go_on(*gates)
    grad_out = other.result(jnp.concatenate, within) * valid
    dng = nt(tied([grad_out], *gates, *states.sends)[0], w_out)
    entering = states.result(dng)
    ng, dy, dz, gin, ggrad, skipg = mixer(
        act, logd, within, gates, dng, local, entering, before, gated_gain.reshape(1, DI), spreader
    )
    ng_keep, ng_send = core_columns(ng)
    in_keep, in_send = core_columns(normed)
    grads = States(total_row, gin[0], True)
    grads.send()
    (turn,) = tied([ng_send], *grads.sends)
    first = tn(turn, grad_out)
    (turn,) = tied([grad_out], first)
    second = tn(ng_keep, turn)
    grad_wout = Scatter(first, second)
    branch = right(tied([ng], second)[0], w_out, hidden, valid)
    traded = Exchange(halves(branch), mine)
    grads.go_on(branch)
    grad_wout.keep(branch)
    grad_wout.stage(("p", "y"))
    (turn,) = tied([dz], branch, *grads.sends, *grad_wout.sends)
    first = tn(in_send[:rows], turn)
    (turn,) = tied([turn], first)
    second = tn(in_keep[:rows], turn)
    grad_wgate = Scatter(first, second)
    back_parts = back_intra(tied([act], second)[0], step, logd, dy, spreader)
    grad_wout.keep(back_parts[1])
    grad_wgate.keep(back_parts[1])
    grad_wout.stage(("y", "p"))
    grad_wgate.stage(("p", "y"))
    (turn,) = tied([dz], back_parts[1], *grad_wout.sends, *grad_wgate.sends, traded.other)
    dgate_normed = right_back(turn, w_gates)
    grad_wout.keep(dgate_normed)
    grad_wout.last_at_once()
    gout = grads.result(dgate_normed)
    dproj, dtaps, dbias, dlog, ddtb = back(
        tied([act], dgate_normed, *grad_wout.sends)[0], step, slope, logd, dy, *back_parts, local,
        entering, before, gin, gout, proj, taps, bias, alog_row, skip_row, spreader, gatherer,
    )
    dtaps = jnp.sum(dtaps.reshape(CONV, 8, MIXED), axis=1).reshape(devices, -1)
    dbias = jnp.sum(dbias, axis=0).reshape(devices, -1)
    dsmall = jnp.concatenate([dtaps, dbias], axis=1)
    dsmall = jnp.pad(dsmall, ((0, 0), (0, SPARE * own_rows - small.shape[0])))
    dsmall = jnp.pad(dsmall.reshape(width, SPARE), ((0, 0), (RATED, 0)))
    small_keep, small_send = (core_rows(dsmall, k) for k in (0, 1))
    grad_wout.settle()
    grad_wgate.keep(ddtb)
    grad_wgate.stage(("y", "p"))
    (turn,) = tied([dproj], *grad_wgate.sends, grad_wout.line)
    first = tn(in_send, turn) + small_send
    (turn,) = tied([dproj], first)
    second = tn(in_keep, turn) + small_keep
    grad_wconv = Scatter(first, second)
    grad_wconv.keep(second)
    grad_wconv.stage(("p", "y"))
    grad_wgate.keep(second, *grad_wconv.sends)
    grad_wgate.last_at_once()
    dnormed = nt(tied([dproj], second, *grad_wconv.sends, *grad_wgate.sends)[0], w_conv)
    grad_wgate.settle(dnormed)
    near = grad_wconv.came
    output = traded.result(jnp.stack, dnormed)
    returned = lax.ppermute(dnormed[rows:], "zc", [(i + 1, i) for i in range(count - 1)])
    dnormed = dnormed[:rows] + dgate_normed
    dnormed = dnormed + jnp.pad(returned, ((rows - EDGE, 0), (0, 0)))
    unit = unit[:rows]
    dunit = dnormed * norm_gain
    dhidden = scale[:rows] * (dunit - unit * jnp.mean(dunit * unit, axis=1, keepdims=True))
    grad_input = Exchange(halves(tied([grad_out + dhidden], *near)[0]), mine).result(jnp.stack)
    grad_skip = jnp.sum(jnp.sum(skipg, axis=0).reshape(HEADS, HDIM), axis=1)
    sums = jnp.concatenate(
        [
            jnp.sum(dnormed * unit, axis=0),
            jnp.sum(ggrad, axis=0),
            ddtb[0],
            dlog[0],
            grad_skip,
        ]
    )
    (sums,) = tied([jnp.pad(sums, (0, -sums.shape[0] % 128)).reshape(-1, 128)], *near)
    sums = sum_everywhere(sums).reshape(-1)
    grad_wconv.stage(("y", "p"))
    grad_wconv.last()
    parts = []
    for size in (width, DI, HEADS, HEADS, HEADS):
        parts.append(sums[:size])
        sums = sums[size:]
    conv_grad = grad_wconv.result()
    small_grad = conv_grad[:, RATED:].reshape(-1)
    return (
        output,
        grad_input,
        parts[0],
        jnp.concatenate([grad_wgate.result(), conv_grad[:, :RATED]], axis=1).reshape(-1),
        small_grad[: conv_weight.shape[0]],
        small_grad[conv_weight.shape[0] : small.shape[0]],
        parts[2],
        parts[3],
        parts[4],
        parts[1],
        grad_wout.result().reshape(-1),
    )


def core_columns(values):
    size = values.shape[1] // (2 * lax.axis_size("y"))
    core = lax.axis_index("core")
    return [
        jnp.concatenate(
            [
                lax.dynamic_slice_in_dim(values, (2 * y + (core + k) % 2) * size, size, 1)
                for y in range(lax.axis_size("y"))
            ],
            axis=1,
        )
        for k in (0, 1)
    ]


def core_rows(values, k):
    size = values.shape[0] // (2 * lax.axis_size("y"))
    core = lax.axis_index("core")
    return jnp.concatenate(
        [
            lax.dynamic_slice_in_dim(values, (2 * y + (core + k) % 2) * size, size, 0)
            for y in range(lax.axis_size("y"))
        ],
        axis=0,
    )


def solution(mesh):
    dp, seq = (mesh.shape["dp"], mesh.shape["seq"])
    finer = Mesh(mesh.devices.reshape(dp // 2, 2, seq // 2, 2), AXES)
    over_dp, over_seq = (("y", "core"), ("zc", "p"))
    tokens = P(over_dp, over_seq, None)
    in_specs = (
        tokens, P(over_dp), P(), P(AXES), P(AXES), P(AXES), P(), P(), P(), P(), P(AXES), tokens,
    )
    out_specs = (
        tokens, tokens, P(), P(AXES), P(AXES), P(AXES), P(), P(), P(), P(), P(AXES),
    )
    return jax.shard_map(
        per_device, mesh=finer, in_specs=in_specs, out_specs=out_specs, check_vma=False
    )
```

```python
import functools

import jax
import jax.numpy as jnp
from jax import lax
from jax.experimental import pallas as pl
from jax.experimental.pallas import tpu as pltpu
from jax.sharding import Mesh
from jax.sharding import PartitionSpec as P

DI = 2048
HEADS = 32
HDIM = 64
STATE = 128
CONV = 4
MIXED = DI + 2 * STATE
RATED = MIXED + HEADS
CUT = 128
EDGE = 8
PAIR = 2 * HDIM
SPARE = 128 - HEADS
WIDE = RATED + SPARE
STRIP = 128
BLOCK = 1024
F32 = jnp.float32
BF16 = jnp.bfloat16
HIGH = lax.Precision.HIGH
EXACT = lax.Precision.HIGHEST
epsilon = 1e-05
FREE = pl.CostEstimate(flops=0, bytes_accessed=0, transcendentals=0)


def shift(block, axis, step=1):
    count = lax.axis_size(axis)
    return lax.ppermute(block, axis, [(i, (i + step) % count) for i in range(count)])


AXES = ("y", "core", "zc", "p")


def offsets(block, axis):
    count = lax.axis_size(axis)
    return [block] + [shift(block, axis, k) for k in range(1, count)]


def ring(block, axis):
    held = [block]
    for _ in range(1, lax.axis_size(axis)):
        held.append(shift(held[-1], axis))
    return held


def after(value, *others):
    return lax.optimization_barrier((value,) + others)[0]


def place_kernel(count, own_rows, parts, where_ref, *refs):
    blocks, wholes = (refs[:count], refs[count:])
    spot = 0
    for block in blocks:
        for k in range(block.shape[0] // own_rows):
            for whole, cuts in zip(wholes, parts):
                for n, (start, stop) in enumerate(cuts):
                    row = (where_ref[spot] * len(cuts) + n) * own_rows
                    whole[pl.ds(pl.multiple_of(row, own_rows), own_rows), :] = block[
                        k * own_rows : (k + 1) * own_rows, start:stop
                    ]
            spot += 1


def place(blocks, own_rows, parts):
    sizes = {axis: lax.axis_size(axis) for axis in AXES}
    index = {axis: lax.axis_index(axis) for axis in AXES}
    devices = 1
    for axis in AXES:
        devices *= sizes[axis]
    where = []
    for slot, lines, _ in blocks:
        for k in lines:
            at = 0
            for axis in AXES:
                back = k if axis == "zc" else slot.get(axis, 0)
                at = at * sizes[axis] + (index[axis] - back) % sizes[axis]
            where.append(at)
    arrays = [block for _, _, block in blocks]
    shapes = [(devices * own_rows * len(cuts), cuts[0][1] - cuts[0][0]) for cuts in parts]
    if own_rows % 8:
        whole = jnp.zeros((devices, own_rows, arrays[0].shape[1]), F32)
        spots = iter(where)
        for block in arrays:
            for k in range(block.shape[0] // own_rows):
                whole = lax.dynamic_update_slice_in_dim(
                    whole, block[None, k * own_rows : (k + 1) * own_rows], next(spots), 0
                )
        return [
            jnp.concatenate([whole[:, :, a:b] for a, b in cuts], axis=1).reshape(shape)
            for cuts, shape in zip(parts, shapes)
        ]
    return pl.pallas_call(
        functools.partial(place_kernel, len(blocks), own_rows, parts),
        in_specs=[pl.BlockSpec(memory_space=pltpu.SMEM)]
        + [pl.BlockSpec(memory_space=pltpu.VMEM)] * len(blocks),
        out_specs=[pl.BlockSpec(memory_space=pltpu.VMEM)] * len(parts),
        out_shape=[jax.ShapeDtypeStruct(shape, F32) for shape in shapes],
        compiler_params=pltpu.CompilerParams(vmem_limit_bytes=48 * 1024 * 1024),
        cost_estimate=FREE,
        name="place",
    )(jnp.stack(where).astype(jnp.int32), *arrays)


def tied(values, *others):
    return list(lax.optimization_barrier((tuple(values), tuple(others)))[0])


class Gather:
    def __init__(self, piece, share):
        self.piece, self.rows, self.share = (piece, piece.shape[0], share)

    def line(self, *tie):
        (piece,) = tied([self.piece], *tie)
        self.lines = list(range(lax.axis_size("zc")))
        self.block = jnp.concatenate(offsets(piece, "zc"), axis=0)

    def line_at_once(self, *tie):
        (piece,) = tied([self.piece], *tie)
        count, index = (lax.axis_size("zc"), lax.axis_index("zc"))
        whole = lax.all_to_all(jnp.broadcast_to(piece, (count,) + piece.shape), "zc", 0, 0)
        self.lines = [index - k for k in range(count)]
        self.block = whole.reshape(-1, piece.shape[1])

    def near(self, *tie):
        (block,) = tied([self.block], *tie)
        self.rings = {axis: ring(block, axis)[1:] for axis in ("p", "y")}
        return [b for r in self.rings.values() for b in r]

    def keep_near(self, *others):
        self.rings = {axis: tied(r, *others) for axis, r in self.rings.items()}

    def keep_far(self, *others):
        arrays = tied([b for _, _, b in self.corners], *others)
        self.corners = [(slot, lines, b) for (slot, lines, _), b in zip(self.corners, arrays)]

    def far(self, *tie):
        middle = int(len(self.lines) * self.share)
        cut = middle * self.rows
        sides = {"p": [b[:cut] for b in self.rings["p"]], "y": [b[cut:] for b in self.rings["y"]]}
        other = {"p": "y", "y": "p"}
        self.corners = []
        for axis, blocks in sides.items():
            lines = self.lines[:middle] if axis == "p" else self.lines[middle:]
            blocks = tied(blocks, *tie)
            for k, block in enumerate(blocks):
                for n, moved in enumerate(ring(block, other[axis])[1:]):
                    self.corners.append(({axis: k + 1, other[axis]: n + 1}, lines, moved))
        return [b for _, _, b in self.corners]

    def held_near(self):
        near = [
            ({axis: k + 1}, self.lines, b) for axis, r in self.rings.items() for k, b in enumerate(r)
        ]
        return [({}, self.lines, self.block)] + near

    def held(self):
        return self.held_near() + self.corners

    def across(self, blocks, *tie):
        arrays = tied([b for _, _, b in blocks], *tie)
        return [
            ({**slot, "core": 1}, lines, shift(b, "core"))
            for (slot, lines, _), b in zip(blocks, arrays)
        ]


def indexed(addends, at, dim):
    total = None
    for addend in addends:
        part = lax.dynamic_index_in_dim(addend, at, dim, keepdims=False)
        total = part if total is None else total + part
    return total


class Scatter:
    def __init__(self, send, keep):
        self.shape = [lax.axis_size(a) for a in ("y", "zc", "p")] + [-1, keep.shape[-1]]
        moved = shift(send, "core")
        self.came = [moved]
        both = [keep.reshape(self.shape), moved.reshape(self.shape)]
        middle = self.shape[1] // 2
        self.parts = [
            ([v[:, :middle] for v in both], ["y", "zc", "p"]),
            ([v[:, middle:] for v in both], ["y", "zc", "p"]),
        ]

    def stage(self, axes):
        self.came, self.sends, parts = ([], [], [])
        for (addends, left), axis in zip(self.parts, axes):
            count, index, dim = (lax.axis_size(axis), lax.axis_index(axis), left.index(axis))
            came = []
            for k in range(1, count):
                moving = indexed(addends, (index + k) % count, dim)
                self.sends.append(moving)
                came.append(shift(moving, axis, k))
            kept = [lax.dynamic_index_in_dim(v, index, dim, keepdims=False) for v in addends]
            parts.append((kept + came, [a for a in left if a != axis]))
            self.came += came
            self.fresh = len(came)
        self.parts = parts

    def keep(self, *others):
        parts = []
        for addends, left in self.parts:
            fresh = self.fresh if left != ["y", "zc", "p"] else 1
            parts.append((addends[:-fresh] + tied(addends[-fresh:], *others), left))
        self.parts = parts

    def last(self, *tie):
        count, index = (lax.axis_size("zc"), lax.axis_index("zc"))
        line = jnp.concatenate([functools.reduce(jnp.add, v) for v, _ in self.parts], axis=0)
        if tie:
            line = after(line, *tie)
        self.came = [
            shift(lax.dynamic_index_in_dim(line, (index + k) % count, 0, keepdims=False), "zc", k)
            for k in range(1, count)
        ]
        self.kept = lax.dynamic_index_in_dim(line, index, 0, keepdims=False)

    def last_at_once(self):
        line = jnp.concatenate([functools.reduce(jnp.add, v) for v, _ in self.parts], axis=0)
        self.sends = [line]
        self.line = lax.all_to_all(line, "zc", 0, 0)

    def settle(self, *others):
        (line,) = tied([self.line], *others) if others else [self.line]
        self.came, self.kept = ([line[k] for k in range(1, line.shape[0])], line[0])

    def result(self):
        return functools.reduce(jnp.add, self.came, self.kept)


def sum_everywhere(values):
    for axis in ("core", "p", "y", "zc"):
        count, index = (lax.axis_size(axis), lax.axis_index(axis))
        if count == 2:
            values = values + shift(values, axis)
        else:
            held = jnp.stack(offsets(values, axis))
            values = functools.reduce(
                jnp.add,
                [
                    lax.dynamic_index_in_dim(held, (index - k) % count, 0, keepdims=False)
                    for k in range(count)
                ],
            )
    return values


class Exchange:
    def __init__(self, block, mine):
        self.mine = mine
        self.keep = lax.dynamic_index_in_dim(block, mine, 0, keepdims=False)
        self.other = shift(lax.dynamic_index_in_dim(block, 1 - mine, 0, keepdims=False), "p")

    def result(self, join, *others):
        (other,) = tied([self.other], *others)
        first = self.mine == 0
        return join([jnp.where(first, self.keep, other), jnp.where(first, other, self.keep)], axis=0)


def before_span(block, mine):
    count = lax.axis_size("zc")
    routes = [[(2 * i + 1, 2 * i + 2 + k) for i in range(count - 1)] for k in (0, 1)]
    ends = [lax.ppermute(block[k, -EDGE:], ("zc", "p"), routes[k]) for k in (0, 1)]
    return jnp.where(mine == 0, ends[0], ends[1])


def halves(span):
    return span.reshape(2, -1, span.shape[-1])


class States:
    chunks = 1

    def __init__(self, decay, added, reverse):
        self.count, self.reverse, self.distance = (lax.axis_size("zc"), reverse, 1)
        rows = added.shape[0] // self.chunks
        decay = jnp.broadcast_to(decay, (8, added.shape[1]))
        self.decay = decay
        self.added = [added[k * rows : (k + 1) * rows] for k in range(self.chunks)]
        self.held = [None] * self.chunks
        self.span = None

    def send(self):
        w = self.distance
        pairs = [(i, i + w) for i in range(self.count - w)]
        route = [(b, a) if self.reverse else (a, b) for a, b in pairs]
        self.came, self.sends = ([], [])
        for k in range(self.chunks):
            block = self.added[k]
            if self.held[k] is not None:
                block = block + self.decay[0:1] * self.held[k]
            if k == 0 and 2 * w < self.count:
                span = self.decay if self.span is None else self.decay * self.span
                block = jnp.concatenate([block, span], axis=0)
            self.sends.append(block)
            self.came.append(lax.ppermute(block, "zc", route))

    def absorb(self, *others):
        w, rows = (self.distance, self.added[0].shape[0])
        came = tied(self.came, *others) if others else self.came
        for k in range(self.chunks):
            new = came[k][:rows]
            if self.held[k] is not None:
                new = self.held[k] + self.span[0:1] * new
            self.held[k] = new
        if 2 * w < self.count:
            span = came[0][rows:]
            self.span = span if self.span is None else self.span * span
        self.distance = 2 * w

    def go_on(self, *others):
        self.absorb(*others)
        while self.distance < self.count:
            self.send()
            if 2 * self.distance >= self.count:
                return
            self.absorb()

    def result(self, *others):
        if self.distance < self.count:
            self.absorb(*others)
        return jnp.concatenate(self.held, axis=0)


def nn(a, b, precision=HIGH):
    return jnp.dot(a, b, precision=precision, preferred_element_type=F32)


def nt(a, b, precision=HIGH):
    return lax.dot_general(
        a, b, (((1,), (1,)), ((), ())), precision=precision, preferred_element_type=F32
    )


def tn(a, b, precision=HIGH):
    return lax.dot_general(
        a, b, (((0,), (0,)), ((), ())), precision=precision, preferred_element_type=F32
    )


def bf16_dot(a, b):
    return jnp.dot(a, b, preferred_element_type=F32)


def split_heads(values):
    top = values.astype(BF16)
    rest = values - top.astype(F32)
    mid = rest.astype(BF16)
    low = (rest - mid.astype(F32)).astype(BF16)
    return jnp.concatenate([top, mid, low], axis=1)


def spread_heads(values, spreader):
    return bf16_dot(split_heads(values), spreader)


def sum_heads(values, gatherer):
    top = values.astype(BF16)
    low = (values - top.astype(F32)).astype(BF16)
    return jnp.dot(top, gatherer, preferred_element_type=F32) + jnp.dot(
        low, gatherer, preferred_element_type=F32
    )


def order_mask(shape, kind):
    row, column = (lax.broadcasted_iota(jnp.int32, shape, d) for d in (0, 1))
    return {"ge": row >= column, "gt": row > column, "le": row <= column, "lt": row < column}[kind]


def triangle(kind):
    return jnp.where(order_mask((CUT, CUT), kind), 1.0, 0.0).astype(F32)


def conv_chunk(window_ref, taps_ref, bias_ref, cols):
    total = bias_ref[:, cols] + taps_ref[0:1, cols] * window_ref[EDGE - 3 : EDGE - 3 + CUT, cols]
    for k in range(1, CONV):
        at = EDGE - 3 + k
        total = total + taps_ref[k : k + 1, cols] * window_ref[at : at + CUT, cols]
    return total


def prepare_kernel(
    proj_ref,
    edge_ref,
    taps_ref,
    bias_ref,
    dtb_ref,
    alog_ref,
    spreader_ref,
    act_ref,
    step_ref,
    slope_ref,
    logd_ref,
    local_ref,
    before_ref,
    total_ref,
    window,
    state,
    logs,
):
    q = pl.program_id(0)

    @pl.when(q == 0)
    def _():
        window[0:EDGE, :] = edge_ref[:, 0:MIXED]
        state[...] = jnp.zeros_like(state)
        logs[...] = jnp.zeros_like(logs)

    @pl.when(q > 0)
    def _():
        window[0:EDGE, :] = window[CUT : CUT + EDGE, :]

    window[EDGE : EDGE + CUT, :] = proj_ref[:, 0:MIXED]

    def conv(c, carry):
        cols = pl.ds(pl.multiple_of(c * STRIP, STRIP), STRIP)
        out = conv_chunk(window, taps_ref, bias_ref, cols)
        act_ref[:, cols] = out * jax.nn.sigmoid(out)
        return carry

    lax.fori_loop(0, MIXED // STRIP, conv, 0, unroll=3)
    raw = proj_ref[:, MIXED:RATED] + dtb_ref[...]
    step = jnp.maximum(raw, 0.0) + jnp.log1p(jnp.exp(-jnp.abs(raw)))
    logd = nn(triangle("ge"), -jnp.exp(alog_ref[...]) * step, EXACT)
    step_ref[...] = step
    slope_ref[...] = jax.nn.sigmoid(raw)
    logd_ref[...] = logd
    last = logd[CUT - 1 : CUT, :]
    tail = spread_heads(jnp.exp(last - logd) * step, spreader_ref[...])
    added = tn(act_ref[:, DI : DI + STATE], act_ref[:, 0:DI] * tail)
    decay = spread_heads(jnp.broadcast_to(jnp.exp(last), (8, HEADS)), spreader_ref[...])
    state[...] = state[...] * decay[0:1, :] + added
    local_ref[0] = state[...]
    before_ref[...] = jnp.exp(logs[...])
    logs[...] = logs[...] + jnp.broadcast_to(last, (8, HEADS))
    total_ref[...] = jnp.exp(logs[...])


def full(shape):
    return pl.BlockSpec(shape, lambda i: (0,) * len(shape))


def params():
    return pltpu.CompilerParams(
        dimension_semantics=("arbitrary",), vmem_limit_bytes=52 * 1024 * 1024
    )


def prepare(proj, taps, bias, dt_bias, a_log, spreader):
    rows = proj.shape[0] - EDGE
    cuts = rows // CUT
    return pl.pallas_call(
        prepare_kernel,
        grid=(cuts,),
        in_specs=[
            pl.BlockSpec((CUT, WIDE), lambda i: (i, 0)),
            pl.BlockSpec((EDGE, WIDE), lambda i: (rows // EDGE, 0)),
            full((CONV, MIXED)),
            full((1, MIXED)),
            full((1, HEADS)),
            full((1, HEADS)),
            full((3 * HEADS, DI)),
        ],
        out_specs=[
            pl.BlockSpec((CUT, MIXED), lambda i: (i, 0)),
            pl.BlockSpec((CUT, HEADS), lambda i: (i, 0)),
            pl.BlockSpec((CUT, HEADS), lambda i: (i, 0)),
            pl.BlockSpec((CUT, HEADS), lambda i: (i, 0)),
            pl.BlockSpec((1, STATE, DI), lambda i: (i, 0, 0)),
            pl.BlockSpec((8, HEADS), lambda i: (i, 0)),
            full((8, HEADS)),
        ],
        out_shape=[
            jax.ShapeDtypeStruct((rows, MIXED), F32),
            jax.ShapeDtypeStruct((rows, HEADS), F32),
            jax.ShapeDtypeStruct((rows, HEADS), F32),
            jax.ShapeDtypeStruct((rows, HEADS), F32),
            jax.ShapeDtypeStruct((cuts, STATE, DI), F32),
            jax.ShapeDtypeStruct((8 * cuts, HEADS), F32),
            jax.ShapeDtypeStruct((8, HEADS), F32),
        ],
        scratch_shapes=[
            pltpu.VMEM((CUT + EDGE, MIXED), F32),
            pltpu.VMEM((STATE, DI), F32),
            pltpu.VMEM((8, HEADS), F32),
        ],
        compiler_params=params(),
        cost_estimate=FREE,
        name="prepare",
    )(proj, proj, taps, bias, dt_bias, a_log, spreader)


def both_columns(pair, left):
    turned = pltpu.roll(pair, HDIM, 1)
    return (jnp.where(left, pair, turned), jnp.where(left, turned, pair))


def stacked_pair(pair, left):
    zero = jnp.zeros_like(pair)
    return jnp.concatenate([jnp.where(left, pair, zero), jnp.where(left, zero, pair)], axis=0)


UNROLL = 16


def intra_kernel(
    act_ref, step_ref, logd_ref, skip_ref, spreader_ref, out_ref, logx, weighted, log_rows, scores
):
    spreader = spreader_ref[...]
    logd = logd_ref[...]
    logx[...] = spread_heads(logd, spreader)
    log_rows[...] = logd.T
    heads_in = act_ref[:, 0:DI]
    weighted[...] = heads_in * spread_heads(step_ref[...], spreader)
    scores[...] = nt(act_ref[:, DI + STATE : MIXED], act_ref[:, DI : DI + STATE])

    def pair(j, carry):
        cols = pl.ds(pl.multiple_of(j * PAIR, PAIR), PAIR)
        left = lax.broadcasted_iota(jnp.int32, (CUT, PAIR), 1) < HDIM
        mask = order_mask((CUT, CUT), "ge")
        mixes = []
        for side, column in enumerate(both_columns(logx[:, cols], left)):
            row = log_rows[pl.ds(2 * j + side, 1), :]
            mixes.append(jnp.exp(jnp.where(mask, column - row, -1e30)) * scores[...])
        out_ref[:, cols] = skip_ref[:, cols] * act_ref[:, cols] + nn(
            jnp.concatenate(mixes, axis=1), stacked_pair(weighted[:, cols], left)
        )
        return carry

    lax.fori_loop(0, HEADS // 2, pair, 0, unroll=UNROLL)


def intra(act, step, logd, skip, spreader):
    rows = act.shape[0]

    def at(width):
        return pl.BlockSpec((CUT, width), lambda i: (i, 0))

    return pl.pallas_call(
        intra_kernel,
        grid=(rows // CUT,),
        in_specs=[at(MIXED), at(HEADS), at(HEADS), full((1, DI)), full((3 * HEADS, DI))],
        out_specs=at(DI),
        out_shape=jax.ShapeDtypeStruct((rows, DI), F32),
        scratch_shapes=[
            pltpu.VMEM((CUT, DI), F32),
            pltpu.VMEM((CUT, DI), F32),
            pltpu.VMEM((HEADS, CUT), F32),
            pltpu.VMEM((CUT, CUT), F32),
        ],
        compiler_params=params(),
        cost_estimate=FREE,
        name="intra",
    )(act, step, logd, skip, spreader)


def mixer_kernel(
    act_ref,
    logd_ref,
    inner_ref,
    gate_left_ref,
    gate_right_ref,
    dng_ref,
    local_ref,
    enter_ref,
    before_ref,
    ggain_ref,
    spreader_ref,
    ng_ref,
    dy_ref,
    dz_ref,
    gin_ref,
    ggrad_ref,
    skipg_ref,
    grown,
    out,
    gstate,
):
    i = pl.program_id(0)
    q = pl.num_programs(0) - 1 - i
    spreader = spreader_ref[...]

    @pl.when(i == 0)
    def _():
        gstate[...] = jnp.zeros_like(gstate)
        ggrad_ref[...] = jnp.zeros_like(ggrad_ref)
        skipg_ref[...] = jnp.zeros_like(skipg_ref)

    logd = logd_ref[...]
    grown[...] = spread_heads(jnp.exp(logd), spreader)
    before = spread_heads(before_ref[...], spreader)[0:1, :]
    entering = enter_ref[...] * before + jnp.where(q == 0, 0.0, local_ref[0])
    c_state = act_ref[:, DI + STATE : MIXED]
    out[...] = grown[...] * nn(c_state, entering) + inner_ref[...]

    def gate(k, carry):
        rows = pl.ds(pl.multiple_of(k * 8, 8), 8)
        ssd = out[rows, :]
        gate_in = jnp.concatenate([gate_left_ref[rows, :], gate_right_ref[rows, :]], axis=1)
        sg = jax.nn.sigmoid(gate_in)
        silu = gate_in * sg
        gated = ssd * silu
        scale = lax.rsqrt(jnp.mean(gated * gated, axis=1, keepdims=True) + epsilon)
        unit = gated * scale
        ng_ref[rows, :] = unit * ggain_ref[...]
        dng = dng_ref[rows, :]
        e = dng * ggain_ref[...]
        ggrad_ref[...] += dng * unit
        dgated = scale * (e - unit * jnp.mean(e * unit, axis=1, keepdims=True))
        dy = dgated * silu
        dy_ref[rows, :] = dy
        dz_ref[rows, :] = dgated * ssd * (sg * (1.0 + gate_in * (1.0 - sg)))
        skipg_ref[...] += dy * act_ref[rows, 0:DI]
        return carry

    lax.fori_loop(0, CUT // 8, gate, 0, unroll=GATE_UNROLL)
    gstate[...] = gstate[...] * grown[CUT - 1 : CUT, :] + tn(c_state, grown[...] * dy_ref[...])
    gin_ref[0] = gstate[...]


GATE_UNROLL = 4


def mixer(act, logd, inner, gates, dng, local, entering, before, ggain, spreader):
    rows = act.shape[0]
    cuts = rows // CUT

    def back(width):
        return pl.BlockSpec((CUT, width), lambda i: (cuts - 1 - i, 0))

    wide = jax.ShapeDtypeStruct((rows, DI), F32)
    return pl.pallas_call(
        mixer_kernel,
        grid=(cuts,),
        in_specs=[
            back(MIXED),
            back(HEADS),
            back(DI),
            back(DI // 2),
            back(DI // 2),
            back(DI),
            pl.BlockSpec((1, STATE, DI), lambda i: (jnp.maximum(cuts - 2 - i, 0), 0, 0)),
            full((STATE, DI)),
            pl.BlockSpec((8, HEADS), lambda i: (cuts - 1 - i, 0)),
            full((1, DI)),
            full((3 * HEADS, DI)),
        ],
        out_specs=[
            back(DI),
            back(DI),
            back(DI),
            pl.BlockSpec((1, STATE, DI), lambda i: (cuts - 1 - i, 0, 0)),
            full((8, DI)),
            full((8, DI)),
        ],
        out_shape=[
            wide,
            wide,
            wide,
            jax.ShapeDtypeStruct((cuts, STATE, DI), F32),
            jax.ShapeDtypeStruct((8, DI), F32),
            jax.ShapeDtypeStruct((8, DI), F32),
        ],
        scratch_shapes=[
            pltpu.VMEM((CUT, DI), F32),
            pltpu.VMEM((CUT, DI), F32),
            pltpu.VMEM((STATE, DI), F32),
        ],
        compiler_params=params(),
        cost_estimate=FREE,
        name="mixer",
    )(act, logd, inner, *gates, dng, local, entering, before, ggain, spreader)


def back_intra_kernel(
    act_ref,
    step_ref,
    logd_ref,
    dy_ref,
    spreader_ref,
    dweighted_ref,
    dstates_ref,
    moved_ref,
    logx,
    weighted,
    log_rows,
    sum_rows,
    scores,
    dscores,
    sum_columns,
):
    spreader = spreader_ref[...]
    logd = logd_ref[...]
    logx[...] = spread_heads(logd, spreader)
    log_rows[...] = logd.T
    weighted[...] = act_ref[:, 0:DI] * spread_heads(step_ref[...], spreader)
    b_state = act_ref[:, DI : DI + STATE]
    c_state = act_ref[:, DI + STATE : MIXED]
    scores[...] = nt(b_state, c_state)
    dscores[...] = jnp.zeros_like(dscores)
    sum_columns[...] = jnp.zeros_like(sum_columns)

    def pair(j, carry):
        cols = pl.ds(pl.multiple_of(j * PAIR, PAIR), PAIR)
        left = lax.broadcasted_iota(jnp.int32, (CUT, PAIR), 1) < HDIM
        mask = order_mask((CUT, CUT), "le")
        strict = order_mask((CUT, CUT), "lt")
        dy = dy_ref[:, cols]
        dmix = nt(stacked_pair(weighted[:, cols], left), dy)
        mixes = []
        lane = lax.broadcasted_iota(jnp.int32, (CUT, CUT), 1)
        for side, column in enumerate(both_columns(logx[:, cols], left)):
            row = log_rows[pl.ds(2 * j + side, 1), :]
            weights = jnp.exp(jnp.where(mask, row - column, -1e30))
            mixes.append(weights * scores[...])
            part = dmix[side * CUT : (side + 1) * CUT, :] * weights
            dscores[...] += part
            moved = jnp.where(strict, part * scores[...], 0.0)
            sum_rows[pl.ds(2 * j + side, 1), :] = jnp.sum(moved, axis=0, keepdims=True)
            sum_columns[...] += jnp.where(
                lane == 2 * j + side, jnp.sum(moved, axis=1, keepdims=True), 0.0
            )
        dweighted_ref[:, cols] = nn(jnp.concatenate(mixes, axis=1), stacked_pair(dy, left))
        return carry

    lax.fori_loop(0, HEADS // 2, pair, 0, unroll=BACK_UNROLL)
    dstates_ref[:, 0:STATE] = nn(dscores[...], c_state)
    dstates_ref[:, STATE : 2 * STATE] = tn(dscores[...], b_state)
    moved_ref[...] = sum_rows[...].T - sum_columns[:, 0:HEADS]


BACK_UNROLL = 16


def back_intra(act, step, logd, dy, spreader):
    rows = act.shape[0]

    def at(width):
        return pl.BlockSpec((CUT, width), lambda i: (i, 0))

    return pl.pallas_call(
        back_intra_kernel,
        grid=(rows // CUT,),
        in_specs=[at(MIXED), at(HEADS), at(HEADS), at(DI), full((3 * HEADS, DI))],
        out_specs=[at(DI), at(2 * STATE), at(HEADS)],
        out_shape=[
            jax.ShapeDtypeStruct((rows, DI), F32),
            jax.ShapeDtypeStruct((rows, 2 * STATE), F32),
            jax.ShapeDtypeStruct((rows, HEADS), F32),
        ],
        scratch_shapes=[
            pltpu.VMEM((CUT, DI), F32),
            pltpu.VMEM((CUT, DI), F32),
            pltpu.VMEM((HEADS, CUT), F32),
            pltpu.VMEM((HEADS, CUT), F32),
            pltpu.VMEM((CUT, CUT), F32),
            pltpu.VMEM((CUT, CUT), F32),
            pltpu.VMEM((CUT, CUT), F32),
        ],
        compiler_params=params(),
        cost_estimate=FREE,
        name="back_intra",
    )(act, step, logd, dy, spreader)


def back_kernel(
    act_ref,
    step_ref,
    slope_ref,
    logd_ref,
    dy_ref,
    dweighted_ref,
    dstates_ref,
    moved_ref,
    local_ref,
    enter_ref,
    before_ref,
    gin_ref,
    gout_ref,
    proj_ref,
    halo_ref,
    taps_ref,
    bias_ref,
    alog_ref,
    skip_ref,
    spreader_ref,
    gatherer_ref,
    dproj_ref,
    dtaps_ref,
    dbias_ref,
    dlog_ref,
    ddtb_ref,
    dact,
    window,
    dwindow,
    after,
):
    i = pl.program_id(0)
    cuts = pl.num_programs(0)
    q = cuts - 1 - i

    @pl.when(i == 0)
    def _():
        after[...] = jnp.zeros_like(after)
        dwindow[...] = jnp.zeros_like(dwindow)
        for ref in (dtaps_ref, dbias_ref, dlog_ref, ddtb_ref):
            ref[...] = jnp.zeros_like(ref)

    @pl.when(i > 0)
    def _():
        dwindow[CUT : CUT + EDGE, :] = dwindow[0:EDGE, :]

    logd = logd_ref[...]
    step = step_ref[...]
    last = logd[CUT - 1 : CUT, :]
    b_state = act_ref[:, DI : DI + STATE]
    c_state = act_ref[:, DI + STATE : MIXED]
    grow_parts = split_heads(jnp.exp(logd))
    tail_parts = split_heads(jnp.exp(last - logd))
    step_parts = split_heads(step)
    before_parts = split_heads(before_ref[...])
    later_parts = split_heads(jnp.exp(after[...]))
    after[...] = after[...] + jnp.broadcast_to(last, (8, HEADS))
    db = dstates_ref[:, 0:STATE]
    dc = dstates_ref[:, STATE : 2 * STATE]
    moved = moved_ref[...]
    lost = jnp.zeros((CUT, HEADS), F32)
    dstep = jnp.zeros((CUT, HEADS), F32)
    kept = jnp.zeros((8, HEADS), F32)
    for c in range(DI // BLOCK):
        cols = slice(c * BLOCK, (c + 1) * BLOCK)
        spreader = spreader_ref[:, cols]
        gatherer = gatherer_ref[cols, :]
        entering = enter_ref[:, cols] * bf16_dot(before_parts, spreader)[0:1, :]
        entering = entering + jnp.where(q == 0, 0.0, local_ref[0, :, cols])
        gout = gout_ref[:, cols] * bf16_dot(later_parts, spreader)[0:1, :]
        gout = gout + jnp.where(i == 0, 0.0, gin_ref[0, :, cols])
        tail = bf16_dot(tail_parts, spreader)
        steps = bf16_dot(step_parts, spreader)
        heads_in = act_ref[:, cols]
        dy = dy_ref[:, cols]
        from_state = tail * nn(b_state, gout)
        stepped = heads_in * steps
        dweighted = dweighted_ref[:, cols] + from_state
        carried = bf16_dot(grow_parts, spreader) * dy
        db = db + nt(tail * stepped, gout)
        dc = dc + nt(carried, entering)
        dact[:, cols] = dweighted * steps + skip_ref[:, cols] * dy
        moved = moved + sum_heads(carried * nn(c_state, entering), gatherer)
        lost = lost + sum_heads(stepped * from_state, gatherer)
        dstep = dstep + sum_heads(heads_in * dweighted, gatherer)
        kept = kept + sum_heads(
            jnp.broadcast_to(jnp.sum(gout * entering, axis=0, keepdims=True), (8, BLOCK)), gatherer
        )
    dact[:, DI : DI + STATE] = db
    dact[:, DI + STATE : MIXED] = dc
    dlog = (
        nn(triangle("le"), moved, EXACT)
        + nn(triangle("gt"), lost, EXACT)
        + jnp.exp(last) * kept[0:1, :]
    )
    rate = -jnp.exp(alog_ref[...])
    dlog_ref[...] += jnp.broadcast_to(
        jnp.sum(dlog * step, axis=0, keepdims=True) * rate, (8, HEADS)
    )
    draw = (dstep + dlog * rate) * slope_ref[...]
    ddtb_ref[...] += jnp.broadcast_to(jnp.sum(draw, axis=0, keepdims=True), (8, HEADS))
    here = pl.ds(pl.multiple_of(q * CUT, CUT), CUT)
    dproj_ref[here, MIXED:WIDE] = jnp.concatenate([draw, jnp.zeros((CUT, SPARE), F32)], axis=1)
    window[0:EDGE, :] = halo_ref[:, 0:MIXED]
    window[EDGE : EDGE + CUT, :] = proj_ref[:, 0:MIXED]

    def conv(c, carry):
        cols = pl.ds(pl.multiple_of(c * STRIP, STRIP), STRIP)
        out = conv_chunk(window, taps_ref, bias_ref, cols)
        sg = jax.nn.sigmoid(out)
        dout = dact[:, cols] * (sg * (1.0 + out * (1.0 - sg)))
        dwindow[0:CUT, cols] = dout
        dbias_ref[:, cols] += jnp.sum(dout.reshape(CUT // 8, 8, STRIP), axis=0)
        for k in range(CONV):
            at = EDGE - 3 + k
            dtaps_ref[8 * k : 8 * k + 8, cols] += jnp.sum(
                (dout * window[at : at + CUT, cols]).reshape(CUT // 8, 8, STRIP), axis=0
            )
        din = taps_ref[CONV - 1 : CONV, cols] * dout
        for k in range(CONV - 1):
            din = din + taps_ref[k : k + 1, cols] * dwindow[3 - k : 3 - k + CUT, cols]
        dproj_ref[here, cols] = din
        return carry

    lax.fori_loop(0, MIXED // STRIP, conv, 0, unroll=3)

    @pl.when(q == 0)
    def _():
        rows = cuts * CUT
        window[0:EDGE, :] = jnp.zeros((EDGE, MIXED), F32)
        window[EDGE : 2 * EDGE, :] = dwindow[0:EDGE, :]
        din = taps_ref[CONV - 1 : CONV, :] * window[0:EDGE, :]
        for k in range(CONV - 1):
            din = din + taps_ref[k : k + 1, :] * window[3 - k : 3 - k + EDGE, :]
        dproj_ref[rows : rows + EDGE, 0:MIXED] = din
        dproj_ref[rows : rows + EDGE, MIXED:WIDE] = jnp.zeros((EDGE, WIDE - MIXED), F32)


def back(
    act, step, slope, logd, dy, dweighted, dstates, moved, local, entering, before, gin, gout, proj, taps, bias, a_log,
    skip, spreader, gatherer,
):
    rows = act.shape[0]
    cuts = rows // CUT

    def at(size):
        return pl.BlockSpec((CUT, size), lambda i: (cuts - 1 - i, 0))

    def halo(i):
        q = cuts - 1 - i
        return (jnp.where(q == 0, rows // EDGE, q * (CUT // EDGE) - 1), 0)

    return pl.pallas_call(
        back_kernel,
        grid=(cuts,),
        in_specs=[
            at(MIXED),
            at(HEADS),
            at(HEADS),
            at(HEADS),
            at(DI),
            at(DI),
            at(2 * STATE),
            at(HEADS),
            pl.BlockSpec((1, STATE, DI), lambda i: (jnp.maximum(cuts - 2 - i, 0), 0, 0)),
            full((STATE, DI)),
            pl.BlockSpec((8, HEADS), lambda i: (cuts - 1 - i, 0)),
            pl.BlockSpec((1, STATE, DI), lambda i: (jnp.minimum(cuts - i, cuts - 1), 0, 0)),
            full((STATE, DI)),
            at(WIDE),
            pl.BlockSpec((EDGE, WIDE), halo),
            full((CONV, MIXED)),
            full((1, MIXED)),
            full((1, HEADS)),
            full((1, DI)),
            full((3 * HEADS, DI)),
            full((DI, HEADS)),
        ],
        out_specs=[
            full((rows + EDGE, WIDE)),
            full((8 * CONV, MIXED)),
            full((8, MIXED)),
            full((8, HEADS)),
            full((8, HEADS)),
        ],
        out_shape=[
            jax.ShapeDtypeStruct((rows + EDGE, WIDE), F32),
            jax.ShapeDtypeStruct((8 * CONV, MIXED), F32),
            jax.ShapeDtypeStruct((8, MIXED), F32),
            jax.ShapeDtypeStruct((8, HEADS), F32),
            jax.ShapeDtypeStruct((8, HEADS), F32),
        ],
        scratch_shapes=[
            pltpu.VMEM((CUT, MIXED), F32),
            pltpu.VMEM((CUT + EDGE, MIXED), F32),
            pltpu.VMEM((CUT + EDGE, MIXED), F32),
            pltpu.VMEM((8, HEADS), F32),
        ],
        compiler_params=params(),
        cost_estimate=FREE,
        name="back",
    )(
        act, step, slope, logd, dy, dweighted, dstates, moved, local, entering, before, gin, gout, proj, proj,
        taps, bias, a_log, skip, spreader, gatherer,
    )


COLUMNS = 512


def right_kernel(x_ref, w_ref, added_ref, scale_ref, out_ref):
    out_ref[...] = (nn(x_ref[...], w_ref[...]) + added_ref[...]) * scale_ref[...]


def right(x, w, added, scale):
    (rows, depth), cols = (x.shape, w.shape[1])
    tile = pl.BlockSpec((rows, COLUMNS), lambda j: (0, j))
    return pl.pallas_call(
        right_kernel,
        grid=(cols // COLUMNS,),
        in_specs=[
            full((rows, depth)), pl.BlockSpec((depth, COLUMNS), lambda j: (0, j)), tile, full((rows, 1)),
        ],
        out_specs=tile,
        out_shape=jax.ShapeDtypeStruct((rows, cols), F32),
        compiler_params=params(),
        cost_estimate=FREE,
        name="right",
    )(x, w, added, scale)


def right_back_kernel(x_ref, *refs):
    *w_refs, out_ref = refs
    total, at = (None, 0)
    for w_ref in w_refs:
        part = nt(x_ref[:, at : at + w_ref.shape[1]], w_ref[...])
        total, at = (part if total is None else total + part, at + w_ref.shape[1])
    out_ref[...] = total


def right_back(x, weights):
    rows, cols = (x.shape[0], weights[0].shape[0])
    return pl.pallas_call(
        right_back_kernel,
        grid=(cols // COLUMNS,),
        in_specs=[full(x.shape)]
        + [pl.BlockSpec((COLUMNS, w.shape[1]), lambda j: (j, 0)) for w in weights],
        out_specs=pl.BlockSpec((rows, COLUMNS), lambda j: (0, j)),
        out_shape=jax.ShapeDtypeStruct((rows, cols), F32),
        compiler_params=params(),
        cost_estimate=FREE,
        name="right_back",
    )(x, *weights)


def head_spreader():
    head = lax.broadcasted_iota(jnp.int32, (3 * HEADS, DI), 0) % HEADS
    return (head == lax.broadcasted_iota(jnp.int32, (3 * HEADS, DI), 1) // HDIM).astype(BF16)


def head_gatherer():
    channel = lax.broadcasted_iota(jnp.int32, (DI, HEADS), 0) // HDIM
    return (channel == lax.broadcasted_iota(jnp.int32, (DI, HEADS), 1)).astype(BF16)


def per_device(
    hidden_in,
    lengths,
    norm_gain,
    in_weight,
    conv_weight,
    conv_bias,
    dt_bias,
    a_log,
    skip_gain,
    gated_gain,
    out_weight,
    cotangent,
):
    width = hidden_in.shape[-1]
    devices = 1
    for axis in AXES:
        devices *= lax.axis_size(axis)
    mine, spot, count = (lax.axis_index("p"), lax.axis_index("zc"), lax.axis_size("zc"))
    own_rows = width // devices

    in_piece = in_weight.reshape(own_rows, -1)
    small = jnp.concatenate([conv_weight, conv_bias])
    padded = jnp.pad(small, (0, SPARE * own_rows - small.shape[0])).reshape(own_rows, SPARE)
    conv = Gather(jnp.concatenate([in_piece[:, DI:], padded], axis=1), 0.5)
    edge = before_span(hidden_in, mine)
    conv.line()
    trade = Exchange(hidden_in, mine)
    hidden = trade.result(jnp.concatenate)
    rows = hidden.shape[0]
    out_piece = out_weight.reshape(-1, width)
    rest = jnp.concatenate([in_piece[:, :width], in_piece[:, width:DI], out_piece], axis=0)
    rest = lax.all_gather(rest, AXES, axis=0).reshape(devices, -1, width)
    w_gates = [
        rest[:, k * own_rows : (k + 1) * own_rows].reshape(width, width) for k in range(DI // width)
    ]
    w_out = rest[:, DI // width * own_rows :].reshape(DI, width)
    near = conv.near(trade.other)
    conv_over = conv.across(conv.held_near()[:1], conv.block)
    far = conv.far()
    conv_over += conv.across(conv.held_near()[1:])
    conv_over += conv.across(conv.corners)
    (w_conv,) = place(conv.held() + conv_over, conv.rows, [[(0, WIDE)]])
    other = Exchange(tied([cotangent], *far)[0], mine)
    smalls = w_conv[:, RATED:].reshape(devices, own_rows * SPARE)
    taps = smalls[:, : conv_weight.shape[0]].reshape(CONV, MIXED)
    bias = smalls[:, conv_weight.shape[0] : small.shape[0]].reshape(1, MIXED)

    extended = jnp.concatenate([hidden, edge], axis=0)
    scale = lax.rsqrt(jnp.mean(extended * extended, axis=1, keepdims=True) + epsilon)
    unit = extended * scale
    normed = unit * norm_gain
    inner = normed[:rows]
    spreader, gatherer = (head_spreader(), head_gatherer())
    dt_row, alog_row = (dt_bias.reshape(1, -1), a_log.reshape(1, -1))
    skip_row = jnp.repeat(skip_gain, HDIM).reshape(1, DI)
    positions = spot * rows + lax.iota(jnp.int32, rows)
    length = lax.dynamic_index_in_dim(lengths, mine, 0, keepdims=False)
    valid = (positions < length).astype(F32)[:, None]
    proj = nn(normed, w_conv)
    act, step, slope, logd, local, before, total = prepare(
        proj, taps, bias, dt_row, alog_row, spreader
    )
    total_row = jnp.repeat(total[0], HDIM).reshape(1, DI)
    states = States(total_row, local[-1], False)
    states.send()
    within = intra(tied([act], *states.sends)[0], step, logd, skip_row, spreader)
    (turn,) = tied([inner], within)
    gates = [nn(turn, w) for w in w_gates]
    states.go_on(*gates)
    grad_out = other.result(jnp.concatenate, within) * valid
    dng = nt(tied([grad_out], *gates, *states.sends)[0], w_out)
    entering = states.result(dng)
    ng, dy, dz, gin, ggrad, skipg = mixer(
        act, logd, within, gates, dng, local, entering, before, gated_gain.reshape(1, DI), spreader
    )
    ng_keep, ng_send = core_columns(ng)
    in_keep, in_send = core_columns(normed)
    grads = States(total_row, gin[0], True)
    grads.send()
    (turn,) = tied([ng_send], *grads.sends)
    first = tn(turn, grad_out)
    (turn,) = tied([grad_out], first)
    second = tn(ng_keep, turn)
    grad_wout = Scatter(first, second)
    branch = right(tied([ng], second)[0], w_out, hidden, valid)
    traded = Exchange(halves(branch), mine)
    grads.go_on(branch)
    grad_wout.keep(branch)
    grad_wout.stage(("p", "y"))
    (turn,) = tied([dz], branch, *grads.sends, *grad_wout.sends)
    first = tn(in_send[:rows], turn)
    (turn,) = tied([turn], first)
    second = tn(in_keep[:rows], turn)
    grad_wgate = Scatter(first, second)
    back_parts = back_intra(tied([act], second)[0], step, logd, dy, spreader)
    grad_wout.keep(back_parts[1])
    grad_wgate.keep(back_parts[1])
    grad_wout.stage(("y", "p"))
    grad_wgate.stage(("p", "y"))
    (turn,) = tied([dz], back_parts[1], *grad_wout.sends, *grad_wgate.sends, traded.other)
    dgate_normed = right_back(turn, w_gates)
    grad_wout.keep(dgate_normed)
    grad_wout.last_at_once()
    gout = grads.result(dgate_normed)
    dproj, dtaps, dbias, dlog, ddtb = back(
        tied([act], dgate_normed, *grad_wout.sends)[0], step, slope, logd, dy, *back_parts, local,
        entering, before, gin, gout, proj, taps, bias, alog_row, skip_row, spreader, gatherer,
    )
    dtaps = jnp.sum(dtaps.reshape(CONV, 8, MIXED), axis=1).reshape(devices, -1)
    dbias = jnp.sum(dbias, axis=0).reshape(devices, -1)
    dsmall = jnp.concatenate([dtaps, dbias], axis=1)
    dsmall = jnp.pad(dsmall, ((0, 0), (0, SPARE * own_rows - small.shape[0])))
    dsmall = jnp.pad(dsmall.reshape(width, SPARE), ((0, 0), (RATED, 0)))
    small_keep, small_send = (core_rows(dsmall, k) for k in (0, 1))
    grad_wout.settle()
    grad_wgate.keep(ddtb)
    grad_wgate.stage(("y", "p"))
    (turn,) = tied([dproj], *grad_wgate.sends, grad_wout.line)
    first = tn(in_send, turn) + small_send
    (turn,) = tied([dproj], first)
    second = tn(in_keep, turn) + small_keep
    grad_wconv = Scatter(first, second)
    grad_wconv.keep(second)
    grad_wconv.stage(("p", "y"))
    grad_wgate.keep(second, *grad_wconv.sends)
    grad_wgate.last_at_once()
    dnormed = nt(tied([dproj], second, *grad_wconv.sends, *grad_wgate.sends)[0], w_conv)
    grad_wgate.settle(dnormed)
    near = grad_wconv.came
    output = traded.result(jnp.stack, dnormed)
    returned = lax.ppermute(dnormed[rows:], "zc", [(i + 1, i) for i in range(count - 1)])
    dnormed = dnormed[:rows] + dgate_normed
    dnormed = dnormed + jnp.pad(returned, ((rows - EDGE, 0), (0, 0)))
    unit = unit[:rows]
    dunit = dnormed * norm_gain
    dhidden = scale[:rows] * (dunit - unit * jnp.mean(dunit * unit, axis=1, keepdims=True))
    grad_input = Exchange(halves(tied([grad_out + dhidden], *near)[0]), mine).result(jnp.stack)
    grad_skip = jnp.sum(jnp.sum(skipg, axis=0).reshape(HEADS, HDIM), axis=1)
    sums = jnp.concatenate(
        [
            jnp.sum(dnormed * unit, axis=0),
            jnp.sum(ggrad, axis=0),
            ddtb[0],
            dlog[0],
            grad_skip,
        ]
    )
    (sums,) = tied([jnp.pad(sums, (0, -sums.shape[0] % 128)).reshape(-1, 128)], *near)
    sums = sum_everywhere(sums).reshape(-1)
    grad_wconv.stage(("y", "p"))
    grad_wconv.last()
    parts = []
    for size in (width, DI, HEADS, HEADS, HEADS):
        parts.append(sums[:size])
        sums = sums[size:]
    conv_grad = grad_wconv.result()
    small_grad = conv_grad[:, RATED:].reshape(-1)
    return (
        output,
        grad_input,
        parts[0],
        jnp.concatenate([grad_wgate.result(), conv_grad[:, :RATED]], axis=1).reshape(-1),
        small_grad[: conv_weight.shape[0]],
        small_grad[conv_weight.shape[0] : small.shape[0]],
        parts[2],
        parts[3],
        parts[4],
        parts[1],
        grad_wout.result().reshape(-1),
    )


def core_columns(values):
    size = values.shape[1] // (2 * lax.axis_size("y"))
    core = lax.axis_index("core")
    return [
        jnp.concatenate(
            [
                lax.dynamic_slice_in_dim(values, (2 * y + (core + k) % 2) * size, size, 1)
                for y in range(lax.axis_size("y"))
            ],
            axis=1,
        )
        for k in (0, 1)
    ]


def core_rows(values, k):
    size = values.shape[0] // (2 * lax.axis_size("y"))
    core = lax.axis_index("core")
    return jnp.concatenate(
        [
            lax.dynamic_slice_in_dim(values, (2 * y + (core + k) % 2) * size, size, 0)
            for y in range(lax.axis_size("y"))
        ],
        axis=0,
    )


def solution(mesh):
    dp, seq = (mesh.shape["dp"], mesh.shape["seq"])
    finer = Mesh(mesh.devices.reshape(dp // 2, 2, seq // 2, 2), AXES)
    over_dp, over_seq = (("y", "core"), ("zc", "p"))
    tokens = P(over_dp, over_seq, None)
    in_specs = (
        tokens, P(over_dp), P(), P(AXES), P(AXES), P(AXES), P(), P(), P(), P(), P(AXES), tokens,
    )
    out_specs = (
        tokens, tokens, P(), P(AXES), P(AXES), P(AXES), P(), P(), P(), P(), P(AXES),
    )
    return jax.shard_map(
        per_device, mesh=finer, in_specs=in_specs, out_specs=out_specs, check_vma=False
    )
```
